256 devices in a mesh: dp: 16 (over z, y_lo), mp: 16 (over y_hi, x, core).
Axes of the slice: x: 4, y: 4 (y_hi: 2, y_lo: 2; y = y_hi * 2 + y_lo), z: 8, core: 2. Of those that a mesh axis runs over, the one named last changes fastest.
Arguments:
- img_emb: bfloat16 [8192, 1536], P('dp')
- txt_emb: bfloat16 [8192, 1536], P(('dp', 'mp'))
- img_feat_t: bfloat16 [1536, 8192], P('mp', 'dp'), may hold values from -6 to 6
- txt_feat_t: bfloat16 [1536, 8192], P('mp', 'dp'), may hold values from -6 to 6
- logit_scale: float32 [1], replicated, may hold values from 8 to 16
- logit_bias: float32 [1], replicated
Outputs:
- row_loss: float32 [8192], P('dp')
- img_head_grad: float32 [1536, 1536], P('mp')
- txt_head_grad: float32 [1536, 1536], P('mp')
The draws below stay inside these ranges and needn't reach their ends.
All inputs are finite; a program needn't handle non-finite values.
Results may differ from the reference program's by a relative error of at most 0.0061.
Values may be sent and summed in bfloat16 or wider, within the bound.
No kernel may reach another device: no remote copies, remote signals or barrier semaphores. Data moves between devices by JAX's collectives and lax.ppermute only.
A program may use at most 64 MiB of HBM per device.

```python
import math
import jax
import jax.numpy as jnp
from jax import lax

E = 1536
DI = 1536
DT = 1536
B_DEV = 512
BATCH = 8192
N_DP = 16


def common_parts(key):
    columns = jnp.exp(jax.random.uniform(jax.random.fold_in(key, 1), (1, E), jnp.float32, math.log(0.3), math.log(3.0)))
    shared = jnp.clip(jax.random.normal(jax.random.fold_in(key, 2), (BATCH, E), jnp.float32), -5.0, 5.0)
    return (columns, shared)


def assemble(key, mixed, columns):
    row_scales = jnp.exp(jax.random.uniform(jax.random.fold_in(key, 3), (BATCH, 1), jnp.float32, math.log(0.5), math.log(5.0)))
    values = mixed * columns * row_scales / math.sqrt(E)
    return values.astype(jnp.bfloat16)


def draw_img_emb(key, part):
    columns, shared = common_parts(key)
    key = jax.random.fold_in(key, 11)
    first, second = jax.random.split(key)
    own = jnp.clip(jax.random.normal(first, (BATCH, E), jnp.float32), -5.0, 5.0)
    return assemble(second, 0.8 * shared + 0.6 * own, columns)


def draw_txt_emb(key, part):
    columns, shared = common_parts(key)
    key = jax.random.fold_in(key, 12)
    first, second = jax.random.split(key)
    own = jnp.clip(jax.random.normal(first, (BATCH, E), jnp.float32), -5.0, 5.0)
    return assemble(second, 0.8 * shared + 0.6 * own, columns)


def draw_logit_bias(key, part):
    key = jax.random.fold_in(key, 13)
    offset = jax.random.uniform(key, (1,), jnp.float32, 1.0, 3.0)
    return (offset - math.log(BATCH)).astype(jnp.float32)


def levels(own_key, dims, pieces, low, high):
    def one(dim, blocks):
        draws = jax.random.uniform(jax.random.fold_in(jax.random.fold_in(own_key, 6), dim), (blocks,), jnp.float32, low / len(pieces), high / len(pieces))
        return jnp.repeat(jnp.exp(draws), dims[dim] // blocks).reshape((-1,) + (1,) * (len(dims) - dim - 1))

    gain = one(*pieces[0])
    for cut in pieces[1:]:
        gain = gain * one(*cut)
    return gain


def scatter_about(stream_key, dims, scale, bound, cuts=(), kind=jnp.bfloat16):
    entries = scale * jax.random.normal(stream_key, dims, jnp.float32)
    if cuts:
        entries = entries * levels(stream_key, dims, cuts, -0.22, 0.18)
    return jnp.clip(entries, -bound, bound).astype(kind)


def setup_inputs(seed: int = 0) -> dict:
    arg_keys = jax.random.split(jax.random.key(seed), 7)
    return {
        "img_emb": draw_img_emb(jax.random.fold_in(arg_keys[6], 71), 0),
        "txt_emb": draw_txt_emb(jax.random.fold_in(arg_keys[6], 71), 0),
        "img_feat_t": scatter_about(arg_keys[2], (DI, BATCH), 1.0, 6.0, ((0, 16), (1, 16))),
        "txt_feat_t": scatter_about(arg_keys[3], (DT, BATCH), 1.0, 6.0, ((0, 16), (1, 16))),
        "logit_scale": jnp.clip(jnp.exp(jax.random.uniform(arg_keys[4], (1,), jnp.float32, math.log(8.0), math.log(16.0))), 8.0, 16.0),
        "logit_bias": draw_logit_bias(jax.random.fold_in(arg_keys[6], 71), 0),
    }


def normalize(raw):
    values = raw.astype(jnp.float32)
    inverse = lax.rsqrt(lax.optimization_barrier(jnp.sum(values * values, axis=1, keepdims=True)) + 1e-06)
    return (values * inverse, inverse)

def through_norm(upstream, normed, inverse):
    return (upstream - normed * lax.optimization_barrier(jnp.sum(normed * upstream, axis=1, keepdims=True))) * inverse

def reference(img_emb, txt_emb, img_feat_t, txt_feat_t, logit_scale, logit_bias):
    normed_img, inv_img = normalize(img_emb)
    normed_txt, inv_txt = normalize(txt_emb)
    images = normed_img.astype(jnp.bfloat16)
    texts = normed_txt.astype(jnp.bfloat16)
    scale = logit_scale[0]
    bias = logit_bias[0]
    all_ids = jnp.arange(BATCH, dtype=jnp.int32)

    def one_block(carry, item):
        block, block_ids = item
        logits = scale * jnp.dot(block, texts.T, preferred_element_type=jnp.float32) + bias
        signs = jnp.where(block_ids[:, None] == all_ids[None, :], 1.0, -1.0).astype(jnp.float32)
        losses = lax.optimization_barrier(jnp.sum(jax.nn.softplus(-signs * logits), axis=1))
        slopes = (scale * -signs * jax.nn.sigmoid(-signs * logits)).astype(jnp.bfloat16)
        image_grad = jnp.dot(slopes, texts, preferred_element_type=jnp.float32)
        carry = carry + jnp.dot(slopes.T, block, preferred_element_type=jnp.float32)
        return (carry, (losses, image_grad))
    start = jnp.zeros((BATCH, E), jnp.float32)
    text_grad, (losses, image_grad) = lax.scan(one_block, start, (images.reshape(N_DP, B_DEV, E), all_ids.reshape(N_DP, B_DEV)))
    d_img = through_norm(image_grad.reshape(BATCH, E), normed_img, inv_img).astype(jnp.bfloat16)
    d_txt = through_norm(text_grad, normed_txt, inv_txt).astype(jnp.bfloat16)
    img_head_grad = jnp.dot(img_feat_t, d_img, preferred_element_type=jnp.float32)
    txt_head_grad = jnp.dot(txt_feat_t, d_txt, preferred_element_type=jnp.float32)
    return (losses.reshape(BATCH), img_head_grad, txt_head_grad)
```

```python
import jax
import jax.numpy as jnp
from jax import lax
from jax.sharding import PartitionSpec as P

F32 = jnp.float32
BF16 = jnp.bfloat16
CHIPS = 8
LANES = 128


def normalize(raw):
    values = raw.astype(F32)
    inverse = lax.rsqrt(jnp.sum(values * values, axis=1, keepdims=True) + 1e-06)
    return (values * inverse, inverse)


def through_norm(upstream, normed, inverse):
    return (upstream - normed * jnp.sum(normed * upstream, axis=1, keepdims=True)) * inverse


def move_dp(value, turn):
    return lax.ppermute(value, "dp", [(d, turn(d)) for d in range(16)])


def swap_core(value):
    return lax.ppermute(value, "mp", [(m, m ^ 1) for m in range(16)])


def same_core():
    return [[2 * chip + core for chip in range(CHIPS)] for core in range(2)]


def scatter_chips(value):
    return lax.all_to_all(value, "mp", 0, 0, tiled=True, axis_index_groups=same_core())


def gather_chips(value):
    return scatter_chips(jnp.concatenate([value] * CHIPS, axis=0))


def gather_texts(block, dp_index):
    along = [0, 1, -1, 2, -2, 3, -3, 4]
    own = [block] + [
        move_dp(block, lambda d, k=k: (d + 2 * k) % 16) for k in along[1:]
    ]
    other = [move_dp(value, lambda d: d ^ 1) for value in own]
    owners = [(dp_index - 2 * k) % 16 for k in along]
    owners += [owner ^ 1 for owner in owners]
    return jnp.concatenate(own + other, axis=0), owners


def split_pair(value):
    high = lax.reduce_precision(value, 8, 7)
    return high, value - high


def with_loss(matrix, losses):
    high, low = split_pair(losses)
    lane = lax.broadcasted_iota(jnp.int32, (matrix.shape[0], LANES), 1)
    extra = jnp.where(lane == 0, high[:, None], jnp.where(lane == 1, low[:, None], 0.0))
    return jnp.concatenate([matrix.astype(BF16), extra.astype(BF16)], axis=1)


def take_loss(extra):
    return extra[:, 0].astype(F32) + extra[:, 1].astype(F32)


def to_pieces(weight):
    rows, width = weight.shape
    pieces = weight.reshape(4, rows // 4, 4, width // 4).transpose(0, 2, 1, 3)
    return pieces.reshape(4 * rows, width // 4)


def from_pieces(pieces, rows, width):
    blocks = pieces.reshape(4, 4, rows // 4, width // 4).transpose(0, 2, 1, 3)
    return blocks.reshape(rows, width)


def sum_batch(weight):
    rows, width = weight.shape
    parts = lax.all_to_all(to_pieces(weight.astype(BF16)), "dp", 0, 0, tiled=True)
    own = jnp.sum(parts.reshape(16, rows // 4, width // 4).astype(F32), axis=0).astype(BF16)
    spread = jnp.broadcast_to(own[None], (16,) + own.shape)
    return from_pieces(lax.all_to_all(spread, "dp", 0, 0), rows, width).astype(F32)


def shards(img_emb, txt_emb, img_feat_t, txt_feat_t, logit_scale, logit_bias):
    rows, width = img_emb.shape
    sub = txt_emb.shape[0]
    half = rows // 2
    dp_index = lax.axis_index("dp")
    mp_index = lax.axis_index("mp")
    core = mp_index % 2
    chip = mp_index // 2
    scale = logit_scale[0]
    bias = logit_bias[0]

    normed_txt, inv_txt = normalize(txt_emb)
    texts, owners = gather_texts(normed_txt.astype(BF16), dp_index)
    normed_img, inv_img = normalize(img_emb)
    images = normed_img.astype(BF16)

    text_ids = jnp.concatenate(
        [owner * rows + mp_index * sub + jnp.arange(sub, dtype=jnp.int32) for owner in owners]
    )
    image_ids = dp_index * rows + jnp.arange(rows, dtype=jnp.int32)
    logits = scale * lax.dot_general(
        texts, images, (((1,), (1,)), ((), ())), preferred_element_type=F32
    ) + bias
    signs = jnp.where(text_ids[:, None] == image_ids[None, :], 1.0, -1.0).astype(F32)
    losses = jnp.sum(jax.nn.softplus(-signs * logits), axis=0)
    slopes = (scale * -signs * jax.nn.sigmoid(-signs * logits)).astype(BF16)

    text_part = jnp.dot(slopes, images, preferred_element_type=F32).astype(BF16)
    order = jnp.stack(owners)
    text_part = jnp.concatenate(
        [
            lax.dynamic_slice_in_dim(
                text_part, jnp.argmax(order == d).astype(jnp.int32) * sub, sub, 0
            )
            for d in range(16)
        ],
        axis=0,
    )
    text_pieces = lax.all_to_all(text_part, "dp", 0, 0, tiled=True)

    image_part = lax.dot_general(
        slopes, texts, (((0,), (0,)), ((), ())), preferred_element_type=F32
    )
    own_start, other_start = core * half, (1 - core) * half
    kept = lax.dynamic_slice_in_dim(image_part, own_start, half, 0)
    sent = lax.dynamic_slice_in_dim(image_part, other_start, half, 0)
    kept_loss = lax.dynamic_slice_in_dim(losses, own_start, half, 0)
    sent_loss = lax.dynamic_slice_in_dim(losses, other_start, half, 0)
    came = swap_core(with_loss(sent, sent_loss))
    both = kept + came[:, :width].astype(F32)
    both_loss = kept_loss + take_loss(came[:, width:])
    pieces = scatter_chips(with_loss(both, both_loss))
    summed = jnp.sum(pieces.reshape(CHIPS, half // CHIPS, -1).astype(F32), axis=0)
    image_grad = summed[:, :width]
    image_loss = summed[:, width] + summed[:, width + 1]
    row_start = own_start + chip * (half // CHIPS)
    d_img = through_norm(
        image_grad,
        lax.dynamic_slice_in_dim(normed_img, row_start, half // CHIPS, 0),
        lax.dynamic_slice_in_dim(inv_img, row_start, half // CHIPS, 0),
    )
    own_half = gather_chips(with_loss(d_img, image_loss))
    other_half = swap_core(own_half)
    img_weight = jnp.dot(
        lax.dynamic_slice_in_dim(img_feat_t, own_start, half, 1),
        own_half[:, :width],
        preferred_element_type=F32,
    ) + jnp.dot(
        lax.dynamic_slice_in_dim(img_feat_t, other_start, half, 1),
        other_half[:, :width],
        preferred_element_type=F32,
    )
    own_loss, other_loss = take_loss(own_half[:, width:]), take_loss(other_half[:, width:])
    row_loss = jnp.where(
        core == 0,
        jnp.concatenate([own_loss, other_loss]),
        jnp.concatenate([other_loss, own_loss]),
    )

    text_grad = jnp.sum(text_pieces.reshape(16, sub, width).astype(F32), axis=0)
    d_txt = through_norm(text_grad, normed_txt, inv_txt).astype(BF16)
    own_txt = gather_chips(d_txt)
    other_txt = swap_core(own_txt)
    by_core = txt_feat_t.reshape(-1, CHIPS, 2, sub)
    even, odd = by_core[:, :, 0].reshape(-1, half), by_core[:, :, 1].reshape(-1, half)
    txt_weight = jnp.dot(
        jnp.where(core == 0, even, odd), own_txt, preferred_element_type=F32
    ) + jnp.dot(jnp.where(core == 0, odd, even), other_txt, preferred_element_type=F32)

    total = sum_batch(jnp.concatenate([img_weight, txt_weight], axis=0))
    out_rows = img_weight.shape[0]
    return (row_loss, total[:out_rows], total[out_rows:])


def solution(mesh):
    in_specs = (P("dp", None), P(("dp", "mp"), None), P("mp", "dp"), P("mp", "dp"), P(), P())
    out_specs = (P("dp"), P("mp", None), P("mp", None))
    return jax.shard_map(shards, mesh=mesh, in_specs=in_specs, out_specs=out_specs, check_vma=False)
```

```python
import jax
import jax.numpy as jnp
from jax import lax
from jax.experimental import pallas as pl
from jax.experimental.pallas import tpu as pltpu
from jax.sharding import PartitionSpec as P

F32 = jnp.float32
BF16 = jnp.bfloat16
LANES = 128
ALONG = (0, 1, -1, 2, -2, 3, -3, 4)
VMEM = pl.BlockSpec(memory_space=pltpu.VMEM)
SMEM = pl.BlockSpec(memory_space=pltpu.SMEM)


def local(kernel, outs, operands, specs=None, scratch=()):
    single = not isinstance(outs, list)
    shapes = [jax.ShapeDtypeStruct(*out) for out in ([outs] if single else outs)]
    result = pl.pallas_call(
        kernel,
        out_shape=shapes,
        in_specs=specs or [VMEM] * len(operands),
        out_specs=[VMEM] * len(shapes),
        scratch_shapes=list(scratch),
        compiler_params=pltpu.CompilerParams(vmem_limit_bytes=40 * 2**20),
    )(*operands)
    return result[0] if single else result


def normalize(raw):
    values = raw.astype(F32)
    inverse = lax.rsqrt(jnp.sum(values * values, axis=1, keepdims=True) + 1e-06)
    return (values * inverse, inverse)


def through_norm(upstream, normed, inverse):
    return (upstream - normed * jnp.sum(normed * upstream, axis=1, keepdims=True)) * inverse


def along_z(value, steps):
    return lax.ppermute(value, "dp", [(d, (d + 2 * steps) % 16) for d in range(16)])


def swap_y(value):
    return lax.ppermute(value, "dp", [(d, d ^ 1) for d in range(16)])


def swap_core(value):
    return lax.ppermute(value, "mp", [(m, m ^ 1) for m in range(16)])


def normalize_kernel(raw_ref, out_ref):
    out_ref[...] = normalize(raw_ref[...])[0].astype(BF16)


def loss_columns(losses):
    high = losses.astype(BF16)
    low = (losses - high.astype(F32)).astype(BF16)
    lane = lax.broadcasted_iota(jnp.int32, (losses.shape[0], LANES), 1)
    zero = jnp.zeros((), BF16)
    return jnp.where(lane == 0, high, jnp.where(lane == 1, low, zero))


def column_loss(extra):
    values = extra.astype(F32)
    return values[:, 0:1] + values[:, 1:2]


def tile_kernel(*refs):
    numbers, places, text_ids = refs[0], refs[1], refs[2]
    blocks, near, far = refs[3:11], refs[11], refs[12]
    keep_ref, keep_loss, send_ref = refs[13], refs[14], refs[15]
    text_outs, texts, slopes = refs[16:24], refs[24], refs[25]
    sub, width = blocks[0].shape
    for i, block in enumerate(blocks):
        texts[pl.ds(i * sub, sub), :] = block[...]
    scale, bias = numbers[0], numbers[1]
    rows = near.shape[0] // 2
    for part, source in enumerate((near, far)):
        for y in range(2):
            own = pl.ds(y * rows, rows)
            logits = scale * lax.dot_general(
                source[own, :], texts[...], (((1,), (1,)), ((), ())), preferred_element_type=F32
            ) + bias
            ids = places[2 * part + y] + lax.broadcasted_iota(jnp.int32, logits.shape, 0)
            match = ids == text_ids[...]
            u = jnp.where(match, -logits, logits)
            e = jnp.exp(-jnp.abs(u))
            w = 1.0 + e
            grown = jnp.where(w == 1.0, e, jnp.log(w) * (e / jnp.where(w == 1.0, 1.0, w - 1.0)))
            losses = jnp.sum(jnp.maximum(u, 0.0) + grown, axis=1, keepdims=True)
            slope = jnp.where(match, -scale, scale) * (jnp.where(u >= 0.0, 1.0, e) / w)
            slope = slope.astype(BF16)
            slopes[pl.ds((2 * part + y) * rows, rows), :] = slope
            grad = jnp.dot(slope, texts[...], preferred_element_type=F32)
            if part == 0:
                keep_ref[own, :] = grad
                keep_loss[own, :] = losses
            else:
                send_ref[own, pl.ds(0, width)] = grad.astype(BF16)
                send_ref[own, pl.ds(width, LANES)] = loss_columns(losses)
    across = (((0,), (0,)), ((), ()))
    text_grad = lax.dot_general(
        slopes[pl.ds(0, 2 * rows), :], near[...], across, preferred_element_type=F32
    ) + lax.dot_general(
        slopes[pl.ds(2 * rows, 2 * rows), :], far[...], across, preferred_element_type=F32
    )
    for i, out in enumerate(text_outs):
        out[...] = text_grad[i * sub : (i + 1) * sub].astype(BF16)


def join_kernel(keep_ref, keep_loss, came_ref, out_ref):
    width = keep_ref.shape[1]
    out_ref[:, pl.ds(0, width)] = (
        keep_ref[...] + came_ref[:, pl.ds(0, width)].astype(F32)
    ).astype(BF16)
    out_ref[:, pl.ds(width, LANES)] = loss_columns(
        keep_loss[...] + column_loss(came_ref[:, pl.ds(width, LANES)])
    )


def grad_kernel(*refs):
    pieces, blocks = refs[0], refs[1:9]
    raw_img, raw_txt, out_ref = refs[9], refs[10], refs[11]
    rows, width = raw_img.shape
    image_grad = pieces[0, :, pl.ds(0, width)].astype(F32)
    losses = column_loss(pieces[0, :, pl.ds(width, LANES)])
    for i in range(1, pieces.shape[0]):
        image_grad += pieces[i, :, pl.ds(0, width)].astype(F32)
        losses += column_loss(pieces[i, :, pl.ds(width, LANES)])
    text_grad = blocks[0][...].astype(F32)
    for block in blocks[1:]:
        text_grad += block[...].astype(F32)
    d_img = through_norm(image_grad, *normalize(raw_img[...])).astype(BF16)
    d_txt = through_norm(text_grad, *normalize(raw_txt[...])).astype(BF16)
    extra = loss_columns(losses)
    for i in range(out_ref.shape[0]):
        out_ref[i, pl.ds(0, rows), pl.ds(0, width)] = d_img
        out_ref[i, pl.ds(0, rows), pl.ds(width, LANES)] = extra
        out_ref[i, pl.ds(rows, rows), pl.ds(0, width)] = d_txt
        out_ref[i, pl.ds(rows, rows), pl.ds(width, LANES)] = jnp.zeros_like(extra)


def weight_kernel(img_ref, txt_ref, grads_ref, keep_ref, send_ref):
    count, rows = img_ref.shape[0] // 2, grads_ref.shape[1] // 2
    width = keep_ref.shape[1]
    for kind, feats in enumerate((img_ref, txt_ref)):
        grads = jnp.concatenate(
            [
                grads_ref[j, pl.ds(kind * rows, rows), pl.ds(0, width)]
                for j in range(grads_ref.shape[0])
            ],
            axis=0,
        )
        both = jnp.dot(feats[...], grads, preferred_element_type=F32)
        keep_ref[pl.ds(kind * count, count), :] = both[:count]
        send_ref[pl.ds(kind * count, count), :] = both[count:].astype(BF16)


def cut_kernel(keep_ref, came_ref, out_ref):
    rows, cols = out_ref.shape[1:]
    for r in range(4):
        for c in range(4):
            place = (pl.ds(r * rows, rows), pl.ds(c * cols, cols))
            out_ref[4 * r + c] = (keep_ref[place] + came_ref[place].astype(F32)).astype(BF16)


def spread_kernel(parts_ref, out_ref):
    total = parts_ref[0].astype(F32)
    for i in range(1, parts_ref.shape[0]):
        total += parts_ref[i].astype(F32)
    total = total.astype(BF16)
    for i in range(out_ref.shape[0]):
        out_ref[i] = total


def paste_kernel(parts_ref, img_ref, txt_ref):
    rows, cols = parts_ref.shape[1:]
    for r in range(4):
        out = (img_ref, txt_ref)[r // 2]
        for c in range(4):
            out[pl.ds((r % 2) * rows, rows), pl.ds(c * cols, cols)] = parts_ref[4 * r + c].astype(F32)


def shards(img_emb, txt_emb, img_feat_t, txt_feat_t, logit_scale, logit_bias):
    rows, width = img_emb.shape
    sub = txt_emb.shape[0]
    half = rows // 2
    feats = img_feat_t.shape[0]
    dp_index = lax.axis_index("dp").astype(jnp.int32)
    mp_index = lax.axis_index("mp").astype(jnp.int32)
    core, chip = mp_index % 2, mp_index // 2
    z, y = dp_index // 2, dp_index % 2

    texts = local(normalize_kernel, ((sub, width), BF16), [txt_emb])
    blocks = [texts] + [along_z(texts, steps) for steps in ALONG[1:]]

    own = lax.dynamic_slice_in_dim(img_emb, core * half, half, 0)
    partner = swap_y(own)
    near_raw = jnp.where(
        y == 0, jnp.concatenate([own, partner]), jnp.concatenate([partner, own])
    )
    far_raw = swap_core(near_raw)
    near = local(normalize_kernel, ((rows, width), BF16), [near_raw])
    far = local(normalize_kernel, ((rows, width), BF16), [far_raw])

    owners = jnp.stack([2 * ((z - steps) % 8) + y for steps in ALONG])
    text_ids = owners[:, None] * rows + mp_index * sub + jnp.arange(sub, dtype=jnp.int32)[None]
    places = jnp.stack(
        [(2 * z + s) * rows + c * half for c in (core, 1 - core) for s in range(2)]
    ).astype(jnp.int32)
    numbers = jnp.concatenate([logit_scale, logit_bias])
    outs = local(
        tile_kernel,
        [((rows, width), F32), ((rows, 1), F32), ((rows, width + LANES), BF16)]
        + [((sub, width), BF16)] * 8,
        [numbers, places, text_ids.astype(jnp.int32).reshape(1, 8 * sub), *blocks, near, far],
        [SMEM, SMEM] + [VMEM] * 11,
        [pltpu.VMEM((8 * sub, width), BF16), pltpu.VMEM((2 * rows, 8 * sub), BF16)],
    )
    keep, keep_loss, send, text_parts = outs[0], outs[1], outs[2], outs[3:]
    text_came = [text_parts[0]] + [
        along_z(part, -steps) for part, steps in zip(text_parts[1:], ALONG[1:], strict=True)
    ]
    joined = local(
        join_kernel, ((rows, width + LANES), BF16), [keep, keep_loss, swap_core(send)]
    )
    plane = [
        [(2 * s + t) * 16 + 2 * k + c for t in range(2) for k in range(8)]
        for s in range(8)
        for c in range(2)
    ]
    pieces = lax.all_to_all(
        joined.reshape(16, sub, width + LANES), ("dp", "mp"), 0, 0, tiled=True,
        axis_index_groups=plane,
    )
    raw_img = lax.dynamic_slice_in_dim(img_emb, core * half + chip * sub, sub, 0)
    spread = local(
        grad_kernel, ((8, 2 * sub, width + LANES), BF16), [pieces, *text_came, raw_img, txt_emb]
    )
    same_core = [[2 * k + c for k in range(8)] for c in range(2)]
    grads = lax.all_to_all(spread, "mp", 0, 0, tiled=True, axis_index_groups=same_core)

    both_img = jnp.concatenate([img_feat_t, swap_core(img_feat_t)])
    both_txt = jnp.concatenate([txt_feat_t, swap_core(txt_feat_t)])
    img_part = lax.dynamic_slice_in_dim(both_img, core * half, half, 1)
    txt_part = both_txt.reshape(2 * feats, 8, 2, sub)
    txt_part = jnp.where(core == 0, txt_part[:, :, 0], txt_part[:, :, 1]).reshape(2 * feats, half)
    kept, sent = local(
        weight_kernel,
        [((2 * feats, width), F32), ((2 * feats, width), BF16)],
        [img_part, txt_part, grads],
    )
    shape = (16, feats // 2, width // 4)
    cut = local(cut_kernel, (shape, BF16), [kept, swap_core(sent)])
    parts = lax.all_to_all(cut, "dp", 0, 0, tiled=True)
    summed = local(spread_kernel, (shape, BF16), [parts])
    weights = lax.all_to_all(summed, "dp", 0, 0, tiled=True)
    img_weight, txt_weight = local(paste_kernel, [((feats, width), F32)] * 2, [weights])

    extra = grads[:, :sub, width : width + 2].astype(F32)
    own_loss = (extra[:, :, 0] + extra[:, :, 1]).reshape(half)
    other_loss = swap_core(own_loss)
    row_loss = jnp.where(
        core == 0,
        jnp.concatenate([own_loss, other_loss]),
        jnp.concatenate([other_loss, own_loss]),
    )
    return (row_loss, img_weight, txt_weight)


def solution(mesh):
    in_specs = (P("dp", None), P(("dp", "mp"), None), P("mp", "dp"), P("mp", "dp"), P(), P())
    out_specs = (P("dp"), P("mp", None), P("mp", None))
    return jax.shard_map(shards, mesh=mesh, in_specs=in_specs, out_specs=out_specs, check_vma=False)
```

```python
import jax
import jax.numpy as jnp
from jax import lax
from jax.experimental import pallas as pl
from jax.experimental.pallas import tpu as pltpu
from jax.sharding import PartitionSpec as P

F32 = jnp.float32
BF16 = jnp.bfloat16
LANES = 128
ALONG = (0, 1, -1, 2, -2, 3, -3, 4)
VMEM = pl.BlockSpec(memory_space=pltpu.VMEM)
SMEM = pl.BlockSpec(memory_space=pltpu.SMEM)


def local(kernel, outs, operands, mib, specs=None, scratch=()):
    single = not isinstance(outs, list)
    shapes = [jax.ShapeDtypeStruct(*out) for out in ([outs] if single else outs)]
    result = pl.pallas_call(
        kernel,
        out_shape=shapes,
        in_specs=specs or [VMEM] * len(operands),
        out_specs=[VMEM] * len(shapes),
        scratch_shapes=list(scratch),
        compiler_params=pltpu.CompilerParams(vmem_limit_bytes=mib * 2**20),
    )(*operands)
    return result[0] if single else result


def normalize(raw):
    values = raw.astype(F32)
    inverse = lax.rsqrt(jnp.sum(values * values, axis=1, keepdims=True) + 1e-06)
    return (values * inverse, inverse)


def through_norm(upstream, normed, inverse):
    return (upstream - normed * jnp.sum(normed * upstream, axis=1, keepdims=True)) * inverse


def along_z(value, steps):
    return lax.ppermute(value, "dp", [(d, (d + 2 * steps) % 16) for d in range(16)])


def swap_y(value):
    return lax.ppermute(value, "dp", [(d, d ^ 1) for d in range(16)])


def swap_core(value):
    return lax.ppermute(value, "mp", [(m, m ^ 1) for m in range(16)])


def normalize_kernel(raw_ref, out_ref):
    out_ref[...] = normalize(raw_ref[...])[0].astype(BF16)


def loss_columns(losses):
    high = losses.astype(BF16)
    low = (losses - high.astype(F32)).astype(BF16)
    lane = lax.broadcasted_iota(jnp.int32, (losses.shape[0], LANES), 1)
    zero = jnp.zeros((), BF16)
    return jnp.where(lane == 0, high, jnp.where(lane == 1, low, zero))


def column_loss(extra):
    values = extra.astype(F32)
    return values[:, 0:1] + values[:, 1:2]


def tile_kernel(*refs):
    numbers, places, text_ids = refs[0], refs[1], refs[2]
    blocks, own, partner = refs[3:19], refs[19], refs[20]
    image_out, keep_ref, send_ref, texts, images, slopes = refs[21:]
    sub, width = blocks[0].shape
    for i, block in enumerate(blocks):
        texts[pl.ds(i * sub, sub), :] = block[...]
    scale, bias = numbers[0], numbers[1]
    rows = own.shape[0]
    pieces = rows // sub
    for part, source in enumerate((own, partner)):
        place = pl.ds(part * rows, rows)
        images[place, :] = normalize(source[...])[0].astype(BF16)
        logits = scale * lax.dot_general(
            images[place, :], texts[...], (((1,), (1,)), ((), ())), preferred_element_type=F32
        ) + bias
        ids = places[part] + lax.broadcasted_iota(jnp.int32, logits.shape, 0)
        match = ids == text_ids[...]
        u = jnp.where(match, -logits, logits)
        e = jnp.exp(-jnp.abs(u))
        w = 1.0 + e
        grown = jnp.where(w == 1.0, e, jnp.log(w) * (e / jnp.where(w == 1.0, 1.0, w - 1.0)))
        losses = jnp.sum(jnp.maximum(u, 0.0) + grown, axis=1, keepdims=True)
        slope = jnp.where(match, -scale, scale) * (jnp.where(u >= 0.0, 1.0, e) / w)
        slopes[place, :] = slope.astype(BF16)
        grad = jnp.dot(slopes[place, :], texts[...], preferred_element_type=F32).astype(BF16)
        extra = loss_columns(losses)
        first = places[2 + part]
        for i in range(pieces):
            image_out[first + i, :, pl.ds(0, width)] = grad[i * sub : (i + 1) * sub]
            image_out[first + i, :, pl.ds(width, LANES)] = extra[i * sub : (i + 1) * sub]
    text_grad = lax.dot_general(
        slopes[...], images[...], (((0,), (0,)), ((), ())), preferred_element_type=F32
    )
    half = text_grad.shape[0] // 2
    keep_ref[...] = text_grad[:half]
    send_ref[...] = text_grad[half:].astype(BF16)


def join_kernel(keep_ref, came_ref, *outs):
    sub = outs[0].shape[0]
    for i, out in enumerate(outs):
        place = pl.ds(i * sub, sub)
        out[...] = (keep_ref[place, :] + came_ref[place, :].astype(F32)).astype(BF16)


def grad_kernel(*refs):
    pieces, blocks = refs[0], refs[1:9]
    raw_img, raw_txt, out_ref = refs[9], refs[10], refs[11]
    width = raw_img.shape[1]
    image_grad = pieces[0, :, pl.ds(0, width)].astype(F32)
    losses = column_loss(pieces[0, :, pl.ds(width, LANES)])
    for i in range(1, pieces.shape[0]):
        image_grad += pieces[i, :, pl.ds(0, width)].astype(F32)
        losses += column_loss(pieces[i, :, pl.ds(width, LANES)])
    text_grad = blocks[0][...].astype(F32)
    for block in blocks[1:]:
        text_grad += block[...].astype(F32)
    d_img = through_norm(image_grad, *normalize(raw_img[...])).astype(BF16)
    d_txt = through_norm(text_grad, *normalize(raw_txt[...])).astype(BF16)
    extra = loss_columns(losses)
    count = out_ref.shape[0] // 2
    for i in range(2 * count):
        out_ref[i, :, pl.ds(0, width)] = d_img if i < count else d_txt
        out_ref[i, :, pl.ds(width, LANES)] = extra


def weight_kernel(feats_ref, grads_ref, keep_ref, send_ref):
    count, width = keep_ref.shape
    grads = jnp.concatenate(
        [grads_ref[j, :, pl.ds(0, width)] for j in range(grads_ref.shape[0])], axis=0
    )
    both = jnp.dot(feats_ref[...], grads, preferred_element_type=F32)
    keep_ref[...] = both[:count]
    send_ref[...] = both[count:].astype(BF16)


def cut_kernel(keep_ref, came_ref, out_ref):
    rows, cols = out_ref.shape[1:]
    for r in range(2):
        for c in range(4):
            place = (pl.ds(r * rows, rows), pl.ds(c * cols, cols))
            out_ref[4 * r + c] = (keep_ref[place] + came_ref[place].astype(F32)).astype(BF16)


def spread_kernel(parts_ref, out_ref):
    total = parts_ref[0].astype(F32)
    for i in range(1, parts_ref.shape[0]):
        total += parts_ref[i].astype(F32)
    total = total.astype(BF16)
    for i in range(out_ref.shape[0]):
        out_ref[i] = total


def paste_kernel(parts_ref, img_ref, txt_ref):
    rows, cols = parts_ref.shape[1:]
    for s in range(8):
        place = (pl.ds((s // 4) * rows, rows), pl.ds((s % 4) * cols, cols))
        img_ref[place] = parts_ref[2 * s].astype(F32)
        txt_ref[place] = parts_ref[2 * s + 1].astype(F32)


def shards(img_emb, txt_emb, img_feat_t, txt_feat_t, logit_scale, logit_bias):
    rows, width = img_emb.shape
    sub = txt_emb.shape[0]
    half = rows // 2
    feats = img_feat_t.shape[0]
    full = width + LANES
    dp_index = lax.axis_index("dp").astype(jnp.int32)
    mp_index = lax.axis_index("mp").astype(jnp.int32)
    core, chip = mp_index % 2, mp_index // 2
    z, y = dp_index // 2, dp_index % 2

    texts = local(normalize_kernel, ((sub, width), BF16), [txt_emb], 4)
    blocks = [texts] + [along_z(texts, steps) for steps in ALONG[1:]]
    blocks += [swap_core(block) for block in blocks]
    own = lax.dynamic_slice_in_dim(img_emb, core * half, half, 0)
    partner = swap_y(own)

    owners = jnp.stack([2 * ((z - steps) % 8) + y for steps in ALONG])
    cores = jnp.stack([mp_index, mp_index ^ 1])
    text_ids = owners[None, :, None] * rows + cores[:, None, None] * sub
    text_ids = text_ids + jnp.arange(sub, dtype=jnp.int32)[None, None]
    image_start = 2 * z * rows + core * half
    places = jnp.stack([image_start + y * rows, image_start + (1 - y) * rows, 8 * y, 8 * (1 - y)])
    numbers = jnp.concatenate([logit_scale, logit_bias])
    image_part, keep, send = local(
        tile_kernel,
        [((16, sub, full), BF16), ((half, width), F32), ((half, width), BF16)],
        [
            numbers,
            places.astype(jnp.int32),
            text_ids.astype(jnp.int32).reshape(1, rows),
            *blocks,
            own,
            partner,
        ],
        24,
        [SMEM, SMEM] + [VMEM] * 19,
        [pltpu.VMEM((rows, width), BF16)] * 2 + [pltpu.VMEM((rows, rows), BF16)],
    )
    plane = [
        [(2 * s + t) * 16 + 2 * k + c for t in range(2) for k in range(8)]
        for s in range(8)
        for c in range(2)
    ]

    def over_plane(value):
        return lax.all_to_all(
            value, ("dp", "mp"), 0, 0, tiled=True, axis_index_groups=plane
        )

    image_pieces = over_plane(image_part)
    text_parts = local(join_kernel, [((sub, width), BF16)] * 8, [keep, swap_core(send)], 8)
    text_came = [text_parts[0]] + [
        along_z(part, -steps) for part, steps in zip(text_parts[1:], ALONG[1:], strict=True)
    ]
    raw_img = lax.dynamic_slice_in_dim(img_emb, core * half + chip * sub, sub, 0)
    spread = local(
        grad_kernel, ((16, sub, full), BF16), [image_pieces, *text_came, raw_img, txt_emb], 12
    )
    grads = over_plane(spread)

    mine = jnp.where(y == 0, img_feat_t, txt_feat_t)
    came = swap_y(jnp.where(y == 0, txt_feat_t, img_feat_t))
    pair = jnp.where(y == 0, jnp.stack([mine, came], 1), jnp.stack([came, mine], 1))
    pair = jnp.concatenate([pair, swap_core(pair)])
    by_half = pair.reshape(2 * feats, 2, 2, half)
    by_half = jnp.where(core == 0, by_half[:, :, 0], by_half[:, :, 1])
    by_turn = pair.reshape(2 * feats, 2, 8, 2, sub)
    by_turn = jnp.where(core == 0, by_turn[:, :, :, 0], by_turn[:, :, :, 1])
    feat_part = jnp.where(y == 0, by_half.reshape(2 * feats, rows), by_turn.reshape(2 * feats, rows))
    kept, sent = local(
        weight_kernel,
        [((feats, width), F32), ((feats, width), BF16)],
        [feat_part, grads],
        12,
    )
    shape = (feats // 2, width // 4)
    cut = local(cut_kernel, ((8, *shape), BF16), [kept, swap_core(sent)], 6)
    same_y = [[2 * s + t for s in range(8)] for t in range(2)]
    parts = lax.all_to_all(cut, "dp", 0, 0, tiled=True, axis_index_groups=same_y)
    summed = local(spread_kernel, ((16, *shape), BF16), [parts], 6)
    weights = lax.all_to_all(summed, "dp", 0, 0, tiled=True)
    img_weight, txt_weight = local(paste_kernel, [((feats, width), F32)] * 2, [weights], 8)

    extra = grads[:, :, width : width + 2].astype(F32)
    both_loss = (extra[:, :, 0] + extra[:, :, 1]).reshape(2, half)
    own_loss = jnp.where(y == 0, both_loss[0], both_loss[1])
    other_loss = swap_core(own_loss)
    row_loss = jnp.where(
        core == 0,
        jnp.concatenate([own_loss, other_loss]),
        jnp.concatenate([other_loss, own_loss]),
    )
    return (row_loss, img_weight, txt_weight)


def solution(mesh):
    in_specs = (P("dp", None), P(("dp", "mp"), None), P("mp", "dp"), P("mp", "dp"), P(), P())
    out_specs = (P("dp"), P("mp", None), P("mp", None))
    return jax.shard_map(shards, mesh=mesh, in_specs=in_specs, out_specs=out_specs, check_vma=False)
```

```python
import jax
import jax.numpy as jnp
from jax import lax
from jax.experimental import pallas as pl
from jax.experimental.pallas import tpu as pltpu
from jax.sharding import PartitionSpec as P

F32 = jnp.float32
BF16 = jnp.bfloat16
LANES = 128
ALONG = (0, 1, -1, 2, -2, 3, -3, 4)
VMEM = pl.BlockSpec(memory_space=pltpu.VMEM)
SMEM = pl.BlockSpec(memory_space=pltpu.SMEM)
HBM = pl.BlockSpec(memory_space=pltpu.HBM)
ANY = pl.BlockSpec(memory_space=pl.ANY)
DMA = pltpu.SemaphoreType.DMA


def local(kernel, outs, operands, mib, specs=None, out_specs=None, scratch=()):
    single = not isinstance(outs, list)
    shapes = [jax.ShapeDtypeStruct(*out) for out in ([outs] if single else outs)]
    result = pl.pallas_call(
        kernel,
        out_shape=shapes,
        in_specs=specs or [VMEM] * len(operands),
        out_specs=out_specs or [VMEM] * len(shapes),
        scratch_shapes=list(scratch),
        compiler_params=pltpu.CompilerParams(vmem_limit_bytes=mib * 2**20),
    )(*operands)
    return result[0] if single else result


def start_all(pairs, sems):
    copies = [
        pltpu.make_async_copy(source, target, sems.at[i]) for i, (source, target) in enumerate(pairs)
    ]
    for copy in copies:
        copy.start()
    return copies


def wait_all(copies):
    for copy in copies:
        copy.wait()


def normalize(raw):
    values = raw.astype(F32)
    inverse = lax.rsqrt(jnp.sum(values * values, axis=1, keepdims=True) + 1e-06)
    return (values * inverse, inverse)


def through_norm(upstream, normed, inverse):
    return (upstream - normed * jnp.sum(normed * upstream, axis=1, keepdims=True)) * inverse


def along_z(value, steps):
    return lax.ppermute(value, "dp", [(d, (d + 2 * steps) % 16) for d in range(16)])


def swap_y(value):
    return lax.ppermute(value, "dp", [(d, d ^ 1) for d in range(16)])


def swap_core(value):
    return lax.ppermute(value, "mp", [(m, m ^ 1) for m in range(16)])


def normalize_kernel(raw_ref, out_ref):
    out_ref[...] = normalize(raw_ref[...])[0].astype(BF16)


def loss_columns(losses):
    high = losses.astype(BF16)
    low = (losses - high.astype(F32)).astype(BF16)
    lane = lax.broadcasted_iota(jnp.int32, (losses.shape[0], LANES), 1)
    zero = jnp.zeros((), BF16)
    return jnp.where(lane == 0, high, jnp.where(lane == 1, low, zero))


def column_loss(extra):
    values = extra.astype(F32)
    return values[:, 0:1] + values[:, 1:2]


def feature_kernel(flags, mine, came, mine_next, came_next, out_ref):
    count, rows = mine.shape
    half = rows // 2
    y, core = flags[0], flags[1]
    source = lax.broadcasted_iota(jnp.int32, (rows, half), 0)
    target = lax.broadcasted_iota(jnp.int32, (rows, half), 1)
    chosen = source == (target // 32) * 64 + core * 32 + target % 32
    pick = jnp.where(chosen, 1.0, 0.0).astype(BF16)
    for i, (here, there) in enumerate(((mine, came), (mine_next, came_next))):
        own = jnp.dot(here[...], pick, preferred_element_type=F32).astype(BF16)
        other = jnp.dot(there[...], pick, preferred_element_type=F32).astype(BF16)
        place = pl.ds(i * count, count)
        out_ref[place, pl.ds(0, half)] = jnp.where(y == 0, own, other)
        out_ref[place, pl.ds(half, half)] = jnp.where(y == 0, other, own)


def tile_kernel(*refs):
    numbers, places, text_ids, image_ids = refs[0], refs[1], refs[2], refs[3]
    blocks, own, partner = refs[4:20], refs[20], refs[21]
    image_out, keep_ref, send_ref, texts, images, slopes, stage, sems = refs[22:]
    sub, width = blocks[0].shape
    for i, block in enumerate(blocks):
        texts[pl.ds(i * sub, sub), :] = block[...]
    scale, bias = numbers[0], numbers[1]
    rows = own.shape[0]
    pieces = rows // sub
    copies = []
    for part, source in enumerate((own, partner)):
        place = pl.ds(part * rows, rows)
        images[place, :] = normalize(source[...])[0].astype(BF16)
        logits = scale * lax.dot_general(
            images[place, :], texts[...], (((1,), (1,)), ((), ())), preferred_element_type=F32
        ) + bias
        match = image_ids[place, :] == text_ids[...]
        u = jnp.where(match, -logits, logits)
        e = jnp.exp(-jnp.abs(u))
        w = 1.0 + e
        grown = jnp.where(w == 1.0, e, jnp.log(w) * (e / jnp.where(w == 1.0, 1.0, w - 1.0)))
        losses = jnp.sum(jnp.maximum(u, 0.0) + grown, axis=1, keepdims=True)
        slope = jnp.where(match, -scale, scale) * (jnp.where(u >= 0.0, 1.0, e) / w)
        slopes[place, :] = slope.astype(BF16)
        grad = jnp.dot(slopes[place, :], texts[...], preferred_element_type=F32).astype(BF16)
        extra = loss_columns(losses)
        for i in range(pieces):
            stage[part * pieces + i, :, pl.ds(0, width)] = grad[i * sub : (i + 1) * sub]
            stage[part * pieces + i, :, pl.ds(width, LANES)] = extra[i * sub : (i + 1) * sub]
        copy = pltpu.make_async_copy(
            stage.at[pl.ds(part * pieces, pieces)],
            image_out.at[pl.ds(places[part], pieces)],
            sems.at[part],
        )
        copy.start()
        copies.append(copy)
    text_grad = lax.dot_general(
        slopes[...], images[...], (((0,), (0,)), ((), ())), preferred_element_type=F32
    )
    half = text_grad.shape[0] // 2
    keep_ref[...] = text_grad[:half]
    send_ref[...] = text_grad[half:].astype(BF16)
    wait_all(copies)


def join_kernel(keep_ref, came_ref, *refs):
    outs, stage, sems = refs[:8], refs[8], refs[9]
    sub = stage.shape[1]
    for i in range(8):
        place = pl.ds(i * sub, sub)
        stage[i] = (keep_ref[place, :] + came_ref[place, :].astype(F32)).astype(BF16)
    wait_all(start_all([(stage.at[i], out) for i, out in enumerate(outs)], sems))


def grad_kernel(*refs):
    pieces, blocks = refs[0], refs[1:9]
    raw_img, raw_txt, out_ref, came, stage, sems = refs[9:]
    width = raw_img.shape[1]
    loads = start_all([(block, came.at[i]) for i, block in enumerate(blocks)], sems)
    image_grad = pieces[0, :, pl.ds(0, width)].astype(F32)
    losses = column_loss(pieces[0, :, pl.ds(width, LANES)])
    for i in range(1, pieces.shape[0]):
        image_grad += pieces[i, :, pl.ds(0, width)].astype(F32)
        losses += column_loss(pieces[i, :, pl.ds(width, LANES)])
    d_img = through_norm(image_grad, *normalize(raw_img[...])).astype(BF16)
    extra = loss_columns(losses)
    wait_all(loads)
    text_grad = came[0].astype(F32)
    for i in range(1, came.shape[0]):
        text_grad += came[i].astype(F32)
    d_txt = through_norm(text_grad, *normalize(raw_txt[...])).astype(BF16)
    for i, value in enumerate((d_img, d_txt)):
        stage[i, :, pl.ds(0, width)] = value
        stage[i, :, pl.ds(width, LANES)] = extra
    count = out_ref.shape[0]
    wait_all(
        start_all([(stage.at[i // (count // 2)], out_ref.at[i]) for i in range(count)], sems)
    )


def weight_kernel(feats_ref, grads_ref, keep_ref, send_ref):
    count, width = keep_ref.shape
    grads = jnp.concatenate(
        [grads_ref[j, :, pl.ds(0, width)] for j in range(grads_ref.shape[0])], axis=0
    )
    both = jnp.dot(feats_ref[...], grads, preferred_element_type=F32)
    keep_ref[...] = both[:count]
    send_ref[...] = both[count:].astype(BF16)


def cut_kernel(keep_ref, came_ref, out_ref, stage, sem):
    rows, cols = out_ref.shape[1:]
    for r in range(2):
        for c in range(4):
            place = (pl.ds(r * rows, rows), pl.ds(c * cols, cols))
            stage[4 * r + c] = (keep_ref[place] + came_ref[place].astype(F32)).astype(BF16)
    wait_all(start_all([(stage, out_ref)], sem))


def spread_kernel(parts_ref, out_ref, stage, sems):
    total = parts_ref[0].astype(F32)
    for i in range(1, parts_ref.shape[0]):
        total += parts_ref[i].astype(F32)
    stage[...] = total.astype(BF16)
    wait_all(start_all([(stage, out_ref.at[i]) for i in range(out_ref.shape[0])], sems))


def paste_kernel(parts_ref, img_ref, txt_ref):
    rows, cols = parts_ref.shape[1:]
    for s in range(8):
        place = (pl.ds((s // 4) * rows, rows), pl.ds((s % 4) * cols, cols))
        img_ref[place] = parts_ref[2 * s].astype(F32)
        txt_ref[place] = parts_ref[2 * s + 1].astype(F32)


def shards(img_emb, txt_emb, img_feat_t, txt_feat_t, logit_scale, logit_bias):
    rows, width = img_emb.shape
    sub = txt_emb.shape[0]
    half = rows // 2
    feats = img_feat_t.shape[0]
    full = width + LANES
    dp_index = lax.axis_index("dp").astype(jnp.int32)
    mp_index = lax.axis_index("mp").astype(jnp.int32)
    core, chip = mp_index % 2, mp_index // 2
    z, y = dp_index // 2, dp_index % 2

    texts = local(normalize_kernel, ((sub, width), BF16), [txt_emb], 4)
    blocks = [texts] + [along_z(texts, steps) for steps in ALONG[1:]]
    blocks += [swap_core(block) for block in blocks]
    by_core = img_emb.reshape(8, 2, sub, width)
    own = lax.dynamic_slice_in_dim(by_core, core, 1, 1).reshape(half, width)
    partner = swap_y(own)

    mine = jnp.where(y == 0, img_feat_t, txt_feat_t)
    came = swap_y(jnp.where(y == 0, txt_feat_t, img_feat_t))
    feat_part = local(
        feature_kernel,
        ((2 * feats, rows), BF16),
        [jnp.stack([y, core]), mine, came, swap_core(mine), swap_core(came)],
        8,
        [SMEM] + [VMEM] * 4,
    )

    owners = jnp.stack([2 * ((z - steps) % 8) + y for steps in ALONG])
    cores = jnp.stack([mp_index, mp_index ^ 1])
    text_ids = owners[None, :, None] * rows + cores[:, None, None] * sub
    text_ids = text_ids + jnp.arange(sub, dtype=jnp.int32)[None, None]
    count = jnp.arange(half, dtype=jnp.int32)
    in_shard = (count // sub) * 2 * sub + core * sub + count % sub
    image_ids = jnp.concatenate(
        [(2 * z + y) * rows + in_shard, (2 * z + 1 - y) * rows + in_shard]
    )
    places = jnp.stack([8 * y, 8 * (1 - y)])
    numbers = jnp.concatenate([logit_scale, logit_bias])
    numbers, feat_part = lax.optimization_barrier((numbers, feat_part))
    image_part, keep, send = local(
        tile_kernel,
        [((16, sub, full), BF16), ((half, width), F32), ((half, width), BF16)],
        [
            numbers,
            places.astype(jnp.int32),
            text_ids.astype(jnp.int32).reshape(1, rows),
            image_ids.astype(jnp.int32).reshape(rows, 1),
            *blocks,
            own,
            partner,
        ],
        24,
        [SMEM, SMEM] + [VMEM] * 20,
        [HBM, VMEM, VMEM],
        [pltpu.VMEM((rows, width), BF16)] * 2
        + [pltpu.VMEM((rows, rows), BF16), pltpu.VMEM((16, sub, full), BF16), DMA((2,))],
    )
    plane = [
        [(2 * s + t) * 16 + 2 * k + c for t in range(2) for k in range(8)]
        for s in range(8)
        for c in range(2)
    ]

    def over_plane(value):
        return lax.all_to_all(
            value, ("dp", "mp"), 0, 0, tiled=True, axis_index_groups=plane
        )

    text_parts = local(
        join_kernel,
        [((sub, width), BF16)] * 8,
        [keep, swap_core(send)],
        10,
        None,
        [HBM] * 8,
        [pltpu.VMEM((8, sub, width), BF16), DMA((8,))],
    )
    image_part, *text_parts = lax.optimization_barrier((image_part, *text_parts))
    image_pieces = over_plane(image_part)
    text_came = [text_parts[0]] + [
        along_z(part, -steps) for part, steps in zip(text_parts[1:], ALONG[1:], strict=True)
    ]
    raw_img = lax.dynamic_slice_in_dim(img_emb, (2 * chip + core) * sub, sub, 0)
    spread = local(
        grad_kernel,
        ((16, sub, full), BF16),
        [image_pieces, *text_came, raw_img, txt_emb],
        12,
        [VMEM] + [ANY] * 8 + [VMEM] * 2,
        [HBM],
        [pltpu.VMEM((8, sub, width), BF16), pltpu.VMEM((2, sub, full), BF16), DMA((16,))],
    )
    grads = over_plane(spread)

    kept, sent = local(
        weight_kernel,
        [((feats, width), F32), ((feats, width), BF16)],
        [feat_part, grads],
        12,
    )
    shape = (feats // 2, width // 4)
    cut = local(
        cut_kernel,
        ((8, *shape), BF16),
        [kept, swap_core(sent)],
        6,
        None,
        [HBM],
        [pltpu.VMEM((8, *shape), BF16), DMA((1,))],
    )
    same_y = [[2 * s + t for s in range(8)] for t in range(2)]
    parts = lax.all_to_all(cut, "dp", 0, 0, tiled=True, axis_index_groups=same_y)
    summed = local(
        spread_kernel,
        ((16, *shape), BF16),
        [parts],
        6,
        None,
        [HBM],
        [pltpu.VMEM(shape, BF16), DMA((16,))],
    )
    weights = lax.all_to_all(summed, "dp", 0, 0, tiled=True)
    img_weight, txt_weight = local(paste_kernel, [((feats, width), F32)] * 2, [weights], 8)

    extra = grads[:, :, width : width + 2].astype(F32)
    both_loss = (extra[:, :, 0] + extra[:, :, 1]).reshape(2, 8, sub)
    own_loss = jnp.where(y == 0, both_loss[0], both_loss[1])
    other_loss = swap_core(own_loss)
    row_loss = jnp.where(
        core == 0, jnp.stack([own_loss, other_loss], 1), jnp.stack([other_loss, own_loss], 1)
    ).reshape(rows)
    return (row_loss, img_weight, txt_weight)


def solution(mesh):
    in_specs = (P("dp", None), P(("dp", "mp"), None), P("mp", "dp"), P("mp", "dp"), P(), P())
    out_specs = (P("dp"), P("mp", None), P("mp", None))
    return jax.shard_map(shards, mesh=mesh, in_specs=in_specs, out_specs=out_specs, check_vma=False)
```

```python
import jax
import jax.numpy as jnp
from jax import lax
from jax.experimental import pallas as pl
from jax.experimental.pallas import tpu as pltpu
from jax.sharding import PartitionSpec as P

F32 = jnp.float32
BF16 = jnp.bfloat16
LANES = 128
ALONG = (0, 1, -1, 2, -2, 3, -3, 4)
VMEM = pl.BlockSpec(memory_space=pltpu.VMEM)
SMEM = pl.BlockSpec(memory_space=pltpu.SMEM)
HBM = pl.BlockSpec(memory_space=pltpu.HBM)
ANY = pl.BlockSpec(memory_space=pl.ANY)
DMA = pltpu.SemaphoreType.DMA
WHOLE = 58


def local(kernel, outs, operands, mib, specs=None, out_specs=None, scratch=()):
    single = not isinstance(outs, list)
    shapes = [jax.ShapeDtypeStruct(*out) for out in ([outs] if single else outs)]
    result = pl.pallas_call(
        kernel,
        out_shape=shapes,
        in_specs=specs or [VMEM] * len(operands),
        out_specs=out_specs or [VMEM] * len(shapes),
        scratch_shapes=list(scratch),
        compiler_params=pltpu.CompilerParams(vmem_limit_bytes=mib * 2**20),
    )(*operands)
    return result[0] if single else result


def start_all(pairs, sems):
    copies = [
        pltpu.make_async_copy(source, target, sems.at[i]) for i, (source, target) in enumerate(pairs)
    ]
    for copy in copies:
        copy.start()
    return copies


def wait_all(copies):
    for copy in copies:
        copy.wait()


def normalize(raw):
    values = raw.astype(F32)
    inverse = lax.rsqrt(jnp.sum(values * values, axis=1, keepdims=True) + 1e-06)
    return (values * inverse, inverse)


def through_norm(upstream, normed, inverse):
    return (upstream - normed * jnp.sum(normed * upstream, axis=1, keepdims=True)) * inverse


def along_z(value, steps):
    return lax.ppermute(value, "dp", [(d, (d + 2 * steps) % 16) for d in range(16)])


def swap_y(value):
    return lax.ppermute(value, "dp", [(d, d ^ 1) for d in range(16)])


def swap_core(value):
    return lax.ppermute(value, "mp", [(m, m ^ 1) for m in range(16)])


def normalize_kernel(raw_ref, out_ref):
    out_ref[...] = normalize(raw_ref[...])[0].astype(BF16)


def loss_columns(losses):
    high = losses.astype(BF16)
    low = (losses - high.astype(F32)).astype(BF16)
    lane = lax.broadcasted_iota(jnp.int32, (losses.shape[0], LANES), 1)
    zero = jnp.zeros((), BF16)
    return jnp.where(lane == 0, high, jnp.where(lane == 1, low, zero))


def column_loss(extra):
    values = extra.astype(F32)
    return values[:, 0:1] + values[:, 1:2]


def feature_kernel(flags, mine, came, mine_next, came_next, out_ref):
    count, rows = mine.shape
    half = rows // 2
    y, core = flags[0], flags[1]
    source = lax.broadcasted_iota(jnp.int32, (rows, half), 0)
    target = lax.broadcasted_iota(jnp.int32, (rows, half), 1)
    chosen = source == (target // 32) * 64 + core * 32 + target % 32
    pick = jnp.where(chosen, 1.0, 0.0).astype(BF16)
    for i, (here, there) in enumerate(((mine, came), (mine_next, came_next))):
        own = jnp.dot(here[...], pick, preferred_element_type=F32).astype(BF16)
        other = jnp.dot(there[...], pick, preferred_element_type=F32).astype(BF16)
        place = pl.ds(i * count, count)
        out_ref[place, pl.ds(0, half)] = jnp.where(y == 0, own, other)
        out_ref[place, pl.ds(half, half)] = jnp.where(y == 0, other, own)


def tile_kernel(*refs):
    numbers, places, text_ids, image_ids = refs[0], refs[1], refs[2], refs[3]
    blocks, own, partner = refs[4:20], refs[20], refs[21]
    image_out, keep_ref, send_ref, texts, images, slopes, stage, sems = refs[22:]
    sub, width = blocks[0].shape
    for i, block in enumerate(blocks):
        texts[pl.ds(i * sub, sub), :] = block[...]
    scale, bias = numbers[0], numbers[1]
    rows = own.shape[0]
    pieces = rows // sub
    copies = []
    for part, source in enumerate((own, partner)):
        place = pl.ds(part * rows, rows)
        images[place, :] = normalize(source[...])[0].astype(BF16)
        logits = scale * lax.dot_general(
            images[place, :], texts[...], (((1,), (1,)), ((), ())), preferred_element_type=F32
        ) + bias
        match = image_ids[place, :] == text_ids[...]
        u = jnp.where(match, -logits, logits)
        e = jnp.exp(-jnp.abs(u))
        w = 1.0 + e
        grown = jnp.where(w == 1.0, e, jnp.log(w) * (e / jnp.where(w == 1.0, 1.0, w - 1.0)))
        losses = jnp.sum(jnp.maximum(u, 0.0) + grown, axis=1, keepdims=True)
        slope = jnp.where(match, -scale, scale) * (jnp.where(u >= 0.0, 1.0, e) / w)
        slopes[place, :] = slope.astype(BF16)
        grad = jnp.dot(slopes[place, :], texts[...], preferred_element_type=F32).astype(BF16)
        extra = loss_columns(losses)
        for i in range(pieces):
            stage[part * pieces + i, :, pl.ds(0, width)] = grad[i * sub : (i + 1) * sub]
            stage[part * pieces + i, :, pl.ds(width, LANES)] = extra[i * sub : (i + 1) * sub]
        copy = pltpu.make_async_copy(
            stage.at[pl.ds(part * pieces, pieces)],
            image_out.at[pl.ds(places[part], pieces)],
            sems.at[part],
        )
        copy.start()
        copies.append(copy)
    text_grad = lax.dot_general(
        slopes[...], images[...], (((0,), (0,)), ((), ())), preferred_element_type=F32
    )
    half = text_grad.shape[0] // 2
    keep_ref[...] = text_grad[:half]
    send_ref[...] = text_grad[half:].astype(BF16)
    wait_all(copies)


def join_kernel(keep_ref, came_ref, *refs):
    outs, stage, sems = refs[:8], refs[8], refs[9]
    sub = stage.shape[1]
    for i in range(8):
        place = pl.ds(i * sub, sub)
        stage[i] = (keep_ref[place, :] + came_ref[place, :].astype(F32)).astype(BF16)
    wait_all(start_all([(stage.at[i], out) for i, out in enumerate(outs)], sems))


def grad_kernel(*refs):
    pieces, blocks = refs[0], refs[1:9]
    raw_img, raw_txt, out_ref, came, stage, sems = refs[9:]
    width = raw_img.shape[1]
    loads = start_all([(block, came.at[i]) for i, block in enumerate(blocks)], sems)
    image_grad = pieces[0, :, pl.ds(0, width)].astype(F32)
    losses = column_loss(pieces[0, :, pl.ds(width, LANES)])
    for i in range(1, pieces.shape[0]):
        image_grad += pieces[i, :, pl.ds(0, width)].astype(F32)
        losses += column_loss(pieces[i, :, pl.ds(width, LANES)])
    d_img = through_norm(image_grad, *normalize(raw_img[...])).astype(BF16)
    extra = loss_columns(losses)
    wait_all(loads)
    text_grad = came[0].astype(F32)
    for i in range(1, came.shape[0]):
        text_grad += came[i].astype(F32)
    d_txt = through_norm(text_grad, *normalize(raw_txt[...])).astype(BF16)
    for i, value in enumerate((d_img, d_txt)):
        stage[i, :, pl.ds(0, width)] = value
        stage[i, :, pl.ds(width, LANES)] = extra
    count = out_ref.shape[0]
    wait_all(
        start_all([(stage.at[i // (count // 2)], out_ref.at[i]) for i in range(count)], sems)
    )


def weight_kernel(feats_ref, grads_ref, keep_ref, send_ref):
    count, width = keep_ref.shape
    grads = jnp.concatenate(
        [grads_ref[j, :, pl.ds(0, width)] for j in range(grads_ref.shape[0])], axis=0
    )
    both = jnp.dot(feats_ref[...], grads, preferred_element_type=F32)
    keep_ref[...] = both[:count]
    send_ref[...] = both[count:].astype(BF16)


def cut_kernel(keep_ref, came_ref, out_ref, stage, sem):
    rows, cols = out_ref.shape[1:]
    for r in range(2):
        for c in range(4):
            place = (pl.ds(r * rows, rows), pl.ds(c * cols, cols))
            stage[4 * r + c] = (keep_ref[place] + came_ref[place].astype(F32)).astype(BF16)
    wait_all(start_all([(stage, out_ref)], sem))


def spread_kernel(parts_ref, out_ref, stage, sems):
    total = parts_ref[0].astype(F32)
    for i in range(1, parts_ref.shape[0]):
        total += parts_ref[i].astype(F32)
    stage[...] = total.astype(BF16)
    wait_all(start_all([(stage, out_ref.at[i]) for i in range(out_ref.shape[0])], sems))


def paste_kernel(parts_ref, img_ref, txt_ref):
    rows, cols = parts_ref.shape[1:]
    for s in range(8):
        place = (pl.ds((s // 4) * rows, rows), pl.ds((s % 4) * cols, cols))
        img_ref[place] = parts_ref[2 * s].astype(F32)
        txt_ref[place] = parts_ref[2 * s + 1].astype(F32)


def shards(img_emb, txt_emb, img_feat_t, txt_feat_t, logit_scale, logit_bias):
    rows, width = img_emb.shape
    sub = txt_emb.shape[0]
    half = rows // 2
    feats = img_feat_t.shape[0]
    full = width + LANES
    dp_index = lax.axis_index("dp").astype(jnp.int32)
    mp_index = lax.axis_index("mp").astype(jnp.int32)
    core, chip = mp_index % 2, mp_index // 2
    z, y = dp_index // 2, dp_index % 2

    texts = local(normalize_kernel, ((sub, width), BF16), [txt_emb], 4)
    blocks = [texts] + [along_z(texts, steps) for steps in ALONG[1:]]
    blocks += [swap_core(block) for block in blocks]
    by_core = img_emb.reshape(8, 2, sub, width)
    own = lax.dynamic_slice_in_dim(by_core, core, 1, 1).reshape(half, width)
    partner = swap_y(own)

    mine = jnp.where(y == 0, img_feat_t, txt_feat_t)
    theirs = jnp.where(y == 0, txt_feat_t, img_feat_t)
    mine, theirs, *blocks = lax.optimization_barrier((mine, theirs, *blocks))
    came = swap_y(theirs)
    feat_part = local(
        feature_kernel,
        ((2 * feats, rows), BF16),
        [jnp.stack([y, core]), mine, came, swap_core(mine), swap_core(came)],
        WHOLE,
        [SMEM] + [VMEM] * 4,
    )

    owners = jnp.stack([2 * ((z - steps) % 8) + y for steps in ALONG])
    cores = jnp.stack([mp_index, mp_index ^ 1])
    text_ids = owners[None, :, None] * rows + cores[:, None, None] * sub
    text_ids = text_ids + jnp.arange(sub, dtype=jnp.int32)[None, None]
    count = jnp.arange(half, dtype=jnp.int32)
    in_shard = (count // sub) * 2 * sub + core * sub + count % sub
    image_ids = jnp.concatenate(
        [(2 * z + y) * rows + in_shard, (2 * z + 1 - y) * rows + in_shard]
    )
    places = jnp.stack([8 * y, 8 * (1 - y)])
    numbers = jnp.concatenate([logit_scale, logit_bias])
    image_part, keep, send = local(
        tile_kernel,
        [((16, sub, full), BF16), ((half, width), F32), ((half, width), BF16)],
        [
            numbers,
            places.astype(jnp.int32),
            text_ids.astype(jnp.int32).reshape(1, rows),
            image_ids.astype(jnp.int32).reshape(rows, 1),
            *blocks,
            own,
            partner,
        ],
        24,
        [SMEM, SMEM] + [VMEM] * 20,
        [HBM, VMEM, VMEM],
        [pltpu.VMEM((rows, width), BF16)] * 2
        + [pltpu.VMEM((rows, rows), BF16), pltpu.VMEM((16, sub, full), BF16), DMA((2,))],
    )
    plane = [
        [(2 * s + t) * 16 + 2 * k + c for t in range(2) for k in range(8)]
        for s in range(8)
        for c in range(2)
    ]

    def over_plane(value):
        return lax.all_to_all(
            value, ("dp", "mp"), 0, 0, tiled=True, axis_index_groups=plane
        )

    text_parts = local(
        join_kernel,
        [((sub, width), BF16)] * 8,
        [keep, swap_core(send)],
        WHOLE,
        None,
        [HBM] * 8,
        [pltpu.VMEM((8, sub, width), BF16), DMA((8,))],
    )
    image_part, feat_part, *text_parts = lax.optimization_barrier(
        (image_part, feat_part, *text_parts)
    )
    image_pieces = over_plane(image_part)
    text_came = [text_parts[0]] + [
        along_z(part, -steps) for part, steps in zip(text_parts[1:], ALONG[1:], strict=True)
    ]
    raw_img = lax.dynamic_slice_in_dim(img_emb, (2 * chip + core) * sub, sub, 0)
    spread = local(
        grad_kernel,
        ((16, sub, full), BF16),
        [image_pieces, *text_came, raw_img, txt_emb],
        WHOLE,
        [VMEM] + [ANY] * 8 + [VMEM] * 2,
        [HBM],
        [pltpu.VMEM((8, sub, width), BF16), pltpu.VMEM((2, sub, full), BF16), DMA((16,))],
    )
    grads = over_plane(spread)

    kept, sent = local(
        weight_kernel,
        [((feats, width), F32), ((feats, width), BF16)],
        [feat_part, grads],
        12,
    )
    shape = (feats // 2, width // 4)
    cut = local(
        cut_kernel,
        ((8, *shape), BF16),
        [kept, swap_core(sent)],
        6,
        None,
        [HBM],
        [pltpu.VMEM((8, *shape), BF16), DMA((1,))],
    )
    same_y = [[2 * s + t for s in range(8)] for t in range(2)]
    parts = lax.all_to_all(cut, "dp", 0, 0, tiled=True, axis_index_groups=same_y)
    summed = local(
        spread_kernel,
        ((16, *shape), BF16),
        [parts],
        WHOLE,
        None,
        [HBM],
        [pltpu.VMEM(shape, BF16), DMA((16,))],
    )
    weights = lax.all_to_all(summed, "dp", 0, 0, tiled=True)
    img_weight, txt_weight = local(paste_kernel, [((feats, width), F32)] * 2, [weights], 8)

    extra = grads[:, :, width : width + 2].astype(F32)
    both_loss = (extra[:, :, 0] + extra[:, :, 1]).reshape(2, 8, sub)
    own_loss = jnp.where(y == 0, both_loss[0], both_loss[1])
    other_loss = swap_core(own_loss)
    row_loss = jnp.where(
        core == 0, jnp.stack([own_loss, other_loss], 1), jnp.stack([other_loss, own_loss], 1)
    ).reshape(rows)
    return (row_loss, img_weight, txt_weight)


def solution(mesh):
    in_specs = (P("dp", None), P(("dp", "mp"), None), P("mp", "dp"), P("mp", "dp"), P(), P())
    out_specs = (P("dp"), P("mp", None), P("mp", None))
    return jax.shard_map(shards, mesh=mesh, in_specs=in_specs, out_specs=out_specs, check_vma=False)
```

```python
import jax
import jax.numpy as jnp
from jax import lax
from jax.experimental import pallas as pl
from jax.experimental.pallas import tpu as pltpu
from jax.sharding import PartitionSpec as P

F32 = jnp.float32
BF16 = jnp.bfloat16
LANES = 128
ALONG = (0, 1, -1, 2, -2, 3, -3, 4)
VMEM = pl.BlockSpec(memory_space=pltpu.VMEM)
SMEM = pl.BlockSpec(memory_space=pltpu.SMEM)
HBM = pl.BlockSpec(memory_space=pltpu.HBM)
ANY = pl.BlockSpec(memory_space=pl.ANY)
DMA = pltpu.SemaphoreType.DMA
WHOLE = 58


def local(kernel, outs, operands, mib, specs=None, out_specs=None, scratch=()):
    single = not isinstance(outs, list)
    shapes = [jax.ShapeDtypeStruct(*out) for out in ([outs] if single else outs)]
    result = pl.pallas_call(
        kernel,
        out_shape=shapes,
        in_specs=specs or [VMEM] * len(operands),
        out_specs=out_specs or [VMEM] * len(shapes),
        scratch_shapes=list(scratch),
        compiler_params=pltpu.CompilerParams(vmem_limit_bytes=mib * 2**20),
    )(*operands)
    return result[0] if single else result


def start_all(pairs, sems):
    copies = [
        pltpu.make_async_copy(source, target, sems.at[i]) for i, (source, target) in enumerate(pairs)
    ]
    for copy in copies:
        copy.start()
    return copies


def wait_all(copies):
    for copy in copies:
        copy.wait()


def normalize(raw):
    values = raw.astype(F32)
    inverse = lax.rsqrt(jnp.sum(values * values, axis=1, keepdims=True) + 1e-06)
    return (values * inverse, inverse)


def through_norm(upstream, normed, inverse):
    return (upstream - normed * jnp.sum(normed * upstream, axis=1, keepdims=True)) * inverse


def along_z(value, steps):
    return lax.ppermute(value, "dp", [(d, (d + 2 * steps) % 16) for d in range(16)])


def swap_y(value):
    return lax.ppermute(value, "dp", [(d, d ^ 1) for d in range(16)])


def swap_core(value):
    return lax.ppermute(value, "mp", [(m, m ^ 1) for m in range(16)])


def swap_x(value):
    return lax.ppermute(value, "mp", [(m, m ^ 2) for m in range(16)])


def normalize_kernel(raw_ref, out_ref):
    out_ref[...] = normalize(raw_ref[...])[0].astype(BF16)


def loss_columns(losses):
    high = losses.astype(BF16)
    low = (losses - high.astype(F32)).astype(BF16)
    lane = lax.broadcasted_iota(jnp.int32, (losses.shape[0], LANES), 1)
    zero = jnp.zeros((), BF16)
    return jnp.where(lane == 0, high, jnp.where(lane == 1, low, zero))


def column_loss(extra):
    values = extra.astype(F32)
    return values[:, 0:1] + values[:, 1:2]


def feature_kernel(flags, *refs):
    sources, out_ref = refs[:4], refs[4]
    rows = sources[0].shape[1]
    count, half = sources[0].shape[0] // 2, rows // 2
    y, core = flags[0], flags[1]
    source = lax.broadcasted_iota(jnp.int32, (rows, half), 0)
    target = lax.broadcasted_iota(jnp.int32, (rows, half), 1)
    chosen = source == (target // 32) * 64 + core * 32 + target % 32
    pick = jnp.where(chosen, 1.0, 0.0).astype(BF16)
    for i, ref in enumerate(sources):
        both = jnp.dot(ref[...], pick, preferred_element_type=F32)
        own, other = both[:count].astype(BF16), both[count:].astype(BF16)
        place = pl.ds(i * count, count)
        out_ref[place, pl.ds(0, half)] = jnp.where(y == 0, own, other)
        out_ref[place, pl.ds(half, half)] = jnp.where(y == 0, other, own)


def tile_kernel(*refs):
    numbers, places, text_ids, image_ids = refs[0], refs[1], refs[2], refs[3]
    blocks, own, partner = refs[4:20], refs[20], refs[21]
    image_out, keep_ref, send_ref, texts, images, slopes = refs[22:]
    sub, width = blocks[0].shape
    for i, block in enumerate(blocks):
        texts[pl.ds(i * sub, sub), :] = block[...]
    scale, bias = numbers[0], numbers[1]
    rows = own.shape[0]
    pieces = rows // sub
    for part, source in enumerate((own, partner)):
        place = pl.ds(part * rows, rows)
        images[place, :] = normalize(source[...])[0].astype(BF16)
        logits = scale * lax.dot_general(
            images[place, :], texts[...], (((1,), (1,)), ((), ())), preferred_element_type=F32
        ) + bias
        match = image_ids[place, :] == text_ids[...]
        u = jnp.where(match, -logits, logits)
        e = jnp.exp(-jnp.abs(u))
        w = 1.0 + e
        grown = jnp.where(w == 1.0, e, jnp.log(w) * (e / jnp.where(w == 1.0, 1.0, w - 1.0)))
        losses = jnp.sum(jnp.maximum(u, 0.0) + grown, axis=1, keepdims=True)
        slope = jnp.where(match, -scale, scale) * (jnp.where(u >= 0.0, 1.0, e) / w)
        slopes[place, :] = slope.astype(BF16)
        grad = jnp.dot(slopes[place, :], texts[...], preferred_element_type=F32).astype(BF16)
        extra = loss_columns(losses)
        first = places[part]
        for i in range(pieces):
            image_out[first + i, :, pl.ds(0, width)] = grad[i * sub : (i + 1) * sub]
            image_out[first + i, :, pl.ds(width, LANES)] = extra[i * sub : (i + 1) * sub]
    text_grad = lax.dot_general(
        slopes[...], images[...], (((0,), (0,)), ((), ())), preferred_element_type=F32
    )
    half = text_grad.shape[0] // 2
    keep_ref[...] = text_grad[:half]
    send_ref[...] = text_grad[half:].astype(BF16)


def join_kernel(keep_ref, came_ref, *refs):
    outs, stage, sems = refs[:8], refs[8], refs[9]
    sub = stage.shape[1]
    for i in range(8):
        place = pl.ds(i * sub, sub)
        stage[i] = (keep_ref[place, :] + came_ref[place, :].astype(F32)).astype(BF16)
    wait_all(start_all([(stage.at[i], out) for i, out in enumerate(outs)], sems))


def text_kernel(*refs):
    blocks, raw_txt, out_ref, came, sems = refs[:8], *refs[8:]
    wait_all(start_all([(block, came.at[i]) for i, block in enumerate(blocks)], sems))
    text_grad = came[0].astype(F32)
    for i in range(1, came.shape[0]):
        text_grad += came[i].astype(F32)
    out_ref[...] = through_norm(text_grad, *normalize(raw_txt[...])).astype(BF16)


def grad_kernel(pieces, d_txt, raw_img, out_ref):
    width = raw_img.shape[1]
    half = width // 2
    image_grad = pieces[0, :, pl.ds(0, width)].astype(F32)
    losses = column_loss(pieces[0, :, pl.ds(width, LANES)])
    for i in range(1, pieces.shape[0]):
        image_grad += pieces[i, :, pl.ds(0, width)].astype(F32)
        losses += column_loss(pieces[i, :, pl.ds(width, LANES)])
    d_img = through_norm(image_grad, *normalize(raw_img[...])).astype(BF16)
    extra = loss_columns(losses)
    for h in range(2):
        place = pl.ds(h * half, half)
        out_ref[0, h, :, pl.ds(0, half)] = d_img[:, h * half : (h + 1) * half]
        out_ref[1, h, :, pl.ds(0, half)] = d_txt[:, place]
        for kind in range(2):
            out_ref[kind, h, :, pl.ds(half, LANES)] = extra


def weight_kernel(feats_ref, grads_ref, keep_ref, send_ref):
    count, width = keep_ref.shape
    grads = jnp.concatenate(
        [grads_ref[j, :, pl.ds(0, width)] for j in range(grads_ref.shape[0])], axis=0
    )
    both = jnp.dot(feats_ref[...], grads, preferred_element_type=F32)
    keep_ref[...] = both[:count]
    send_ref[...] = both[count:].astype(BF16)


def cut_kernel(keep_ref, came_ref, out_ref):
    rows, cols = out_ref.shape[2:]
    total = keep_ref[...] + came_ref[...].astype(F32)
    for part in range(2):
        for s in range(8):
            row, col = part * 4 * rows + (s // 2) * rows, (s % 2) * cols
            out_ref[s, part] = total[row : row + rows, col : col + cols].astype(BF16)


def sum_kernel(parts_ref, own_ref, other_ref):
    for part, out in enumerate((own_ref, other_ref)):
        total = parts_ref[0, part].astype(F32)
        for i in range(1, parts_ref.shape[0]):
            total += parts_ref[i, part].astype(F32)
        out[...] = total.astype(BF16)


def paste_kernel(flags, parts_ref, img_ref, txt_ref):
    rows, cols = parts_ref.shape[2:]
    first = flags[0] == 0
    for s in range(8):
        row, col = (s // 2) * rows, (s % 2) * cols
        for kind, out in enumerate((img_ref, txt_ref)):
            own, other = parts_ref[2 * s + kind, 0], parts_ref[2 * s + kind, 1]
            out[pl.ds(row, rows), pl.ds(col, cols)] = jnp.where(first, own, other).astype(F32)
            out[pl.ds(row, rows), pl.ds(2 * cols + col, cols)] = jnp.where(
                first, other, own
            ).astype(F32)


def shards(img_emb, txt_emb, img_feat_t, txt_feat_t, logit_scale, logit_bias):
    rows, width = img_emb.shape
    sub = txt_emb.shape[0]
    half = rows // 2
    feats = img_feat_t.shape[0]
    full = width + LANES
    dp_index = lax.axis_index("dp").astype(jnp.int32)
    mp_index = lax.axis_index("mp").astype(jnp.int32)
    core, chip = mp_index % 2, mp_index // 2
    z, y = dp_index // 2, dp_index % 2

    texts = local(normalize_kernel, ((sub, width), BF16), [txt_emb], 4)
    blocks = [texts] + [along_z(texts, steps) for steps in ALONG[1:]]
    blocks += [swap_core(block) for block in blocks]
    mine = jnp.where(y == 0, img_feat_t, txt_feat_t)
    came = swap_y(jnp.where(y == 0, txt_feat_t, img_feat_t))
    by_core = img_emb.reshape(8, 2, sub, width)
    own = lax.dynamic_slice_in_dim(by_core, core, 1, 1).reshape(half, width)
    own, came = lax.optimization_barrier((own, came))
    partner = swap_y(own)
    pair = jnp.concatenate([mine, came])
    pair_x = swap_x(pair)
    feat_part = local(
        feature_kernel,
        ((4 * feats, rows), BF16),
        [jnp.stack([y, core]), pair, pair_x, swap_core(pair), swap_core(pair_x)],
        8,
        [SMEM] + [VMEM] * 4,
    )

    owners = jnp.stack([2 * ((z - steps) % 8) + y for steps in ALONG])
    cores = jnp.stack([mp_index, mp_index ^ 1])
    text_ids = owners[None, :, None] * rows + cores[:, None, None] * sub
    text_ids = text_ids + jnp.arange(sub, dtype=jnp.int32)[None, None]
    count = jnp.arange(half, dtype=jnp.int32)
    in_shard = (count // sub) * 2 * sub + core * sub + count % sub
    image_ids = jnp.concatenate(
        [(2 * z + y) * rows + in_shard, (2 * z + 1 - y) * rows + in_shard]
    )
    places = jnp.stack([8 * y, 8 * (1 - y)])
    numbers = jnp.concatenate([logit_scale, logit_bias])
    numbers, feat_part = lax.optimization_barrier((numbers, feat_part))
    image_part, keep, send = local(
        tile_kernel,
        [((16, sub, full), BF16), ((half, width), F32), ((half, width), BF16)],
        [
            numbers,
            places.astype(jnp.int32),
            text_ids.astype(jnp.int32).reshape(1, rows),
            image_ids.astype(jnp.int32).reshape(rows, 1),
            *blocks,
            own,
            partner,
        ],
        24,
        [SMEM, SMEM] + [VMEM] * 20,
        None,
        [pltpu.VMEM((rows, width), BF16)] * 2
        + [pltpu.VMEM((rows, rows), BF16)],
    )
    plane = [
        [(2 * s + t) * 16 + 2 * k + c for t in range(2) for k in range(8)]
        for s in range(8)
        for c in range(2)
    ]

    def over_plane(value):
        return lax.all_to_all(
            value, ("dp", "mp"), 0, 0, tiled=True, axis_index_groups=plane
        )

    text_parts = local(
        join_kernel,
        [((sub, width), BF16)] * 8,
        [keep, swap_core(send)],
        WHOLE,
        None,
        [HBM] * 8,
        [pltpu.VMEM((8, sub, width), BF16), DMA((8,))],
    )
    image_pieces = over_plane(image_part)
    text_came = [text_parts[0]] + [
        along_z(part, -steps) for part, steps in zip(text_parts[1:], ALONG[1:], strict=True)
    ]
    d_txt = local(
        text_kernel,
        ((sub, width), BF16),
        [*text_came, txt_emb],
        WHOLE,
        [ANY] * 8 + [VMEM],
        None,
        [pltpu.VMEM((8, sub, width), BF16), DMA((8,))],
    )
    raw_img = lax.dynamic_slice_in_dim(img_emb, (2 * chip + core) * sub, sub, 0)
    narrow = width // 2
    kinds = local(
        grad_kernel,
        ((2, 2, sub, narrow + LANES), BF16),
        [image_pieces, d_txt, raw_img],
        12,
    )
    spread = jnp.broadcast_to(kinds[:, None], (2, 4, 2, sub, narrow + LANES))
    grads = over_plane(spread.reshape(16, sub, narrow + LANES))

    kept, sent = local(
        weight_kernel,
        [((2 * feats, narrow), F32), ((2 * feats, narrow), BF16)],
        [feat_part, grads],
        12,
    )
    shape = (feats // 4, narrow // 2)
    cut = local(cut_kernel, ((8, 2, *shape), BF16), [kept, swap_core(sent)], 6)
    same_y = [[2 * s + t for s in range(8)] for t in range(2)]
    parts = lax.all_to_all(cut, "dp", 0, 0, tiled=True, axis_index_groups=same_y)
    own_sum, other_sum = local(sum_kernel, [(shape, BF16)] * 2, [parts], 6)
    summed = jnp.stack([own_sum, swap_x(other_sum)])
    weights = lax.all_to_all(
        jnp.broadcast_to(summed[None], (16, 2, *shape)), "dp", 0, 0, tiled=True
    )
    img_weight, txt_weight = local(
        paste_kernel,
        [((feats, width), F32)] * 2,
        [(chip % 2).reshape(1), weights],
        8,
        [SMEM, VMEM],
    )

    extra = grads[:, :, narrow : narrow + 2].astype(F32)
    both_loss = (extra[:, :, 0] + extra[:, :, 1]).reshape(2, 8, sub)
    own_loss = jnp.where(y == 0, both_loss[0], both_loss[1])
    other_loss = swap_core(own_loss)
    row_loss = jnp.where(
        core == 0, jnp.stack([own_loss, other_loss], 1), jnp.stack([other_loss, own_loss], 1)
    ).reshape(rows)
    return (row_loss, img_weight, txt_weight)


def solution(mesh):
    in_specs = (P("dp", None), P(("dp", "mp"), None), P("mp", "dp"), P("mp", "dp"), P(), P())
    out_specs = (P("dp"), P("mp", None), P("mp", None))
    return jax.shard_map(shards, mesh=mesh, in_specs=in_specs, out_specs=out_specs, check_vma=False)
```

```python
import jax
import jax.numpy as jnp
from jax import lax
from jax.experimental import pallas as pl
from jax.experimental.pallas import tpu as pltpu
from jax.sharding import PartitionSpec as P

F32 = jnp.float32
BF16 = jnp.bfloat16
LANES = 128
ALONG = (0, 1, -1, 2, -2, 3, -3, 4)
VMEM = pl.BlockSpec(memory_space=pltpu.VMEM)
SMEM = pl.BlockSpec(memory_space=pltpu.SMEM)
HBM = pl.BlockSpec(memory_space=pltpu.HBM)
ANY = pl.BlockSpec(memory_space=pl.ANY)
DMA = pltpu.SemaphoreType.DMA
WHOLE = 58


def local(kernel, outs, operands, mib, specs=None, out_specs=None, scratch=()):
    single = not isinstance(outs, list)
    shapes = [jax.ShapeDtypeStruct(*out) for out in ([outs] if single else outs)]
    result = pl.pallas_call(
        kernel,
        out_shape=shapes,
        in_specs=specs or [VMEM] * len(operands),
        out_specs=out_specs or [VMEM] * len(shapes),
        scratch_shapes=list(scratch),
        compiler_params=pltpu.CompilerParams(vmem_limit_bytes=mib * 2**20),
    )(*operands)
    return result[0] if single else result


def start_all(pairs, sems):
    copies = [
        pltpu.make_async_copy(source, target, sems.at[i]) for i, (source, target) in enumerate(pairs)
    ]
    for copy in copies:
        copy.start()
    return copies


def wait_all(copies):
    for copy in copies:
        copy.wait()


def normalize(raw):
    values = raw.astype(F32)
    inverse = lax.rsqrt(jnp.sum(values * values, axis=1, keepdims=True) + 1e-06)
    return (values * inverse, inverse)


def through_norm(upstream, normed, inverse):
    return (upstream - normed * jnp.sum(normed * upstream, axis=1, keepdims=True)) * inverse


def along_z(value, steps):
    return lax.ppermute(value, "dp", [(d, (d + 2 * steps) % 16) for d in range(16)])


def swap_y(value):
    return lax.ppermute(value, "dp", [(d, d ^ 1) for d in range(16)])


def swap_core(value):
    return lax.ppermute(value, "mp", [(m, m ^ 1) for m in range(16)])


def swap_x(value):
    return lax.ppermute(value, "mp", [(m, m ^ 2) for m in range(16)])


def loss_columns(losses):
    high = losses.astype(BF16)
    low = (losses - high.astype(F32)).astype(BF16)
    lane = lax.broadcasted_iota(jnp.int32, (losses.shape[0], LANES), 1)
    zero = jnp.zeros((), BF16)
    return jnp.where(lane == 0, high, jnp.where(lane == 1, low, zero))


def column_loss(extra):
    values = extra.astype(F32)
    return values[:, 0:1] + values[:, 1:2]


def feature_kernel(flags, *refs):
    sources, out_ref = refs[:4], refs[4]
    rows = sources[0].shape[1]
    count, half = sources[0].shape[0] // 2, rows // 2
    y, core = flags[0], flags[1]
    source = lax.broadcasted_iota(jnp.int32, (rows, half), 0)
    target = lax.broadcasted_iota(jnp.int32, (rows, half), 1)
    chosen = source == (target // 32) * 64 + core * 32 + target % 32
    pick = jnp.where(chosen, 1.0, 0.0).astype(BF16)
    for i, ref in enumerate(sources):
        both = jnp.dot(ref[...], pick, preferred_element_type=F32)
        own, other = both[:count].astype(BF16), both[count:].astype(BF16)
        place = pl.ds(i * count, count)
        out_ref[place, pl.ds(0, half)] = jnp.where(y == 0, own, other)
        out_ref[place, pl.ds(half, half)] = jnp.where(y == 0, other, own)


def tile_kernel(*refs):
    numbers, places, text_ids, image_ids = refs[0], refs[1], refs[2], refs[3]
    blocks, own, partner = refs[4:6], refs[6], refs[7]
    image_out, keep_ref, send_ref, texts, images, slopes = refs[8:]
    sub, width = image_out.shape[1], own.shape[1]
    scale, bias = numbers[0], numbers[1]
    rows = own.shape[0]
    pieces = rows // sub
    for i, block in enumerate(blocks):
        texts[pl.ds(i * rows, rows), :] = normalize(block[...])[0].astype(BF16)
    for part, source in enumerate((own, partner)):
        place = pl.ds(part * rows, rows)
        images[place, :] = normalize(source[...])[0].astype(BF16)
        logits = scale * lax.dot_general(
            images[place, :], texts[...], (((1,), (1,)), ((), ())), preferred_element_type=F32
        ) + bias
        match = image_ids[place, :] == text_ids[...]
        u = jnp.where(match, -logits, logits)
        e = jnp.exp(-jnp.abs(u))
        w = 1.0 + e
        grown = jnp.where(w == 1.0, e, jnp.log(w) * (e / jnp.where(w == 1.0, 1.0, w - 1.0)))
        losses = jnp.sum(jnp.maximum(u, 0.0) + grown, axis=1, keepdims=True)
        slope = jnp.where(match, -scale, scale) * (jnp.where(u >= 0.0, 1.0, e) / w)
        slopes[place, :] = slope.astype(BF16)
        grad = jnp.dot(slopes[place, :], texts[...], preferred_element_type=F32).astype(BF16)
        extra = loss_columns(losses)
        first = places[part]
        for i in range(pieces):
            image_out[first + i, :, pl.ds(0, width)] = grad[i * sub : (i + 1) * sub]
            image_out[first + i, :, pl.ds(width, LANES)] = extra[i * sub : (i + 1) * sub]
    text_grad = lax.dot_general(
        slopes[...], images[...], (((0,), (0,)), ((), ())), preferred_element_type=F32
    )
    half = text_grad.shape[0] // 2
    keep_ref[...] = text_grad[:half]
    send_ref[...] = text_grad[half:].astype(BF16)


def join_kernel(flags, keep_ref, came_ref, *refs):
    outs, stage, sems = refs[:8], refs[8], refs[9]
    sub = stage.shape[1]
    for i, steps in enumerate(ALONG):
        owner = lax.rem(flags[0] + (8 - steps), 8)
        place = pl.ds(pl.multiple_of(owner * sub, sub), sub)
        stage[i] = (keep_ref[place, :] + came_ref[place, :].astype(F32)).astype(BF16)
    wait_all(start_all([(stage.at[i], out) for i, out in enumerate(outs)], sems))


def text_kernel(*refs):
    blocks, raw_txt, out_ref, came, sems = refs[:8], *refs[8:]
    wait_all(start_all([(block, came.at[i]) for i, block in enumerate(blocks)], sems))
    text_grad = came[0].astype(F32)
    for i in range(1, came.shape[0]):
        text_grad += came[i].astype(F32)
    out_ref[...] = through_norm(text_grad, *normalize(raw_txt[...])).astype(BF16)


def grad_kernel(pieces, d_txt, raw_img, out_ref):
    width = raw_img.shape[1]
    half = width // 2
    image_grad = pieces[0, :, pl.ds(0, width)].astype(F32)
    losses = column_loss(pieces[0, :, pl.ds(width, LANES)])
    for i in range(1, pieces.shape[0]):
        image_grad += pieces[i, :, pl.ds(0, width)].astype(F32)
        losses += column_loss(pieces[i, :, pl.ds(width, LANES)])
    d_img = through_norm(image_grad, *normalize(raw_img[...])).astype(BF16)
    extra = loss_columns(losses)
    for h in range(2):
        place = pl.ds(h * half, half)
        out_ref[0, h, :, pl.ds(0, half)] = d_img[:, h * half : (h + 1) * half]
        out_ref[1, h, :, pl.ds(0, half)] = d_txt[:, place]
        for kind in range(2):
            out_ref[kind, h, :, pl.ds(half, LANES)] = extra


def weight_kernel(feats_ref, grads_ref, keep_ref, send_ref):
    count, width = keep_ref.shape
    grads = jnp.concatenate(
        [grads_ref[j, :, pl.ds(0, width)] for j in range(grads_ref.shape[0])], axis=0
    )
    both = jnp.dot(feats_ref[...], grads, preferred_element_type=F32)
    keep_ref[...] = both[:count]
    send_ref[...] = both[count:].astype(BF16)


def cut_kernel(keep_ref, came_ref, out_ref):
    rows, cols = out_ref.shape[2:]
    total = keep_ref[...] + came_ref[...].astype(F32)
    for part in range(2):
        for s in range(8):
            row, col = part * 4 * rows + (s // 2) * rows, (s % 2) * cols
            out_ref[s, part] = total[row : row + rows, col : col + cols].astype(BF16)


def sum_kernel(parts_ref, own_ref, other_ref):
    for part, out in enumerate((own_ref, other_ref)):
        total = parts_ref[0, part].astype(F32)
        for i in range(1, parts_ref.shape[0]):
            total += parts_ref[i, part].astype(F32)
        out[...] = total.astype(BF16)


def paste_kernel(flags, parts_ref, img_ref, txt_ref):
    rows, cols = parts_ref.shape[2:]
    first = flags[0] == 0
    for s in range(8):
        row, col = (s // 2) * rows, (s % 2) * cols
        for kind, out in enumerate((img_ref, txt_ref)):
            own, other = parts_ref[2 * s + kind, 0], parts_ref[2 * s + kind, 1]
            out[pl.ds(row, rows), pl.ds(col, cols)] = jnp.where(first, own, other).astype(F32)
            out[pl.ds(row, rows), pl.ds(2 * cols + col, cols)] = jnp.where(
                first, other, own
            ).astype(F32)


def shards(img_emb, txt_emb, img_feat_t, txt_feat_t, logit_scale, logit_bias):
    rows, width = img_emb.shape
    sub = txt_emb.shape[0]
    half = rows // 2
    feats = img_feat_t.shape[0]
    full = width + LANES
    dp_index = lax.axis_index("dp").astype(jnp.int32)
    mp_index = lax.axis_index("mp").astype(jnp.int32)
    core, chip = mp_index % 2, mp_index // 2
    z, y = dp_index // 2, dp_index % 2

    same_y = [[2 * s + t for s in range(8)] for t in range(2)]

    def over_z(value):
        return lax.all_to_all(value, "dp", 0, 0, tiled=True, axis_index_groups=same_y)

    texts = over_z(jnp.broadcast_to(txt_emb[None], (8, sub, width))).reshape(half, width)
    mine = jnp.where(y == 0, img_feat_t, txt_feat_t)
    came = swap_y(jnp.where(y == 0, txt_feat_t, img_feat_t))
    by_core = img_emb.reshape(8, 2, sub, width)
    own = lax.dynamic_slice_in_dim(by_core, core, 1, 1).reshape(half, width)
    partner = swap_y(own)
    pair = jnp.concatenate([mine, came])
    pair_x = swap_x(pair)
    feat_part = local(
        feature_kernel,
        ((4 * feats, rows), BF16),
        [jnp.stack([y, core]), pair, pair_x, swap_core(pair), swap_core(pair_x)],
        8,
        [SMEM] + [VMEM] * 4,
    )

    owners = 2 * jnp.arange(8, dtype=jnp.int32) + y
    cores = jnp.stack([mp_index, mp_index ^ 1])
    text_ids = owners[None, :, None] * rows + cores[:, None, None] * sub
    text_ids = text_ids + jnp.arange(sub, dtype=jnp.int32)[None, None]
    count = jnp.arange(half, dtype=jnp.int32)
    in_shard = (count // sub) * 2 * sub + core * sub + count % sub
    image_ids = jnp.concatenate(
        [(2 * z + y) * rows + in_shard, (2 * z + 1 - y) * rows + in_shard]
    )
    places = jnp.stack([8 * y, 8 * (1 - y)])
    numbers = jnp.concatenate([logit_scale, logit_bias])
    numbers, feat_part = lax.optimization_barrier((numbers, feat_part))
    image_part, keep, send = local(
        tile_kernel,
        [((16, sub, full), BF16), ((half, width), F32), ((half, width), BF16)],
        [
            numbers,
            places.astype(jnp.int32),
            text_ids.astype(jnp.int32).reshape(1, rows),
            image_ids.astype(jnp.int32).reshape(rows, 1),
            texts,
            swap_core(texts),
            own,
            partner,
        ],
        24,
        [SMEM, SMEM] + [VMEM] * 6,
        None,
        [pltpu.VMEM((rows, width), BF16)] * 2
        + [pltpu.VMEM((rows, rows), BF16)],
    )
    plane = [
        [(2 * s + t) * 16 + 2 * k + c for t in range(2) for k in range(8)]
        for s in range(8)
        for c in range(2)
    ]

    def over_plane(value):
        return lax.all_to_all(
            value, ("dp", "mp"), 0, 0, tiled=True, axis_index_groups=plane
        )

    came_grad = swap_core(send)
    image_part, came_grad = lax.optimization_barrier((image_part, came_grad))
    text_parts = local(
        join_kernel,
        [((sub, width), BF16)] * 8,
        [z.reshape(1), keep, came_grad],
        WHOLE,
        [SMEM, VMEM, VMEM],
        [HBM] * 8,
        [pltpu.VMEM((8, sub, width), BF16), DMA((8,))],
    )
    image_pieces = over_plane(image_part)
    text_came = [text_parts[0]] + [
        along_z(part, -steps) for part, steps in zip(text_parts[1:], ALONG[1:], strict=True)
    ]
    d_txt = local(
        text_kernel,
        ((sub, width), BF16),
        [*text_came, txt_emb],
        WHOLE,
        [ANY] * 8 + [VMEM],
        None,
        [pltpu.VMEM((8, sub, width), BF16), DMA((8,))],
    )
    raw_img = lax.dynamic_slice_in_dim(img_emb, (2 * chip + core) * sub, sub, 0)
    narrow = width // 2
    kinds = local(
        grad_kernel,
        ((2, 2, sub, narrow + LANES), BF16),
        [image_pieces, d_txt, raw_img],
        12,
    )
    spread = jnp.broadcast_to(kinds[:, None], (2, 4, 2, sub, narrow + LANES))
    grads = over_plane(spread.reshape(16, sub, narrow + LANES))

    kept, sent = local(
        weight_kernel,
        [((2 * feats, narrow), F32), ((2 * feats, narrow), BF16)],
        [feat_part, grads],
        12,
    )
    shape = (feats // 4, narrow // 2)
    cut = local(cut_kernel, ((8, 2, *shape), BF16), [kept, swap_core(sent)], 6)
    parts = over_z(cut)
    own_sum, other_sum = local(sum_kernel, [(shape, BF16)] * 2, [parts], 6)
    summed = jnp.stack([own_sum, swap_x(other_sum)])
    weights = lax.all_to_all(
        jnp.broadcast_to(summed[None], (16, 2, *shape)), "dp", 0, 0, tiled=True
    )
    img_weight, txt_weight = local(
        paste_kernel,
        [((feats, width), F32)] * 2,
        [(chip % 2).reshape(1), weights],
        8,
        [SMEM, VMEM],
    )

    extra = grads[:, :, narrow : narrow + 2].astype(F32)
    both_loss = (extra[:, :, 0] + extra[:, :, 1]).reshape(2, 8, sub)
    own_loss = jnp.where(y == 0, both_loss[0], both_loss[1])
    other_loss = swap_core(own_loss)
    row_loss = jnp.where(
        core == 0, jnp.stack([own_loss, other_loss], 1), jnp.stack([other_loss, own_loss], 1)
    ).reshape(rows)
    return (row_loss, img_weight, txt_weight)


def solution(mesh):
    in_specs = (P("dp", None), P(("dp", "mp"), None), P("mp", "dp"), P("mp", "dp"), P(), P())
    out_specs = (P("dp"), P("mp", None), P("mp", None))
    return jax.shard_map(shards, mesh=mesh, in_specs=in_specs, out_specs=out_specs, check_vma=False)
```

```python
import jax
import jax.numpy as jnp
from jax import lax
from jax.experimental import pallas as pl
from jax.experimental.pallas import tpu as pltpu
from jax.sharding import PartitionSpec as P

F32 = jnp.float32
BF16 = jnp.bfloat16
LANES = 128
ALONG = (0, 1, -1, 2, -2, 3, -3, 4)
VMEM = pl.BlockSpec(memory_space=pltpu.VMEM)
SMEM = pl.BlockSpec(memory_space=pltpu.SMEM)
HBM = pl.BlockSpec(memory_space=pltpu.HBM)
ANY = pl.BlockSpec(memory_space=pl.ANY)
DMA = pltpu.SemaphoreType.DMA
WHOLE = 58


def local(kernel, outs, operands, mib, specs=None, out_specs=None, scratch=(), cost=None):
    single = not isinstance(outs, list)
    shapes = [jax.ShapeDtypeStruct(*out) for out in ([outs] if single else outs)]
    result = pl.pallas_call(
        kernel,
        out_shape=shapes,
        in_specs=specs or [VMEM] * len(operands),
        out_specs=out_specs or [VMEM] * len(shapes),
        scratch_shapes=list(scratch),
        cost_estimate=cost and pl.CostEstimate(flops=cost, bytes_accessed=0, transcendentals=0),
        compiler_params=pltpu.CompilerParams(vmem_limit_bytes=mib * 2**20),
    )(*operands)
    return result[0] if single else result


def start_all(pairs, sems):
    copies = [
        pltpu.make_async_copy(source, target, sems.at[i]) for i, (source, target) in enumerate(pairs)
    ]
    for copy in copies:
        copy.start()
    return copies


def wait_all(copies):
    for copy in copies:
        copy.wait()


def normalize(raw):
    values = raw.astype(F32)
    inverse = lax.rsqrt(jnp.sum(values * values, axis=1, keepdims=True) + 1e-06)
    return (values * inverse, inverse)


def through_norm(upstream, normed, inverse):
    return (upstream - normed * jnp.sum(normed * upstream, axis=1, keepdims=True)) * inverse


def along_z(value, steps):
    return lax.ppermute(value, "dp", [(d, (d + 2 * steps) % 16) for d in range(16)])


def swap_y(value):
    return lax.ppermute(value, "dp", [(d, d ^ 1) for d in range(16)])


def swap_core(value):
    return lax.ppermute(value, "mp", [(m, m ^ 1) for m in range(16)])


def swap_x(value):
    return lax.ppermute(value, "mp", [(m, m ^ 2) for m in range(16)])


def loss_columns(losses):
    high = losses.astype(BF16)
    low = (losses - high.astype(F32)).astype(BF16)
    lane = lax.broadcasted_iota(jnp.int32, (losses.shape[0], LANES), 1)
    zero = jnp.zeros((), BF16)
    return jnp.where(lane == 0, high, jnp.where(lane == 1, low, zero))


def column_loss(extra):
    values = extra.astype(F32)
    return values[:, 0:1] + values[:, 1:2]


def feature_kernel(flags, *refs):
    sources, out_ref = refs[:4], refs[4]
    rows = sources[0].shape[1]
    count, half = sources[0].shape[0] // 2, rows // 2
    y, core = flags[0], flags[1]
    source = lax.broadcasted_iota(jnp.int32, (rows, half), 0)
    target = lax.broadcasted_iota(jnp.int32, (rows, half), 1)
    chosen = source == (target // 32) * 64 + core * 32 + target % 32
    pick = jnp.where(chosen, 1.0, 0.0).astype(BF16)
    for i, ref in enumerate(sources):
        both = jnp.dot(ref[...], pick, preferred_element_type=F32)
        own, other = both[:count].astype(BF16), both[count:].astype(BF16)
        place = pl.ds(i * count, count)
        out_ref[place, pl.ds(0, half)] = jnp.where(y == 0, own, other)
        out_ref[place, pl.ds(half, half)] = jnp.where(y == 0, other, own)


def tile_kernel(
    numbers, text_ids, image_ids, near, far, own, partner,
    texts, slopes, loss_ref, keep_ref, send_ref, images,
):
    scale, bias = numbers[0], numbers[1]
    rows = own.shape[0]
    for i, block in enumerate((near, far)):
        texts[pl.ds(i * rows, rows), :] = normalize(block[...])[0].astype(BF16)
    for part, source in enumerate((own, partner)):
        place = pl.ds(part * rows, rows)
        images[place, :] = normalize(source[...])[0].astype(BF16)
        logits = scale * lax.dot_general(
            images[place, :], texts[...], (((1,), (1,)), ((), ())), preferred_element_type=F32
        ) + bias
        match = image_ids[place, :] == text_ids[...]
        u = jnp.where(match, -logits, logits)
        e = jnp.exp(-jnp.abs(u))
        w = 1.0 + e
        grown = jnp.where(w == 1.0, e, jnp.log(w) * (e / jnp.where(w == 1.0, 1.0, w - 1.0)))
        loss_ref[place, :] = jnp.sum(jnp.maximum(u, 0.0) + grown, axis=1, keepdims=True)
        slope = jnp.where(match, -scale, scale) * (jnp.where(u >= 0.0, 1.0, e) / w)
        slopes[place, :] = slope.astype(BF16)
    text_grad = lax.dot_general(
        slopes[...], images[...], (((0,), (0,)), ((), ())), preferred_element_type=F32
    )
    half = text_grad.shape[0] // 2
    keep_ref[...] = text_grad[:half]
    send_ref[...] = text_grad[half:].astype(BF16)


def image_kernel(places, texts, slopes, loss_ref, image_out):
    sub, width = image_out.shape[1], texts.shape[1]
    rows = slopes.shape[0] // 2
    for part in range(2):
        place = pl.ds(part * rows, rows)
        grad = jnp.dot(slopes[place, :], texts[...], preferred_element_type=F32).astype(BF16)
        extra = loss_columns(loss_ref[place, :])
        first = places[part]
        for i in range(rows // sub):
            image_out[first + i, :, pl.ds(0, width)] = grad[i * sub : (i + 1) * sub]
            image_out[first + i, :, pl.ds(width, LANES)] = extra[i * sub : (i + 1) * sub]


def join_kernel(flags, keep_ref, came_ref, *refs):
    outs, stage, sems = refs[:8], refs[8], refs[9]
    sub = stage.shape[1]
    for i, steps in enumerate(ALONG):
        owner = lax.rem(flags[0] + (8 - steps), 8)
        place = pl.ds(pl.multiple_of(owner * sub, sub), sub)
        stage[i] = (keep_ref[place, :] + came_ref[place, :].astype(F32)).astype(BF16)
    wait_all(start_all([(stage.at[i], out) for i, out in enumerate(outs)], sems))


def text_kernel(*refs):
    blocks, raw_txt, out_ref, came, sems = refs[:8], *refs[8:]
    wait_all(start_all([(block, came.at[i]) for i, block in enumerate(blocks)], sems))
    text_grad = came[0].astype(F32)
    for i in range(1, came.shape[0]):
        text_grad += came[i].astype(F32)
    out_ref[...] = through_norm(text_grad, *normalize(raw_txt[...])).astype(BF16)


def grad_kernel(pieces, d_txt, raw_img, out_ref):
    width = raw_img.shape[1]
    half = width // 2
    image_grad = pieces[0, :, pl.ds(0, width)].astype(F32)
    losses = column_loss(pieces[0, :, pl.ds(width, LANES)])
    for i in range(1, pieces.shape[0]):
        image_grad += pieces[i, :, pl.ds(0, width)].astype(F32)
        losses += column_loss(pieces[i, :, pl.ds(width, LANES)])
    d_img = through_norm(image_grad, *normalize(raw_img[...])).astype(BF16)
    extra = loss_columns(losses)
    for h in range(2):
        place = pl.ds(h * half, half)
        out_ref[0, h, :, pl.ds(0, half)] = d_img[:, h * half : (h + 1) * half]
        out_ref[1, h, :, pl.ds(0, half)] = d_txt[:, place]
        for kind in range(2):
            out_ref[kind, h, :, pl.ds(half, LANES)] = extra


def weight_kernel(feats_ref, grads_ref, keep_ref, send_ref):
    count, width = keep_ref.shape
    grads = jnp.concatenate(
        [grads_ref[j, :, pl.ds(0, width)] for j in range(grads_ref.shape[0])], axis=0
    )
    both = jnp.dot(feats_ref[...], grads, preferred_element_type=F32)
    keep_ref[...] = both[:count]
    send_ref[...] = both[count:].astype(BF16)


def cut_kernel(keep_ref, came_ref, out_ref):
    rows, cols = out_ref.shape[2:]
    total = keep_ref[...] + came_ref[...].astype(F32)
    for part in range(2):
        for s in range(8):
            row, col = part * 4 * rows + (s // 2) * rows, (s % 2) * cols
            out_ref[s, part] = total[row : row + rows, col : col + cols].astype(BF16)


def sum_kernel(parts_ref, own_ref, other_ref):
    for part, out in enumerate((own_ref, other_ref)):
        total = parts_ref[0, part].astype(F32)
        for i in range(1, parts_ref.shape[0]):
            total += parts_ref[i, part].astype(F32)
        out[...] = total.astype(BF16)


def paste_kernel(flags, parts_ref, img_ref, txt_ref):
    rows, cols = parts_ref.shape[2:]
    first = flags[0] == 0
    for s in range(8):
        row, col = (s // 2) * rows, (s % 2) * cols
        for kind, out in enumerate((img_ref, txt_ref)):
            own, other = parts_ref[2 * s + kind, 0], parts_ref[2 * s + kind, 1]
            out[pl.ds(row, rows), pl.ds(col, cols)] = jnp.where(first, own, other).astype(F32)
            out[pl.ds(row, rows), pl.ds(2 * cols + col, cols)] = jnp.where(
                first, other, own
            ).astype(F32)


def shards(img_emb, txt_emb, img_feat_t, txt_feat_t, logit_scale, logit_bias):
    rows, width = img_emb.shape
    sub = txt_emb.shape[0]
    half = rows // 2
    feats = img_feat_t.shape[0]
    full = width + LANES
    dp_index = lax.axis_index("dp").astype(jnp.int32)
    mp_index = lax.axis_index("mp").astype(jnp.int32)
    core, chip = mp_index % 2, mp_index // 2
    z, y = dp_index // 2, dp_index % 2

    same_y = [[2 * s + t for s in range(8)] for t in range(2)]

    def over_z(value):
        return lax.all_to_all(value, "dp", 0, 0, tiled=True, axis_index_groups=same_y)

    texts = over_z(jnp.broadcast_to(txt_emb[None], (8, sub, width))).reshape(half, width)
    mine = jnp.where(y == 0, img_feat_t, txt_feat_t)
    came = swap_y(jnp.where(y == 0, txt_feat_t, img_feat_t))
    by_core = img_emb.reshape(8, 2, sub, width)
    own = lax.dynamic_slice_in_dim(by_core, core, 1, 1).reshape(half, width)
    partner = swap_y(own)
    pair = jnp.concatenate([mine, came])
    pair_x = swap_x(pair)
    owners = 2 * jnp.arange(8, dtype=jnp.int32) + y
    cores = jnp.stack([mp_index, mp_index ^ 1])
    text_ids = owners[None, :, None] * rows + cores[:, None, None] * sub
    text_ids = text_ids + jnp.arange(sub, dtype=jnp.int32)[None, None]
    count = jnp.arange(half, dtype=jnp.int32)
    in_shard = (count // sub) * 2 * sub + core * sub + count % sub
    image_ids = jnp.concatenate(
        [(2 * z + y) * rows + in_shard, (2 * z + 1 - y) * rows + in_shard]
    )
    places = jnp.stack([8 * y, 8 * (1 - y)])
    numbers = jnp.concatenate([logit_scale, logit_bias])
    unit, slope, losses, keep, send = local(
        tile_kernel,
        [
            ((rows, width), BF16),
            ((rows, rows), BF16),
            ((rows, 1), F32),
            ((half, width), F32),
            ((half, width), BF16),
        ],
        [
            numbers,
            text_ids.astype(jnp.int32).reshape(1, rows),
            image_ids.astype(jnp.int32).reshape(rows, 1),
            texts,
            swap_core(texts),
            own,
            partner,
        ],
        24,
        [SMEM] + [VMEM] * 6,
        None,
        [pltpu.VMEM((rows, width), BF16)],
        4 * 10**9,
    )
    came_grad = swap_core(send)
    image_part = local(
        image_kernel,
        ((16, sub, full), BF16),
        [places.astype(jnp.int32), unit, slope, losses],
        16,
        [SMEM] + [VMEM] * 3,
        cost=2 * 10**9,
    )
    plane = [
        [(2 * s + t) * 16 + 2 * k + c for t in range(2) for k in range(8)]
        for s in range(8)
        for c in range(2)
    ]

    def over_plane(value):
        return lax.all_to_all(
            value, ("dp", "mp"), 0, 0, tiled=True, axis_index_groups=plane
        )

    text_parts = local(
        join_kernel,
        [((sub, width), BF16)] * 8,
        [z.reshape(1), keep, came_grad],
        WHOLE,
        [SMEM, VMEM, VMEM],
        [HBM] * 8,
        [pltpu.VMEM((8, sub, width), BF16), DMA((8,))],
    )
    image_part, pair_x, *text_parts = lax.optimization_barrier((image_part, pair_x, *text_parts))
    image_pieces = over_plane(image_part)
    text_came = [text_parts[0]] + [
        along_z(part, -steps) for part, steps in zip(text_parts[1:], ALONG[1:], strict=True)
    ]
    d_txt = local(
        text_kernel,
        ((sub, width), BF16),
        [*text_came, txt_emb],
        WHOLE,
        [ANY] * 8 + [VMEM],
        None,
        [pltpu.VMEM((8, sub, width), BF16), DMA((8,))],
    )
    feat_part = local(
        feature_kernel,
        ((4 * feats, rows), BF16),
        [jnp.stack([y, core]), pair, pair_x, swap_core(pair), swap_core(pair_x)],
        8,
        [SMEM] + [VMEM] * 4,
    )
    raw_img = lax.dynamic_slice_in_dim(img_emb, (2 * chip + core) * sub, sub, 0)
    raw_img, feat_part = lax.optimization_barrier((raw_img, feat_part))
    narrow = width // 2
    kinds = local(
        grad_kernel,
        ((2, 2, sub, narrow + LANES), BF16),
        [image_pieces, d_txt, raw_img],
        12,
    )
    spread = jnp.broadcast_to(kinds[:, None], (2, 4, 2, sub, narrow + LANES))
    grads = over_plane(spread.reshape(16, sub, narrow + LANES))

    kept, sent = local(
        weight_kernel,
        [((2 * feats, narrow), F32), ((2 * feats, narrow), BF16)],
        [feat_part, grads],
        12,
    )
    shape = (feats // 4, narrow // 2)
    cut = local(cut_kernel, ((8, 2, *shape), BF16), [kept, swap_core(sent)], 6)
    parts = over_z(cut)
    own_sum, other_sum = local(sum_kernel, [(shape, BF16)] * 2, [parts], 6)
    summed = jnp.stack([own_sum, swap_x(other_sum)])
    weights = lax.all_to_all(
        jnp.broadcast_to(summed[None], (16, 2, *shape)), "dp", 0, 0, tiled=True
    )
    img_weight, txt_weight = local(
        paste_kernel,
        [((feats, width), F32)] * 2,
        [(chip % 2).reshape(1), weights],
        8,
        [SMEM, VMEM],
    )

    extra = grads[:, :, narrow : narrow + 2].astype(F32)
    both_loss = (extra[:, :, 0] + extra[:, :, 1]).reshape(2, 8, sub)
    own_loss = jnp.where(y == 0, both_loss[0], both_loss[1])
    other_loss = swap_core(own_loss)
    row_loss = jnp.where(
        core == 0, jnp.stack([own_loss, other_loss], 1), jnp.stack([other_loss, own_loss], 1)
    ).reshape(rows)
    return (row_loss, img_weight, txt_weight)


def solution(mesh):
    in_specs = (P("dp", None), P(("dp", "mp"), None), P("mp", "dp"), P("mp", "dp"), P(), P())
    out_specs = (P("dp"), P("mp", None), P("mp", None))
    return jax.shard_map(shards, mesh=mesh, in_specs=in_specs, out_specs=out_specs, check_vma=False)
```

```python
import jax
import jax.numpy as jnp
from jax import lax
from jax.experimental import pallas as pl
from jax.experimental.pallas import tpu as pltpu
from jax.sharding import PartitionSpec as P

F32 = jnp.float32
BF16 = jnp.bfloat16
LANES = 128
ALONG = (0, 1, -1, 2, -2, 3, -3, 4)
VMEM = pl.BlockSpec(memory_space=pltpu.VMEM)
SMEM = pl.BlockSpec(memory_space=pltpu.SMEM)
HBM = pl.BlockSpec(memory_space=pltpu.HBM)
ANY = pl.BlockSpec(memory_space=pl.ANY)
DMA = pltpu.SemaphoreType.DMA
WHOLE = 58


def local(kernel, outs, operands, mib, specs=None, out_specs=None, scratch=()):
    single = not isinstance(outs, list)
    shapes = [jax.ShapeDtypeStruct(*out) for out in ([outs] if single else outs)]
    result = pl.pallas_call(
        kernel,
        out_shape=shapes,
        in_specs=specs or [VMEM] * len(operands),
        out_specs=out_specs or [VMEM] * len(shapes),
        scratch_shapes=list(scratch),
        compiler_params=pltpu.CompilerParams(vmem_limit_bytes=mib * 2**20),
    )(*operands)
    return result[0] if single else result


def start_all(pairs, sems):
    copies = [
        pltpu.make_async_copy(source, target, sems.at[i]) for i, (source, target) in enumerate(pairs)
    ]
    for copy in copies:
        copy.start()
    return copies


def wait_all(copies):
    for copy in copies:
        copy.wait()


def normalize(raw):
    values = raw.astype(F32)
    inverse = lax.rsqrt(jnp.sum(values * values, axis=1, keepdims=True) + 1e-06)
    return (values * inverse, inverse)


def through_norm(upstream, normed, inverse):
    return (upstream - normed * jnp.sum(normed * upstream, axis=1, keepdims=True)) * inverse


def along_z(value, steps):
    return lax.ppermute(value, "dp", [(d, (d + 2 * steps) % 16) for d in range(16)])


def swap_y(value):
    return lax.ppermute(value, "dp", [(d, d ^ 1) for d in range(16)])


def swap_core(value):
    return lax.ppermute(value, "mp", [(m, m ^ 1) for m in range(16)])


def swap_x(value):
    return lax.ppermute(value, "mp", [(m, m ^ 2) for m in range(16)])


def normalize_kernel(raw_ref, out_ref):
    out_ref[...] = normalize(raw_ref[...])[0].astype(BF16)


def loss_columns(losses):
    high = losses.astype(BF16)
    low = (losses - high.astype(F32)).astype(BF16)
    lane = lax.broadcasted_iota(jnp.int32, (losses.shape[0], LANES), 1)
    zero = jnp.zeros((), BF16)
    return jnp.where(lane == 0, high, jnp.where(lane == 1, low, zero))


def column_loss(extra):
    values = extra.astype(F32)
    return values[:, 0:1] + values[:, 1:2]


def feature_kernel(flags, *refs):
    sources, out_ref = refs[:4], refs[4]
    rows = sources[0].shape[1]
    count, half = sources[0].shape[0] // 2, rows // 2
    y, core = flags[0], flags[1]
    source = lax.broadcasted_iota(jnp.int32, (rows, half), 0)
    target = lax.broadcasted_iota(jnp.int32, (rows, half), 1)
    chosen = source == (target // 32) * 64 + core * 32 + target % 32
    pick = jnp.where(chosen, 1.0, 0.0).astype(BF16)
    for i, ref in enumerate(sources):
        both = jnp.dot(ref[...], pick, preferred_element_type=F32)
        own, other = both[:count].astype(BF16), both[count:].astype(BF16)
        place = pl.ds(i * count, count)
        out_ref[place, pl.ds(0, half)] = jnp.where(y == 0, own, other)
        out_ref[place, pl.ds(half, half)] = jnp.where(y == 0, other, own)


def tile_kernel(*refs):
    numbers, places, text_ids, image_ids = refs[0], refs[1], refs[2], refs[3]
    blocks, own, partner = refs[4:20], refs[20], refs[21]
    image_out, keep_ref, send_ref, texts, images, slopes = refs[22:]
    sub, width = blocks[0].shape
    scale, bias = numbers[0], numbers[1]
    rows = own.shape[0]
    pieces = rows // sub
    for i, block in enumerate(blocks):
        texts[pl.ds(i * sub, sub), :] = block[...]
    for part, source in enumerate((own, partner)):
        place = pl.ds(part * rows, rows)
        images[place, :] = normalize(source[...])[0].astype(BF16)
        logits = scale * lax.dot_general(
            images[place, :], texts[...], (((1,), (1,)), ((), ())), preferred_element_type=F32
        ) + bias
        match = image_ids[place, :] == text_ids[...]
        u = jnp.where(match, -logits, logits)
        e = jnp.exp(-jnp.abs(u))
        w = 1.0 + e
        grown = jnp.where(w == 1.0, e, jnp.log(w) * (e / jnp.where(w == 1.0, 1.0, w - 1.0)))
        losses = jnp.sum(jnp.maximum(u, 0.0) + grown, axis=1, keepdims=True)
        slope = jnp.where(match, -scale, scale) * (jnp.where(u >= 0.0, 1.0, e) / w)
        slopes[place, :] = slope.astype(BF16)
        grad = jnp.dot(slopes[place, :], texts[...], preferred_element_type=F32).astype(BF16)
        extra = loss_columns(losses)
        first = places[part]
        for i in range(pieces):
            image_out[first + i, :, pl.ds(0, width)] = grad[i * sub : (i + 1) * sub]
            image_out[first + i, :, pl.ds(width, LANES)] = extra[i * sub : (i + 1) * sub]
    text_grad = lax.dot_general(
        slopes[...], images[...], (((0,), (0,)), ((), ())), preferred_element_type=F32
    )
    half = text_grad.shape[0] // 2
    keep_ref[...] = text_grad[:half]
    send_ref[...] = text_grad[half:].astype(BF16)


def join_kernel(keep_ref, came_ref, *refs):
    outs, stage, sems = refs[:8], refs[8], refs[9]
    sub = stage.shape[1]
    for i in range(8):
        place = pl.ds(i * sub, sub)
        stage[i] = (keep_ref[place, :] + came_ref[place, :].astype(F32)).astype(BF16)
    wait_all(start_all([(stage.at[i], out) for i, out in enumerate(outs)], sems))


def text_kernel(*refs):
    blocks, raw_txt, out_ref, came, sems = refs[:8], *refs[8:]
    wait_all(start_all([(block, came.at[i]) for i, block in enumerate(blocks)], sems))
    text_grad = came[0].astype(F32)
    for i in range(1, came.shape[0]):
        text_grad += came[i].astype(F32)
    out_ref[...] = through_norm(text_grad, *normalize(raw_txt[...])).astype(BF16)


def grad_kernel(pieces, d_txt, raw_img, out_ref):
    width = raw_img.shape[1]
    half = width // 2
    image_grad = pieces[0, :, pl.ds(0, width)].astype(F32)
    losses = column_loss(pieces[0, :, pl.ds(width, LANES)])
    for i in range(1, pieces.shape[0]):
        image_grad += pieces[i, :, pl.ds(0, width)].astype(F32)
        losses += column_loss(pieces[i, :, pl.ds(width, LANES)])
    d_img = through_norm(image_grad, *normalize(raw_img[...])).astype(BF16)
    extra = loss_columns(losses)
    for h in range(2):
        place = pl.ds(h * half, half)
        out_ref[0, h, :, pl.ds(0, half)] = d_img[:, h * half : (h + 1) * half]
        out_ref[1, h, :, pl.ds(0, half)] = d_txt[:, place]
        for kind in range(2):
            out_ref[kind, h, :, pl.ds(half, LANES)] = extra


def weight_kernel(feats_ref, grads_ref, keep_ref, send_ref):
    count, width = keep_ref.shape
    grads = jnp.concatenate(
        [grads_ref[j, :, pl.ds(0, width)] for j in range(grads_ref.shape[0])], axis=0
    )
    both = jnp.dot(feats_ref[...], grads, preferred_element_type=F32)
    keep_ref[...] = both[:count]
    send_ref[...] = both[count:].astype(BF16)


def cut_kernel(keep_ref, came_ref, out_ref):
    rows, cols = out_ref.shape[2:]
    total = keep_ref[...] + came_ref[...].astype(F32)
    for part in range(2):
        for s in range(8):
            row, col = part * 4 * rows + (s // 2) * rows, (s % 2) * cols
            out_ref[s, part] = total[row : row + rows, col : col + cols].astype(BF16)


def sum_kernel(parts_ref, own_ref, other_ref):
    for part, out in enumerate((own_ref, other_ref)):
        total = parts_ref[0, part].astype(F32)
        for i in range(1, parts_ref.shape[0]):
            total += parts_ref[i, part].astype(F32)
        out[...] = total.astype(BF16)


def paste_kernel(flags, parts_ref, img_ref, txt_ref):
    rows, cols = parts_ref.shape[2:]
    first = flags[0] == 0
    for s in range(8):
        row, col = (s // 2) * rows, (s % 2) * cols
        for kind, out in enumerate((img_ref, txt_ref)):
            own, other = parts_ref[2 * s + kind, 0], parts_ref[2 * s + kind, 1]
            out[pl.ds(row, rows), pl.ds(col, cols)] = jnp.where(first, own, other).astype(F32)
            out[pl.ds(row, rows), pl.ds(2 * cols + col, cols)] = jnp.where(
                first, other, own
            ).astype(F32)


def shards(img_emb, txt_emb, img_feat_t, txt_feat_t, logit_scale, logit_bias):
    rows, width = img_emb.shape
    sub = txt_emb.shape[0]
    half = rows // 2
    feats = img_feat_t.shape[0]
    full = width + LANES
    dp_index = lax.axis_index("dp").astype(jnp.int32)
    mp_index = lax.axis_index("mp").astype(jnp.int32)
    core, chip = mp_index % 2, mp_index // 2
    z, y = dp_index // 2, dp_index % 2

    same_y = [[2 * s + t for s in range(8)] for t in range(2)]

    def over_z(value):
        return lax.all_to_all(value, "dp", 0, 0, tiled=True, axis_index_groups=same_y)

    texts = local(normalize_kernel, ((sub, width), BF16), [txt_emb], 4)
    blocks = [texts] + [along_z(texts, steps) for steps in ALONG[1:]]
    blocks += [swap_core(block) for block in blocks]
    by_core = img_emb.reshape(8, 2, sub, width)
    own = lax.dynamic_slice_in_dim(by_core, core, 1, 1).reshape(half, width)
    partner = swap_y(own)

    owners = jnp.stack([2 * ((z - steps) % 8) + y for steps in ALONG])
    cores = jnp.stack([mp_index, mp_index ^ 1])
    text_ids = owners[None, :, None] * rows + cores[:, None, None] * sub
    text_ids = text_ids + jnp.arange(sub, dtype=jnp.int32)[None, None]
    count = jnp.arange(half, dtype=jnp.int32)
    in_shard = (count // sub) * 2 * sub + core * sub + count % sub
    image_ids = jnp.concatenate(
        [(2 * z + y) * rows + in_shard, (2 * z + 1 - y) * rows + in_shard]
    )
    places = jnp.stack([8 * y, 8 * (1 - y)])
    numbers = jnp.concatenate([logit_scale, logit_bias])
    image_part, keep, send = local(
        tile_kernel,
        [((16, sub, full), BF16), ((half, width), F32), ((half, width), BF16)],
        [
            numbers,
            places.astype(jnp.int32),
            text_ids.astype(jnp.int32).reshape(1, rows),
            image_ids.astype(jnp.int32).reshape(rows, 1),
            *blocks,
            own,
            partner,
        ],
        24,
        [SMEM, SMEM] + [VMEM] * 20,
        None,
        [pltpu.VMEM((rows, width), BF16)] * 2
        + [pltpu.VMEM((rows, rows), BF16)],
    )
    plane = [
        [(2 * s + t) * 16 + 2 * k + c for t in range(2) for k in range(8)]
        for s in range(8)
        for c in range(2)
    ]

    def over_plane(value):
        return lax.all_to_all(
            value, ("dp", "mp"), 0, 0, tiled=True, axis_index_groups=plane
        )

    came_grad = swap_core(send)
    mine = jnp.where(y == 0, img_feat_t, txt_feat_t)
    theirs = jnp.where(y == 0, txt_feat_t, img_feat_t)
    mine, theirs, partner = lax.optimization_barrier((mine, theirs, partner))
    pair = jnp.concatenate([mine, swap_y(theirs)])
    pair_x = swap_x(pair)
    image_part, came_grad, pair_x = lax.optimization_barrier((image_part, came_grad, pair_x))
    feat_part = local(
        feature_kernel,
        ((4 * feats, rows), BF16),
        [jnp.stack([y, core]), pair, pair_x, swap_core(pair), swap_core(pair_x)],
        8,
        [SMEM] + [VMEM] * 4,
    )
    text_parts = local(
        join_kernel,
        [((sub, width), BF16)] * 8,
        [keep, came_grad],
        WHOLE,
        None,
        [HBM] * 8,
        [pltpu.VMEM((8, sub, width), BF16), DMA((8,))],
    )
    image_pieces = over_plane(image_part)
    text_came = [text_parts[0]] + [
        along_z(part, -steps) for part, steps in zip(text_parts[1:], ALONG[1:], strict=True)
    ]
    raw_txt, feat_part = lax.optimization_barrier((txt_emb, feat_part))
    d_txt = local(
        text_kernel,
        ((sub, width), BF16),
        [*text_came, raw_txt],
        WHOLE,
        [ANY] * 8 + [VMEM],
        None,
        [pltpu.VMEM((8, sub, width), BF16), DMA((8,))],
    )
    raw_img = lax.dynamic_slice_in_dim(img_emb, (2 * chip + core) * sub, sub, 0)
    narrow = width // 2
    kinds = local(
        grad_kernel,
        ((2, 2, sub, narrow + LANES), BF16),
        [image_pieces, d_txt, raw_img],
        12,
    )
    spread = jnp.broadcast_to(kinds[:, None], (2, 4, 2, sub, narrow + LANES))
    grads = over_plane(spread.reshape(16, sub, narrow + LANES))

    kept, sent = local(
        weight_kernel,
        [((2 * feats, narrow), F32), ((2 * feats, narrow), BF16)],
        [feat_part, grads],
        12,
    )
    shape = (feats // 4, narrow // 2)
    cut = local(cut_kernel, ((8, 2, *shape), BF16), [kept, swap_core(sent)], 6)
    parts = over_z(cut)
    own_sum, other_sum = local(sum_kernel, [(shape, BF16)] * 2, [parts], 6)
    summed = jnp.stack([own_sum, swap_x(other_sum)])
    weights = lax.all_to_all(
        jnp.broadcast_to(summed[None], (16, 2, *shape)), "dp", 0, 0, tiled=True
    )
    img_weight, txt_weight = local(
        paste_kernel,
        [((feats, width), F32)] * 2,
        [(chip % 2).reshape(1), weights],
        8,
        [SMEM, VMEM],
    )

    extra = grads[:, :, narrow : narrow + 2].astype(F32)
    both_loss = (extra[:, :, 0] + extra[:, :, 1]).reshape(2, 8, sub)
    own_loss = jnp.where(y == 0, both_loss[0], both_loss[1])
    other_loss = swap_core(own_loss)
    row_loss = jnp.where(
        core == 0, jnp.stack([own_loss, other_loss], 1), jnp.stack([other_loss, own_loss], 1)
    ).reshape(rows)
    return (row_loss, img_weight, txt_weight)


def solution(mesh):
    in_specs = (P("dp", None), P(("dp", "mp"), None), P("mp", "dp"), P("mp", "dp"), P(), P())
    out_specs = (P("dp"), P("mp", None), P("mp", None))
    return jax.shard_map(shards, mesh=mesh, in_specs=in_specs, out_specs=out_specs, check_vma=False)
```

```python
import jax
import jax.numpy as jnp
from jax import lax
from jax.experimental import pallas as pl
from jax.experimental.pallas import tpu as pltpu
from jax.sharding import PartitionSpec as P

F32 = jnp.float32
BF16 = jnp.bfloat16
LANES = 128
ALONG = (0, 1, -1, 2, -2, 3, -3, 4)
VMEM = pl.BlockSpec(memory_space=pltpu.VMEM)
SMEM = pl.BlockSpec(memory_space=pltpu.SMEM)
HBM = pl.BlockSpec(memory_space=pltpu.HBM)
ANY = pl.BlockSpec(memory_space=pl.ANY)
DMA = pltpu.SemaphoreType.DMA
WHOLE = 58


def local(kernel, outs, operands, mib, specs=None, out_specs=None, scratch=()):
    single = not isinstance(outs, list)
    shapes = [jax.ShapeDtypeStruct(*out) for out in ([outs] if single else outs)]
    result = pl.pallas_call(
        kernel,
        out_shape=shapes,
        in_specs=specs or [VMEM] * len(operands),
        out_specs=out_specs or [VMEM] * len(shapes),
        scratch_shapes=list(scratch),
        compiler_params=pltpu.CompilerParams(vmem_limit_bytes=mib * 2**20),
    )(*operands)
    return result[0] if single else result


def start_all(pairs, sems):
    copies = [
        pltpu.make_async_copy(source, target, sems.at[i]) for i, (source, target) in enumerate(pairs)
    ]
    for copy in copies:
        copy.start()
    return copies


def wait_all(copies):
    for copy in copies:
        copy.wait()


def normalize(raw):
    values = raw.astype(F32)
    inverse = lax.rsqrt(jnp.sum(values * values, axis=1, keepdims=True) + 1e-06)
    return (values * inverse, inverse)


def through_norm(upstream, normed, inverse):
    return (upstream - normed * jnp.sum(normed * upstream, axis=1, keepdims=True)) * inverse


def along_z(value, steps):
    return lax.ppermute(value, "dp", [(d, (d + 2 * steps) % 16) for d in range(16)])


def swap_y(value):
    return lax.ppermute(value, "dp", [(d, d ^ 1) for d in range(16)])


def swap_core(value):
    return lax.ppermute(value, "mp", [(m, m ^ 1) for m in range(16)])


def swap_x(value):
    return lax.ppermute(value, "mp", [(m, m ^ 2) for m in range(16)])


def swap_both(value):
    pairs = [(16 * d + m, 16 * (d ^ 1) + (m ^ 2)) for d in range(16) for m in range(16)]
    return lax.ppermute(value, ("dp", "mp"), pairs)


def loss_columns(losses):
    high = losses.astype(BF16)
    low = (losses - high.astype(F32)).astype(BF16)
    lane = lax.broadcasted_iota(jnp.int32, (losses.shape[0], LANES), 1)
    zero = jnp.zeros((), BF16)
    return jnp.where(lane == 0, high, jnp.where(lane == 1, low, zero))


def column_loss(extra):
    values = extra.astype(F32)
    return values[:, 0:1] + values[:, 1:2]


def feature_kernel(flags, *refs):
    sources, out_ref = refs[:4], refs[4]
    rows = sources[0].shape[1]
    count, half = sources[0].shape[0] // 2, rows // 2
    y, core = flags[0], flags[1]
    source = lax.broadcasted_iota(jnp.int32, (rows, half), 0)
    target = lax.broadcasted_iota(jnp.int32, (rows, half), 1)
    chosen = source == (target // 32) * 64 + core * 32 + target % 32
    pick = jnp.where(chosen, 1.0, 0.0).astype(BF16)
    for i, ref in enumerate(sources):
        both = jnp.dot(ref[...], pick, preferred_element_type=F32)
        own, other = both[:count].astype(BF16), both[count:].astype(BF16)
        place = pl.ds(i * count, count)
        out_ref[place, pl.ds(0, half)] = jnp.where(y == 0, own, other)
        out_ref[place, pl.ds(half, half)] = jnp.where(y == 0, other, own)


def tile_kernel(*refs):
    numbers, places, text_ids, image_ids = refs[0], refs[1], refs[2], refs[3]
    blocks, own, partner = refs[4:6], refs[6], refs[7]
    image_out, keep_ref, send_ref, texts, images, slopes = refs[8:]
    sub, width = image_out.shape[1], own.shape[1]
    scale, bias = numbers[0], numbers[1]
    rows = own.shape[0]
    pieces = rows // sub
    for i, block in enumerate(blocks):
        texts[pl.ds(i * rows, rows), :] = normalize(block[...])[0].astype(BF16)
    for part, source in enumerate((own, partner)):
        place = pl.ds(part * rows, rows)
        images[place, :] = normalize(source[...])[0].astype(BF16)
        logits = scale * lax.dot_general(
            images[place, :], texts[...], (((1,), (1,)), ((), ())), preferred_element_type=F32
        ) + bias
        match = image_ids[place, :] == text_ids[...]
        u = jnp.where(match, -logits, logits)
        e = jnp.exp(-jnp.abs(u))
        w = 1.0 + e
        grown = jnp.where(w == 1.0, e, jnp.log(w) * (e / jnp.where(w == 1.0, 1.0, w - 1.0)))
        losses = jnp.sum(jnp.maximum(u, 0.0) + grown, axis=1, keepdims=True)
        slope = jnp.where(match, -scale, scale) * (jnp.where(u >= 0.0, 1.0, e) / w)
        slopes[place, :] = slope.astype(BF16)
        grad = jnp.dot(slopes[place, :], texts[...], preferred_element_type=F32).astype(BF16)
        extra = loss_columns(losses)
        first = places[part]
        for i in range(pieces):
            image_out[first + i, :, pl.ds(0, width)] = grad[i * sub : (i + 1) * sub]
            image_out[first + i, :, pl.ds(width, LANES)] = extra[i * sub : (i + 1) * sub]
    text_grad = lax.dot_general(
        slopes[...], images[...], (((0,), (0,)), ((), ())), preferred_element_type=F32
    )
    half = text_grad.shape[0] // 2
    keep_ref[...] = text_grad[:half]
    send_ref[...] = text_grad[half:].astype(BF16)


def join_kernel(flags, keep_ref, came_ref, *refs):
    outs, stage, sems = refs[:8], refs[8], refs[9]
    sub = stage.shape[1]
    for i, steps in enumerate(ALONG):
        owner = lax.rem(flags[0] + (8 - steps), 8)
        place = pl.ds(pl.multiple_of(owner * sub, sub), sub)
        stage[i] = (keep_ref[place, :] + came_ref[place, :].astype(F32)).astype(BF16)
    wait_all(start_all([(stage.at[i], out) for i, out in enumerate(outs)], sems))


def text_kernel(*refs):
    blocks, raw_txt, out_ref, came, sems = refs[:8], *refs[8:]
    wait_all(start_all([(block, came.at[i]) for i, block in enumerate(blocks)], sems))
    text_grad = came[0].astype(F32)
    for i in range(1, came.shape[0]):
        text_grad += came[i].astype(F32)
    out_ref[...] = through_norm(text_grad, *normalize(raw_txt[...])).astype(BF16)


def grad_kernel(pieces, d_txt, raw_img, out_ref):
    width = raw_img.shape[1]
    half = width // 2
    image_grad = pieces[0, :, pl.ds(0, width)].astype(F32)
    losses = column_loss(pieces[0, :, pl.ds(width, LANES)])
    for i in range(1, pieces.shape[0]):
        image_grad += pieces[i, :, pl.ds(0, width)].astype(F32)
        losses += column_loss(pieces[i, :, pl.ds(width, LANES)])
    d_img = through_norm(image_grad, *normalize(raw_img[...])).astype(BF16)
    extra = loss_columns(losses)
    for h in range(2):
        place = pl.ds(h * half, half)
        out_ref[0, h, :, pl.ds(0, half)] = d_img[:, h * half : (h + 1) * half]
        out_ref[1, h, :, pl.ds(0, half)] = d_txt[:, place]
        for kind in range(2):
            out_ref[kind, h, :, pl.ds(half, LANES)] = extra


def weight_kernel(feats_ref, grads_ref, keep_ref, send_ref):
    count, width = keep_ref.shape
    grads = jnp.concatenate(
        [grads_ref[j, :, pl.ds(0, width)] for j in range(grads_ref.shape[0])], axis=0
    )
    both = jnp.dot(feats_ref[...], grads, preferred_element_type=F32)
    keep_ref[...] = both[:count]
    send_ref[...] = both[count:].astype(BF16)


def cut_kernel(keep_ref, came_ref, out_ref):
    rows, cols = out_ref.shape[2:]
    total = keep_ref[...] + came_ref[...].astype(F32)
    for part in range(2):
        for s in range(8):
            row, col = part * 4 * rows + (s // 2) * rows, (s % 2) * cols
            out_ref[s, part] = total[row : row + rows, col : col + cols].astype(BF16)


def sum_kernel(parts_ref, own_ref, other_ref):
    for part, out in enumerate((own_ref, other_ref)):
        total = parts_ref[0, part].astype(F32)
        for i in range(1, parts_ref.shape[0]):
            total += parts_ref[i, part].astype(F32)
        out[...] = total.astype(BF16)


def paste_kernel(flags, parts_ref, img_ref, txt_ref):
    rows, cols = parts_ref.shape[2:]
    first = flags[0] == 0
    for s in range(8):
        row, col = (s // 2) * rows, (s % 2) * cols
        for kind, out in enumerate((img_ref, txt_ref)):
            own, other = parts_ref[2 * s + kind, 0], parts_ref[2 * s + kind, 1]
            out[pl.ds(row, rows), pl.ds(col, cols)] = jnp.where(first, own, other).astype(F32)
            out[pl.ds(row, rows), pl.ds(2 * cols + col, cols)] = jnp.where(
                first, other, own
            ).astype(F32)


def shards(img_emb, txt_emb, img_feat_t, txt_feat_t, logit_scale, logit_bias):
    rows, width = img_emb.shape
    sub = txt_emb.shape[0]
    half = rows // 2
    feats = img_feat_t.shape[0]
    full = width + LANES
    dp_index = lax.axis_index("dp").astype(jnp.int32)
    mp_index = lax.axis_index("mp").astype(jnp.int32)
    core, chip = mp_index % 2, mp_index // 2
    z, y = dp_index // 2, dp_index % 2

    same_y = [[2 * s + t for s in range(8)] for t in range(2)]

    def over_z(value):
        return lax.all_to_all(value, "dp", 0, 0, tiled=True, axis_index_groups=same_y)

    texts = over_z(jnp.broadcast_to(txt_emb[None], (8, sub, width))).reshape(half, width)
    mine = jnp.where(y == 0, img_feat_t, txt_feat_t)
    theirs = jnp.where(y == 0, txt_feat_t, img_feat_t)
    came, mine_x, came_x = swap_y(theirs), swap_x(mine), swap_both(theirs)
    by_core = img_emb.reshape(8, 2, sub, width)
    own = lax.dynamic_slice_in_dim(by_core, core, 1, 1).reshape(half, width)
    partner = swap_y(own)
    owners = 2 * jnp.arange(8, dtype=jnp.int32) + y
    cores = jnp.stack([mp_index, mp_index ^ 1])
    text_ids = owners[None, :, None] * rows + cores[:, None, None] * sub
    text_ids = text_ids + jnp.arange(sub, dtype=jnp.int32)[None, None]
    count = jnp.arange(half, dtype=jnp.int32)
    in_shard = (count // sub) * 2 * sub + core * sub + count % sub
    image_ids = jnp.concatenate(
        [(2 * z + y) * rows + in_shard, (2 * z + 1 - y) * rows + in_shard]
    )
    places = jnp.stack([8 * y, 8 * (1 - y)])
    numbers = jnp.concatenate([logit_scale, logit_bias])
    numbers, came, mine_x, came_x = lax.optimization_barrier((numbers, came, mine_x, came_x))
    image_part, keep, send = local(
        tile_kernel,
        [((16, sub, full), BF16), ((half, width), F32), ((half, width), BF16)],
        [
            numbers,
            places.astype(jnp.int32),
            text_ids.astype(jnp.int32).reshape(1, rows),
            image_ids.astype(jnp.int32).reshape(rows, 1),
            texts,
            swap_core(texts),
            own,
            partner,
        ],
        24,
        [SMEM, SMEM] + [VMEM] * 6,
        None,
        [pltpu.VMEM((rows, width), BF16)] * 2
        + [pltpu.VMEM((rows, rows), BF16)],
    )
    plane = [
        [(2 * s + t) * 16 + 2 * k + c for t in range(2) for k in range(8)]
        for s in range(8)
        for c in range(2)
    ]

    def over_plane(value):
        return lax.all_to_all(
            value, ("dp", "mp"), 0, 0, tiled=True, axis_index_groups=plane
        )

    came_grad = swap_core(send)
    image_part, came_grad = lax.optimization_barrier((image_part, came_grad))
    text_parts = local(
        join_kernel,
        [((sub, width), BF16)] * 8,
        [z.reshape(1), keep, came_grad],
        WHOLE,
        [SMEM, VMEM, VMEM],
        [HBM] * 8,
        [pltpu.VMEM((8, sub, width), BF16), DMA((8,))],
    )
    image_pieces = over_plane(image_part)
    text_came = [text_parts[0]] + [
        along_z(part, -steps) for part, steps in zip(text_parts[1:], ALONG[1:], strict=True)
    ]
    pair = jnp.concatenate([mine, came])
    pair_x = jnp.concatenate([mine_x, came_x])
    feat_part = local(
        feature_kernel,
        ((4 * feats, rows), BF16),
        [jnp.stack([y, core]), pair, pair_x, swap_core(pair), swap_core(pair_x)],
        8,
        [SMEM] + [VMEM] * 4,
    )
    raw_txt, feat_part = lax.optimization_barrier((txt_emb, feat_part))
    d_txt = local(
        text_kernel,
        ((sub, width), BF16),
        [*text_came, raw_txt],
        WHOLE,
        [ANY] * 8 + [VMEM],
        None,
        [pltpu.VMEM((8, sub, width), BF16), DMA((8,))],
    )
    raw_img = lax.dynamic_slice_in_dim(img_emb, (2 * chip + core) * sub, sub, 0)
    narrow = width // 2
    kinds = local(
        grad_kernel,
        ((2, 2, sub, narrow + LANES), BF16),
        [image_pieces, d_txt, raw_img],
        12,
    )
    spread = jnp.broadcast_to(kinds[:, None], (2, 4, 2, sub, narrow + LANES))
    grads = over_plane(spread.reshape(16, sub, narrow + LANES))

    kept, sent = local(
        weight_kernel,
        [((2 * feats, narrow), F32), ((2 * feats, narrow), BF16)],
        [feat_part, grads],
        12,
    )
    shape = (feats // 4, narrow // 2)
    cut = local(cut_kernel, ((8, 2, *shape), BF16), [kept, swap_core(sent)], 6)
    parts = over_z(cut)
    own_sum, other_sum = local(sum_kernel, [(shape, BF16)] * 2, [parts], 6)
    summed = jnp.stack([own_sum, swap_x(other_sum)])
    weights = lax.all_to_all(
        jnp.broadcast_to(summed[None], (16, 2, *shape)), "dp", 0, 0, tiled=True
    )
    img_weight, txt_weight = local(
        paste_kernel,
        [((feats, width), F32)] * 2,
        [(chip % 2).reshape(1), weights],
        8,
        [SMEM, VMEM],
    )

    extra = grads[:, :, narrow : narrow + 2].astype(F32)
    both_loss = (extra[:, :, 0] + extra[:, :, 1]).reshape(2, 8, sub)
    own_loss = jnp.where(y == 0, both_loss[0], both_loss[1])
    other_loss = swap_core(own_loss)
    row_loss = jnp.where(
        core == 0, jnp.stack([own_loss, other_loss], 1), jnp.stack([other_loss, own_loss], 1)
    ).reshape(rows)
    return (row_loss, img_weight, txt_weight)


def solution(mesh):
    in_specs = (P("dp", None), P(("dp", "mp"), None), P("mp", "dp"), P("mp", "dp"), P(), P())
    out_specs = (P("dp"), P("mp", None), P("mp", None))
    return jax.shard_map(shards, mesh=mesh, in_specs=in_specs, out_specs=out_specs, check_vma=False)
```

```python
import jax
import jax.numpy as jnp
from jax import lax
from jax.experimental import pallas as pl
from jax.experimental.pallas import tpu as pltpu
from jax.sharding import PartitionSpec as P

F32 = jnp.float32
BF16 = jnp.bfloat16
LANES = 128
ALONG = (0, 1, -1, 2, -2, 3, -3, 4)
VMEM = pl.BlockSpec(memory_space=pltpu.VMEM)
SMEM = pl.BlockSpec(memory_space=pltpu.SMEM)
HBM = pl.BlockSpec(memory_space=pltpu.HBM)
ANY = pl.BlockSpec(memory_space=pl.ANY)
DMA = pltpu.SemaphoreType.DMA
WHOLE = 58


def local(kernel, outs, operands, mib, specs=None, out_specs=None, scratch=()):
    single = not isinstance(outs, list)
    shapes = [jax.ShapeDtypeStruct(*out) for out in ([outs] if single else outs)]
    result = pl.pallas_call(
        kernel,
        out_shape=shapes,
        in_specs=specs or [VMEM] * len(operands),
        out_specs=out_specs or [VMEM] * len(shapes),
        scratch_shapes=list(scratch),
        compiler_params=pltpu.CompilerParams(vmem_limit_bytes=mib * 2**20),
    )(*operands)
    return result[0] if single else result


def start_all(pairs, sems):
    copies = [
        pltpu.make_async_copy(source, target, sems.at[i]) for i, (source, target) in enumerate(pairs)
    ]
    for copy in copies:
        copy.start()
    return copies


def wait_all(copies):
    for copy in copies:
        copy.wait()


def normalize(raw):
    values = raw.astype(F32)
    inverse = lax.rsqrt(jnp.sum(values * values, axis=1, keepdims=True) + 1e-06)
    return (values * inverse, inverse)


def through_norm(upstream, normed, inverse):
    return (upstream - normed * jnp.sum(normed * upstream, axis=1, keepdims=True)) * inverse


def along_z(value, steps):
    return lax.ppermute(value, "dp", [(d, (d + 2 * steps) % 16) for d in range(16)])


def swap_y(value):
    return lax.ppermute(value, "dp", [(d, d ^ 1) for d in range(16)])


def swap_core(value):
    return lax.ppermute(value, "mp", [(m, m ^ 1) for m in range(16)])


def swap_x(value):
    return lax.ppermute(value, "mp", [(m, m ^ 2) for m in range(16)])


def swap_both(value):
    pairs = [(16 * d + m, 16 * (d ^ 1) + (m ^ 2)) for d in range(16) for m in range(16)]
    return lax.ppermute(value, ("dp", "mp"), pairs)


def loss_columns(losses):
    high = losses.astype(BF16)
    low = (losses - high.astype(F32)).astype(BF16)
    lane = lax.broadcasted_iota(jnp.int32, (losses.shape[0], LANES), 1)
    zero = jnp.zeros((), BF16)
    return jnp.where(lane == 0, high, jnp.where(lane == 1, low, zero))


def column_loss(extra):
    values = extra.astype(F32)
    return values[:, 0:1] + values[:, 1:2]


def feature_kernel(flags, *refs):
    sources, out_ref = refs[:8], refs[8]
    count, rows = sources[0].shape
    half = rows // 2
    y, core = flags[0], flags[1]
    source = lax.broadcasted_iota(jnp.int32, (rows, half), 0)
    target = lax.broadcasted_iota(jnp.int32, (rows, half), 1)
    chosen = source == (target // 32) * 64 + core * 32 + target % 32
    pick = jnp.where(chosen, 1.0, 0.0).astype(BF16)
    for i in range(4):
        own = jnp.dot(sources[2 * i][...], pick, preferred_element_type=F32).astype(BF16)
        other = jnp.dot(sources[2 * i + 1][...], pick, preferred_element_type=F32).astype(BF16)
        place = pl.ds(i * count, count)
        out_ref[place, pl.ds(0, half)] = jnp.where(y == 0, own, other)
        out_ref[place, pl.ds(half, half)] = jnp.where(y == 0, other, own)


def tile_kernel(*refs):
    numbers, places, text_ids, image_ids = refs[0], refs[1], refs[2], refs[3]
    blocks, own, partner = refs[4:6], refs[6], refs[7]
    image_out, keep_ref, send_ref, texts, images, slopes = refs[8:]
    sub, width = image_out.shape[1], own.shape[1]
    scale, bias = numbers[0], numbers[1]
    rows = own.shape[0]
    pieces = rows // sub
    for i, block in enumerate(blocks):
        texts[pl.ds(i * rows, rows), :] = normalize(block[...])[0].astype(BF16)
    for part, source in enumerate((own, partner)):
        place = pl.ds(part * rows, rows)
        images[place, :] = normalize(source[...])[0].astype(BF16)
        logits = scale * lax.dot_general(
            images[place, :], texts[...], (((1,), (1,)), ((), ())), preferred_element_type=F32
        ) + bias
        match = image_ids[place, :] == text_ids[...]
        u = jnp.where(match, -logits, logits)
        e = jnp.exp(-jnp.abs(u))
        w = 1.0 + e
        inverse = 1.0 / w
        grown = jnp.log(w) + (e - (w - 1.0)) * inverse
        losses = jnp.sum(jnp.maximum(u, 0.0) + grown, axis=1, keepdims=True)
        slope = jnp.where(match, -scale, scale) * (jnp.where(u >= 0.0, 1.0, e) * inverse)
        slopes[place, :] = slope.astype(BF16)
        grad = jnp.dot(slopes[place, :], texts[...], preferred_element_type=F32).astype(BF16)
        extra = loss_columns(losses)
        first = places[part]
        for i in range(pieces):
            image_out[first + i, :, pl.ds(0, width)] = grad[i * sub : (i + 1) * sub]
            image_out[first + i, :, pl.ds(width, LANES)] = extra[i * sub : (i + 1) * sub]
    text_grad = lax.dot_general(
        slopes[...], images[...], (((0,), (0,)), ((), ())), preferred_element_type=F32
    )
    half = text_grad.shape[0] // 2
    keep_ref[...] = text_grad[:half]
    send_ref[...] = text_grad[half:].astype(BF16)


def join_kernel(flags, keep_ref, came_ref, *refs):
    outs, stage, sems = refs[:8], refs[8], refs[9]
    sub = stage.shape[1]
    for i, steps in enumerate(ALONG):
        owner = lax.rem(flags[0] + (8 - steps), 8)
        place = pl.ds(pl.multiple_of(owner * sub, sub), sub)
        stage[i] = (keep_ref[place, :] + came_ref[place, :].astype(F32)).astype(BF16)
    wait_all(start_all([(stage.at[i], out) for i, out in enumerate(outs)], sems))


def text_kernel(*refs):
    blocks, raw_txt, out_ref, came, sems = refs[:8], *refs[8:]
    wait_all(start_all([(block, came.at[i]) for i, block in enumerate(blocks)], sems))
    text_grad = came[0].astype(F32)
    for i in range(1, came.shape[0]):
        text_grad += came[i].astype(F32)
    out_ref[...] = through_norm(text_grad, *normalize(raw_txt[...])).astype(BF16)


def grad_kernel(pieces, d_txt, raw_img, out_ref):
    width = raw_img.shape[1]
    half = width // 2
    image_grad = pieces[0, :, pl.ds(0, width)].astype(F32)
    losses = column_loss(pieces[0, :, pl.ds(width, LANES)])
    for i in range(1, pieces.shape[0]):
        image_grad += pieces[i, :, pl.ds(0, width)].astype(F32)
        losses += column_loss(pieces[i, :, pl.ds(width, LANES)])
    d_img = through_norm(image_grad, *normalize(raw_img[...])).astype(BF16)
    extra = loss_columns(losses)
    for h in range(2):
        place = pl.ds(h * half, half)
        out_ref[0, h, :, pl.ds(0, half)] = d_img[:, h * half : (h + 1) * half]
        out_ref[1, h, :, pl.ds(0, half)] = d_txt[:, place]
        for kind in range(2):
            out_ref[kind, h, :, pl.ds(half, LANES)] = extra


def weight_kernel(feats_ref, grads_ref, keep_ref, send_ref):
    count, width = keep_ref.shape
    grads = jnp.concatenate(
        [grads_ref[j, :, pl.ds(0, width)] for j in range(grads_ref.shape[0])], axis=0
    )
    both = jnp.dot(feats_ref[...], grads, preferred_element_type=F32)
    keep_ref[...] = both[:count]
    send_ref[...] = both[count:].astype(BF16)


def cut_kernel(keep_ref, came_ref, out_ref):
    rows, cols = out_ref.shape[2:]
    total = keep_ref[...] + came_ref[...].astype(F32)
    for part in range(2):
        for s in range(8):
            row, col = part * 4 * rows + (s // 2) * rows, (s % 2) * cols
            out_ref[s, part] = total[row : row + rows, col : col + cols].astype(BF16)


def sum_kernel(parts_ref, own_ref, other_ref):
    for part, out in enumerate((own_ref, other_ref)):
        total = parts_ref[0, part].astype(F32)
        for i in range(1, parts_ref.shape[0]):
            total += parts_ref[i, part].astype(F32)
        out[...] = total.astype(BF16)


def paste_kernel(flags, parts_ref, img_ref, txt_ref):
    rows, cols = parts_ref.shape[2:]
    first = flags[0] == 0
    for s in range(8):
        row, col = (s // 2) * rows, (s % 2) * cols
        for kind, out in enumerate((img_ref, txt_ref)):
            own, other = parts_ref[2 * s + kind, 0], parts_ref[2 * s + kind, 1]
            out[pl.ds(row, rows), pl.ds(col, cols)] = jnp.where(first, own, other).astype(F32)
            out[pl.ds(row, rows), pl.ds(2 * cols + col, cols)] = jnp.where(
                first, other, own
            ).astype(F32)


def shards(img_emb, txt_emb, img_feat_t, txt_feat_t, logit_scale, logit_bias):
    rows, width = img_emb.shape
    sub = txt_emb.shape[0]
    half = rows // 2
    feats = img_feat_t.shape[0]
    full = width + LANES
    dp_index = lax.axis_index("dp").astype(jnp.int32)
    mp_index = lax.axis_index("mp").astype(jnp.int32)
    core, chip = mp_index % 2, mp_index // 2
    z, y = dp_index // 2, dp_index % 2

    same_y = [[2 * s + t for s in range(8)] for t in range(2)]

    def over_z(value):
        return lax.all_to_all(value, "dp", 0, 0, tiled=True, axis_index_groups=same_y)

    texts = over_z(jnp.broadcast_to(txt_emb[None], (8, sub, width))).reshape(half, width)
    mine = jnp.where(y == 0, img_feat_t, txt_feat_t)
    theirs = jnp.where(y == 0, txt_feat_t, img_feat_t)
    came, mine_x, came_x = swap_y(theirs), swap_x(mine), swap_both(theirs)
    sources = (mine, came, mine_x, came_x)
    feat_part = local(
        feature_kernel,
        ((4 * feats, rows), BF16),
        [jnp.stack([y, core]), *sources, *map(swap_core, sources)],
        8,
        [SMEM] + [VMEM] * 8,
    )
    texts, feat_part = lax.optimization_barrier((texts, feat_part))
    by_core = img_emb.reshape(8, 2, sub, width)
    own = lax.dynamic_slice_in_dim(by_core, core, 1, 1).reshape(half, width)
    partner = swap_y(own)
    owners = 2 * jnp.arange(8, dtype=jnp.int32) + y
    cores = jnp.stack([mp_index, mp_index ^ 1])
    text_ids = owners[None, :, None] * rows + cores[:, None, None] * sub
    text_ids = text_ids + jnp.arange(sub, dtype=jnp.int32)[None, None]
    count = jnp.arange(half, dtype=jnp.int32)
    in_shard = (count // sub) * 2 * sub + core * sub + count % sub
    image_ids = jnp.concatenate(
        [(2 * z + y) * rows + in_shard, (2 * z + 1 - y) * rows + in_shard]
    )
    places = jnp.stack([8 * y, 8 * (1 - y)])
    numbers = jnp.concatenate([logit_scale, logit_bias])
    image_part, keep, send = local(
        tile_kernel,
        [((16, sub, full), BF16), ((half, width), F32), ((half, width), BF16)],
        [
            numbers,
            places.astype(jnp.int32),
            text_ids.astype(jnp.int32).reshape(1, rows),
            image_ids.astype(jnp.int32).reshape(rows, 1),
            texts,
            swap_core(texts),
            own,
            partner,
        ],
        24,
        [SMEM, SMEM] + [VMEM] * 6,
        None,
        [pltpu.VMEM((rows, width), BF16)] * 2
        + [pltpu.VMEM((rows, rows), BF16)],
    )
    plane = [
        [(2 * s + t) * 16 + 2 * k + c for t in range(2) for k in range(8)]
        for s in range(8)
        for c in range(2)
    ]

    def over_plane(value):
        return lax.all_to_all(
            value, ("dp", "mp"), 0, 0, tiled=True, axis_index_groups=plane
        )

    came_grad = swap_core(send)
    image_part, came_grad = lax.optimization_barrier((image_part, came_grad))
    text_parts = local(
        join_kernel,
        [((sub, width), BF16)] * 8,
        [z.reshape(1), keep, came_grad],
        WHOLE,
        [SMEM, VMEM, VMEM],
        [HBM] * 8,
        [pltpu.VMEM((8, sub, width), BF16), DMA((8,))],
    )
    image_pieces = over_plane(image_part)
    text_came = [text_parts[0]] + [
        along_z(part, -steps) for part, steps in zip(text_parts[1:], ALONG[1:], strict=True)
    ]
    d_txt = local(
        text_kernel,
        ((sub, width), BF16),
        [*text_came, txt_emb],
        WHOLE,
        [ANY] * 8 + [VMEM],
        None,
        [pltpu.VMEM((8, sub, width), BF16), DMA((8,))],
    )
    raw_img = lax.dynamic_slice_in_dim(img_emb, (2 * chip + core) * sub, sub, 0)
    narrow = width // 2
    kinds = local(
        grad_kernel,
        ((2, 2, sub, narrow + LANES), BF16),
        [image_pieces, d_txt, raw_img],
        12,
    )
    spread = jnp.broadcast_to(kinds[:, None], (2, 4, 2, sub, narrow + LANES))
    grads = over_plane(spread.reshape(16, sub, narrow + LANES))

    kept, sent = local(
        weight_kernel,
        [((2 * feats, narrow), F32), ((2 * feats, narrow), BF16)],
        [feat_part, grads],
        12,
    )
    shape = (feats // 4, narrow // 2)
    cut = local(cut_kernel, ((8, 2, *shape), BF16), [kept, swap_core(sent)], 6)
    parts = over_z(cut)
    own_sum, other_sum = local(sum_kernel, [(shape, BF16)] * 2, [parts], 6)
    summed = jnp.stack([own_sum, swap_x(other_sum)])
    weights = lax.all_to_all(
        jnp.broadcast_to(summed[None], (16, 2, *shape)), "dp", 0, 0, tiled=True
    )
    img_weight, txt_weight = local(
        paste_kernel,
        [((feats, width), F32)] * 2,
        [(chip % 2).reshape(1), weights],
        8,
        [SMEM, VMEM],
    )

    extra = grads[:, :, narrow : narrow + 2].astype(F32)
    both_loss = (extra[:, :, 0] + extra[:, :, 1]).reshape(2, 8, sub)
    own_loss = jnp.where(y == 0, both_loss[0], both_loss[1])
    other_loss = swap_core(own_loss)
    row_loss = jnp.where(
        core == 0, jnp.stack([own_loss, other_loss], 1), jnp.stack([other_loss, own_loss], 1)
    ).reshape(rows)
    return (row_loss, img_weight, txt_weight)


def solution(mesh):
    in_specs = (P("dp", None), P(("dp", "mp"), None), P("mp", "dp"), P("mp", "dp"), P(), P())
    out_specs = (P("dp"), P("mp", None), P("mp", None))
    return jax.shard_map(shards, mesh=mesh, in_specs=in_specs, out_specs=out_specs, check_vma=False)
```

```python
import jax
import jax.numpy as jnp
from jax import lax
from jax.experimental import pallas as pl
from jax.experimental.pallas import tpu as pltpu
from jax.sharding import PartitionSpec as P

F32 = jnp.float32
BF16 = jnp.bfloat16
LANES = 128
ALONG = (0, 1, -1, 2, -2, 3, -3, 4)
VMEM = pl.BlockSpec(memory_space=pltpu.VMEM)
SMEM = pl.BlockSpec(memory_space=pltpu.SMEM)
HBM = pl.BlockSpec(memory_space=pltpu.HBM)
ANY = pl.BlockSpec(memory_space=pl.ANY)
DMA = pltpu.SemaphoreType.DMA
WHOLE = 58


def local(kernel, outs, operands, mib, specs=None, out_specs=None, scratch=(), cost=None):
    single = not isinstance(outs, list)
    shapes = [jax.ShapeDtypeStruct(*out) for out in ([outs] if single else outs)]
    result = pl.pallas_call(
        kernel,
        out_shape=shapes,
        in_specs=specs or [VMEM] * len(operands),
        out_specs=out_specs or [VMEM] * len(shapes),
        scratch_shapes=list(scratch),
        cost_estimate=cost and pl.CostEstimate(flops=cost, bytes_accessed=0, transcendentals=0),
        compiler_params=pltpu.CompilerParams(vmem_limit_bytes=mib * 2**20),
    )(*operands)
    return result[0] if single else result


def start_all(pairs, sems):
    copies = [
        pltpu.make_async_copy(source, target, sems.at[i]) for i, (source, target) in enumerate(pairs)
    ]
    for copy in copies:
        copy.start()
    return copies


def wait_all(copies):
    for copy in copies:
        copy.wait()


def normalize(raw):
    values = raw.astype(F32)
    inverse = lax.rsqrt(jnp.sum(values * values, axis=1, keepdims=True) + 1e-06)
    return (values * inverse, inverse)


def through_norm(upstream, normed, inverse):
    return (upstream - normed * jnp.sum(normed * upstream, axis=1, keepdims=True)) * inverse


def along_z(value, steps):
    return lax.ppermute(value, "dp", [(d, (d + 2 * steps) % 16) for d in range(16)])


def swap_y(value):
    return lax.ppermute(value, "dp", [(d, d ^ 1) for d in range(16)])


def swap_core(value):
    return lax.ppermute(value, "mp", [(m, m ^ 1) for m in range(16)])


def swap_x(value):
    return lax.ppermute(value, "mp", [(m, m ^ 2) for m in range(16)])


def swap_both(value):
    pairs = [(16 * d + m, 16 * (d ^ 1) + (m ^ 2)) for d in range(16) for m in range(16)]
    return lax.ppermute(value, ("dp", "mp"), pairs)


def loss_columns(losses):
    high = losses.astype(BF16)
    low = (losses - high.astype(F32)).astype(BF16)
    lane = lax.broadcasted_iota(jnp.int32, (losses.shape[0], LANES), 1)
    zero = jnp.zeros((), BF16)
    return jnp.where(lane == 0, high, jnp.where(lane == 1, low, zero))


def column_loss(extra):
    values = extra.astype(F32)
    return values[:, 0:1] + values[:, 1:2]


def feature_kernel(flags, *refs):
    sources, out_ref = refs[:8], refs[8]
    count, rows = sources[0].shape
    half = rows // 2
    y, core = flags[0], flags[1]
    source = lax.broadcasted_iota(jnp.int32, (rows, half), 0)
    target = lax.broadcasted_iota(jnp.int32, (rows, half), 1)
    chosen = source == (target // 32) * 64 + core * 32 + target % 32
    pick = jnp.where(chosen, 1.0, 0.0).astype(BF16)
    for i in range(4):
        own = jnp.dot(sources[2 * i][...], pick, preferred_element_type=F32).astype(BF16)
        other = jnp.dot(sources[2 * i + 1][...], pick, preferred_element_type=F32).astype(BF16)
        place = pl.ds(i * count, count)
        out_ref[place, pl.ds(0, half)] = jnp.where(y == 0, own, other)
        out_ref[place, pl.ds(half, half)] = jnp.where(y == 0, other, own)


def tile_kernel(
    numbers, text_ids, image_ids, near, far, own, partner,
    texts, slopes, loss_ref, keep_ref, send_ref, images,
):
    scale, bias = numbers[0], numbers[1]
    rows = own.shape[0]
    for i, block in enumerate((near, far)):
        texts[pl.ds(i * rows, rows), :] = normalize(block[...])[0].astype(BF16)
    for part, source in enumerate((own, partner)):
        place = pl.ds(part * rows, rows)
        images[place, :] = normalize(source[...])[0].astype(BF16)
        logits = scale * lax.dot_general(
            images[place, :], texts[...], (((1,), (1,)), ((), ())), preferred_element_type=F32
        ) + bias
        match = image_ids[place, :] == text_ids[...]
        u = jnp.where(match, -logits, logits)
        e = jnp.exp(-jnp.abs(u))
        w = 1.0 + e
        inverse = 1.0 / w
        grown = jnp.log(w) + (e - (w - 1.0)) * inverse
        loss_ref[place, :] = jnp.sum(jnp.maximum(u, 0.0) + grown, axis=1, keepdims=True)
        slope = jnp.where(match, -scale, scale) * (jnp.where(u >= 0.0, 1.0, e) * inverse)
        slopes[place, :] = slope.astype(BF16)
    text_grad = lax.dot_general(
        slopes[...], images[...], (((0,), (0,)), ((), ())), preferred_element_type=F32
    )
    half = text_grad.shape[0] // 2
    keep_ref[...] = text_grad[:half]
    send_ref[...] = text_grad[half:].astype(BF16)


def image_kernel(places, texts, slopes, loss_ref, image_out):
    sub, width = image_out.shape[1], texts.shape[1]
    rows = slopes.shape[0] // 2
    for part in range(2):
        place = pl.ds(part * rows, rows)
        grad = jnp.dot(slopes[place, :], texts[...], preferred_element_type=F32).astype(BF16)
        extra = loss_columns(loss_ref[place, :])
        first = places[part]
        for i in range(rows // sub):
            image_out[first + i, :, pl.ds(0, width)] = grad[i * sub : (i + 1) * sub]
            image_out[first + i, :, pl.ds(width, LANES)] = extra[i * sub : (i + 1) * sub]


def join_kernel(flags, keep_ref, came_ref, *refs):
    outs, stage, sems = refs[:8], refs[8], refs[9]
    sub = stage.shape[1]
    for i, steps in enumerate(ALONG):
        owner = lax.rem(flags[0] + (8 - steps), 8)
        place = pl.ds(pl.multiple_of(owner * sub, sub), sub)
        stage[i] = (keep_ref[place, :] + came_ref[place, :].astype(F32)).astype(BF16)
    wait_all(start_all([(stage.at[i], out) for i, out in enumerate(outs)], sems))


def text_kernel(*refs):
    blocks, raw_txt, out_ref, came, sems = refs[:8], *refs[8:]
    wait_all(start_all([(block, came.at[i]) for i, block in enumerate(blocks)], sems))
    text_grad = came[0].astype(F32)
    for i in range(1, came.shape[0]):
        text_grad += came[i].astype(F32)
    out_ref[...] = through_norm(text_grad, *normalize(raw_txt[...])).astype(BF16)


def grad_kernel(pieces, d_txt, raw_img, out_ref):
    width = raw_img.shape[1]
    half = width // 2
    image_grad = pieces[0, :, pl.ds(0, width)].astype(F32)
    losses = column_loss(pieces[0, :, pl.ds(width, LANES)])
    for i in range(1, pieces.shape[0]):
        image_grad += pieces[i, :, pl.ds(0, width)].astype(F32)
        losses += column_loss(pieces[i, :, pl.ds(width, LANES)])
    d_img = through_norm(image_grad, *normalize(raw_img[...])).astype(BF16)
    extra = loss_columns(losses)
    for h in range(2):
        place = pl.ds(h * half, half)
        out_ref[0, h, :, pl.ds(0, half)] = d_img[:, h * half : (h + 1) * half]
        out_ref[1, h, :, pl.ds(0, half)] = d_txt[:, place]
        for kind in range(2):
            out_ref[kind, h, :, pl.ds(half, LANES)] = extra


def weight_kernel(feats_ref, grads_ref, keep_ref, send_ref):
    count, width = keep_ref.shape
    grads = jnp.concatenate(
        [grads_ref[j, :, pl.ds(0, width)] for j in range(grads_ref.shape[0])], axis=0
    )
    both = jnp.dot(feats_ref[...], grads, preferred_element_type=F32)
    keep_ref[...] = both[:count]
    send_ref[...] = both[count:].astype(BF16)


def cut_kernel(keep_ref, came_ref, out_ref):
    rows, cols = out_ref.shape[2:]
    total = keep_ref[...] + came_ref[...].astype(F32)
    for part in range(2):
        for s in range(8):
            row, col = part * 4 * rows + (s // 2) * rows, (s % 2) * cols
            out_ref[s, part] = total[row : row + rows, col : col + cols].astype(BF16)


def sum_kernel(parts_ref, own_ref, other_ref):
    for part, out in enumerate((own_ref, other_ref)):
        total = parts_ref[0, part].astype(F32)
        for i in range(1, parts_ref.shape[0]):
            total += parts_ref[i, part].astype(F32)
        out[...] = total.astype(BF16)


def paste_kernel(flags, parts_ref, img_ref, txt_ref):
    rows, cols = parts_ref.shape[2:]
    first = flags[0] == 0
    for s in range(8):
        row, col = (s // 2) * rows, (s % 2) * cols
        for kind, out in enumerate((img_ref, txt_ref)):
            own, other = parts_ref[2 * s + kind, 0], parts_ref[2 * s + kind, 1]
            out[pl.ds(row, rows), pl.ds(col, cols)] = jnp.where(first, own, other).astype(F32)
            out[pl.ds(row, rows), pl.ds(2 * cols + col, cols)] = jnp.where(
                first, other, own
            ).astype(F32)


def shards(img_emb, txt_emb, img_feat_t, txt_feat_t, logit_scale, logit_bias):
    rows, width = img_emb.shape
    sub = txt_emb.shape[0]
    half = rows // 2
    feats = img_feat_t.shape[0]
    full = width + LANES
    dp_index = lax.axis_index("dp").astype(jnp.int32)
    mp_index = lax.axis_index("mp").astype(jnp.int32)
    core, chip = mp_index % 2, mp_index // 2
    z, y = dp_index // 2, dp_index % 2

    same_y = [[2 * s + t for s in range(8)] for t in range(2)]

    def over_z(value):
        return lax.all_to_all(value, "dp", 0, 0, tiled=True, axis_index_groups=same_y)

    texts = over_z(jnp.broadcast_to(txt_emb[None], (8, sub, width))).reshape(half, width)
    mine = jnp.where(y == 0, img_feat_t, txt_feat_t)
    theirs = jnp.where(y == 0, txt_feat_t, img_feat_t)
    came, mine_x, came_x = swap_y(theirs), swap_x(mine), swap_both(theirs)
    sources = (mine, came, mine_x, came_x)
    feat_part = local(
        feature_kernel,
        ((4 * feats, rows), BF16),
        [jnp.stack([y, core]), *sources, *map(swap_core, sources)],
        8,
        [SMEM] + [VMEM] * 8,
    )
    texts, feat_part = lax.optimization_barrier((texts, feat_part))
    by_core = img_emb.reshape(8, 2, sub, width)
    own = lax.dynamic_slice_in_dim(by_core, core, 1, 1).reshape(half, width)
    partner = swap_y(own)
    owners = 2 * jnp.arange(8, dtype=jnp.int32) + y
    cores = jnp.stack([mp_index, mp_index ^ 1])
    text_ids = owners[None, :, None] * rows + cores[:, None, None] * sub
    text_ids = text_ids + jnp.arange(sub, dtype=jnp.int32)[None, None]
    count = jnp.arange(half, dtype=jnp.int32)
    in_shard = (count // sub) * 2 * sub + core * sub + count % sub
    image_ids = jnp.concatenate(
        [(2 * z + y) * rows + in_shard, (2 * z + 1 - y) * rows + in_shard]
    )
    places = jnp.stack([8 * y, 8 * (1 - y)])
    numbers = jnp.concatenate([logit_scale, logit_bias])
    unit, slope, losses, keep, send = local(
        tile_kernel,
        [
            ((rows, width), BF16),
            ((rows, rows), BF16),
            ((rows, 1), F32),
            ((half, width), F32),
            ((half, width), BF16),
        ],
        [
            numbers,
            text_ids.astype(jnp.int32).reshape(1, rows),
            image_ids.astype(jnp.int32).reshape(rows, 1),
            texts,
            swap_core(texts),
            own,
            partner,
        ],
        24,
        [SMEM] + [VMEM] * 6,
        None,
        [pltpu.VMEM((rows, width), BF16)],
        4 * 10**9,
    )
    came_grad = swap_core(send)
    image_part = local(
        image_kernel,
        ((16, sub, full), BF16),
        [places.astype(jnp.int32), unit, slope, losses],
        16,
        [SMEM] + [VMEM] * 3,
        cost=2 * 10**9,
    )
    plane = [
        [(2 * s + t) * 16 + 2 * k + c for t in range(2) for k in range(8)]
        for s in range(8)
        for c in range(2)
    ]

    def over_plane(value):
        return lax.all_to_all(
            value, ("dp", "mp"), 0, 0, tiled=True, axis_index_groups=plane
        )

    image_part, came_grad = lax.optimization_barrier((image_part, came_grad))
    text_parts = local(
        join_kernel,
        [((sub, width), BF16)] * 8,
        [z.reshape(1), keep, came_grad],
        WHOLE,
        [SMEM, VMEM, VMEM],
        [HBM] * 8,
        [pltpu.VMEM((8, sub, width), BF16), DMA((8,))],
    )
    image_pieces = over_plane(image_part)
    text_came = [text_parts[0]] + [
        along_z(part, -steps) for part, steps in zip(text_parts[1:], ALONG[1:], strict=True)
    ]
    d_txt = local(
        text_kernel,
        ((sub, width), BF16),
        [*text_came, txt_emb],
        WHOLE,
        [ANY] * 8 + [VMEM],
        None,
        [pltpu.VMEM((8, sub, width), BF16), DMA((8,))],
    )
    raw_img = lax.dynamic_slice_in_dim(img_emb, (2 * chip + core) * sub, sub, 0)
    narrow = width // 2
    kinds = local(
        grad_kernel,
        ((2, 2, sub, narrow + LANES), BF16),
        [image_pieces, d_txt, raw_img],
        12,
    )
    spread = jnp.broadcast_to(kinds[:, None], (2, 4, 2, sub, narrow + LANES))
    grads = over_plane(spread.reshape(16, sub, narrow + LANES))

    kept, sent = local(
        weight_kernel,
        [((2 * feats, narrow), F32), ((2 * feats, narrow), BF16)],
        [feat_part, grads],
        12,
    )
    shape = (feats // 4, narrow // 2)
    cut = local(cut_kernel, ((8, 2, *shape), BF16), [kept, swap_core(sent)], 6)
    parts = over_z(cut)
    own_sum, other_sum = local(sum_kernel, [(shape, BF16)] * 2, [parts], 6)
    summed = jnp.stack([own_sum, swap_x(other_sum)])
    weights = lax.all_to_all(
        jnp.broadcast_to(summed[None], (16, 2, *shape)), "dp", 0, 0, tiled=True
    )
    img_weight, txt_weight = local(
        paste_kernel,
        [((feats, width), F32)] * 2,
        [(chip % 2).reshape(1), weights],
        8,
        [SMEM, VMEM],
    )

    extra = grads[:, :, narrow : narrow + 2].astype(F32)
    both_loss = (extra[:, :, 0] + extra[:, :, 1]).reshape(2, 8, sub)
    own_loss = jnp.where(y == 0, both_loss[0], both_loss[1])
    other_loss = swap_core(own_loss)
    row_loss = jnp.where(
        core == 0, jnp.stack([own_loss, other_loss], 1), jnp.stack([other_loss, own_loss], 1)
    ).reshape(rows)
    return (row_loss, img_weight, txt_weight)


def solution(mesh):
    in_specs = (P("dp", None), P(("dp", "mp"), None), P("mp", "dp"), P("mp", "dp"), P(), P())
    out_specs = (P("dp"), P("mp", None), P("mp", None))
    return jax.shard_map(shards, mesh=mesh, in_specs=in_specs, out_specs=out_specs, check_vma=False)
```

```python
import jax
import jax.numpy as jnp
from jax import lax
from jax.experimental import pallas as pl
from jax.experimental.pallas import tpu as pltpu
from jax.sharding import PartitionSpec as P

F32 = jnp.float32
BF16 = jnp.bfloat16
LANES = 128
ALONG = (0, 1, -1, 2, -2, 3, -3, 4)
VMEM = pl.BlockSpec(memory_space=pltpu.VMEM)
SMEM = pl.BlockSpec(memory_space=pltpu.SMEM)
HBM = pl.BlockSpec(memory_space=pltpu.HBM)
ANY = pl.BlockSpec(memory_space=pl.ANY)
DMA = pltpu.SemaphoreType.DMA
WHOLE = 58


def local(kernel, outs, operands, mib, specs=None, out_specs=None, scratch=()):
    single = not isinstance(outs, list)
    shapes = [jax.ShapeDtypeStruct(*out) for out in ([outs] if single else outs)]
    result = pl.pallas_call(
        kernel,
        out_shape=shapes,
        in_specs=specs or [VMEM] * len(operands),
        out_specs=out_specs or [VMEM] * len(shapes),
        scratch_shapes=list(scratch),
        compiler_params=pltpu.CompilerParams(vmem_limit_bytes=mib * 2**20),
    )(*operands)
    return result[0] if single else result


def start_all(pairs, sems):
    copies = [
        pltpu.make_async_copy(source, target, sems.at[i]) for i, (source, target) in enumerate(pairs)
    ]
    for copy in copies:
        copy.start()
    return copies


def wait_all(copies):
    for copy in copies:
        copy.wait()


def normalize(raw):
    values = raw.astype(F32)
    inverse = lax.rsqrt(jnp.sum(values * values, axis=1, keepdims=True) + 1e-06)
    return (values * inverse, inverse)


def through_norm(upstream, normed, inverse):
    return (upstream - normed * jnp.sum(normed * upstream, axis=1, keepdims=True)) * inverse


def along_z(value, steps):
    return lax.ppermute(value, "dp", [(d, (d + 2 * steps) % 16) for d in range(16)])


def swap_y(value):
    return lax.ppermute(value, "dp", [(d, d ^ 1) for d in range(16)])


def swap_core(value):
    return lax.ppermute(value, "mp", [(m, m ^ 1) for m in range(16)])


def swap_x(value):
    return lax.ppermute(value, "mp", [(m, m ^ 2) for m in range(16)])


def swap_both(value):
    pairs = [(16 * d + m, 16 * (d ^ 1) + (m ^ 2)) for d in range(16) for m in range(16)]
    return lax.ppermute(value, ("dp", "mp"), pairs)


def loss_columns(losses):
    high = losses.astype(BF16)
    low = (losses - high.astype(F32)).astype(BF16)
    lane = lax.broadcasted_iota(jnp.int32, (losses.shape[0], LANES), 1)
    zero = jnp.zeros((), BF16)
    return jnp.where(lane == 0, high, jnp.where(lane == 1, low, zero))


def column_loss(extra):
    values = extra.astype(F32)
    return values[:, 0:1] + values[:, 1:2]


def feature_kernel(flags, *refs):
    sources, out_ref = refs[:8], refs[8]
    count, rows = sources[0].shape
    half = rows // 2
    y, core = flags[0], flags[1]
    source = lax.broadcasted_iota(jnp.int32, (rows, half), 0)
    target = lax.broadcasted_iota(jnp.int32, (rows, half), 1)
    chosen = source == (target // 32) * 64 + core * 32 + target % 32
    pick = jnp.where(chosen, 1.0, 0.0).astype(BF16)
    for i in range(4):
        own = jnp.dot(sources[2 * i][...], pick, preferred_element_type=F32).astype(BF16)
        other = jnp.dot(sources[2 * i + 1][...], pick, preferred_element_type=F32).astype(BF16)
        place = pl.ds(i * count, count)
        out_ref[place, pl.ds(0, half)] = jnp.where(y == 0, own, other)
        out_ref[place, pl.ds(half, half)] = jnp.where(y == 0, other, own)


def tile_kernel(*refs):
    numbers, places, text_ids, image_ids = refs[0], refs[1], refs[2], refs[3]
    blocks, own, partner = refs[4:6], refs[6], refs[7]
    image_out, keep_ref, send_ref, texts, images, slopes = refs[8:]
    sub, width = image_out.shape[1], own.shape[1]
    scale, bias = numbers[0], numbers[1]
    rows = own.shape[0]
    pieces = rows // sub
    for i, block in enumerate(blocks):
        texts[pl.ds(i * rows, rows), :] = normalize(block[...])[0].astype(BF16)
    for part, source in enumerate((own, partner)):
        place = pl.ds(part * rows, rows)
        images[place, :] = normalize(source[...])[0].astype(BF16)
        logits = scale * lax.dot_general(
            images[place, :], texts[...], (((1,), (1,)), ((), ())), preferred_element_type=F32
        ) + bias
        match = image_ids[place, :] == text_ids[...]
        u = jnp.where(match, -logits, logits)
        e = jnp.exp(-jnp.abs(u))
        w = 1.0 + e
        inverse = 1.0 / w
        grown = jnp.log(w) + (e - (w - 1.0)) * inverse
        losses = jnp.sum(jnp.maximum(u, 0.0) + grown, axis=1, keepdims=True)
        slope = jnp.where(match, -scale, scale) * (jnp.where(u >= 0.0, 1.0, e) * inverse)
        slopes[place, :] = slope.astype(BF16)
        grad = jnp.dot(slopes[place, :], texts[...], preferred_element_type=F32).astype(BF16)
        extra = loss_columns(losses)
        first = places[part]
        for i in range(pieces):
            image_out[first + i, :, pl.ds(0, width)] = grad[i * sub : (i + 1) * sub]
            image_out[first + i, :, pl.ds(width, LANES)] = extra[i * sub : (i + 1) * sub]
    text_grad = lax.dot_general(
        slopes[...], images[...], (((0,), (0,)), ((), ())), preferred_element_type=F32
    )
    half = text_grad.shape[0] // 2
    keep_ref[...] = text_grad[:half]
    send_ref[...] = text_grad[half:].astype(BF16)


def join_kernel(flags, keep_ref, came_ref, *refs):
    outs, stage, sems = refs[:8], refs[8], refs[9]
    sub = stage.shape[1]
    for i, steps in enumerate(ALONG):
        owner = lax.rem(flags[0] + (8 - steps), 8)
        place = pl.ds(pl.multiple_of(owner * sub, sub), sub)
        stage[i] = (keep_ref[place, :] + came_ref[place, :].astype(F32)).astype(BF16)
    wait_all(start_all([(stage.at[i], out) for i, out in enumerate(outs)], sems))


def text_kernel(*refs):
    blocks, raw_txt, out_ref, came, sems = refs[:8], *refs[8:]
    wait_all(start_all([(block, came.at[i]) for i, block in enumerate(blocks)], sems))
    text_grad = came[0].astype(F32)
    for i in range(1, came.shape[0]):
        text_grad += came[i].astype(F32)
    out_ref[...] = through_norm(text_grad, *normalize(raw_txt[...])).astype(BF16)


def grad_kernel(pieces, d_txt, raw_img, out_ref):
    width = raw_img.shape[1]
    half = width // 2
    image_grad = pieces[0, :, pl.ds(0, width)].astype(F32)
    losses = column_loss(pieces[0, :, pl.ds(width, LANES)])
    for i in range(1, pieces.shape[0]):
        image_grad += pieces[i, :, pl.ds(0, width)].astype(F32)
        losses += column_loss(pieces[i, :, pl.ds(width, LANES)])
    d_img = through_norm(image_grad, *normalize(raw_img[...])).astype(BF16)
    extra = loss_columns(losses)
    for h in range(2):
        place = pl.ds(h * half, half)
        out_ref[0, h, :, pl.ds(0, half)] = d_img[:, h * half : (h + 1) * half]
        out_ref[1, h, :, pl.ds(0, half)] = d_txt[:, place]
        for kind in range(2):
            out_ref[kind, h, :, pl.ds(half, LANES)] = extra


def weight_kernel(feats_ref, grads_ref, keep_ref, send_ref):
    count, width = keep_ref.shape
    grads = jnp.concatenate(
        [grads_ref[j, :, pl.ds(0, width)] for j in range(grads_ref.shape[0])], axis=0
    )
    both = jnp.dot(feats_ref[...], grads, preferred_element_type=F32)
    keep_ref[...] = both[:count]
    send_ref[...] = both[count:].astype(BF16)


def cut_kernel(keep_ref, came_ref, out_ref):
    rows, cols = out_ref.shape[2:]
    total = keep_ref[...] + came_ref[...].astype(F32)
    for part in range(2):
        for s in range(8):
            row, col = part * 4 * rows + (s // 2) * rows, (s % 2) * cols
            out_ref[s, part] = total[row : row + rows, col : col + cols].astype(BF16)


def sum_kernel(flags, parts_ref, out_ref):
    totals = []
    for part in range(2):
        total = parts_ref[0, part].astype(F32)
        for i in range(1, parts_ref.shape[0]):
            total += parts_ref[i, part].astype(F32)
        totals.append(total)
    first = flags[0] == 0
    for i in range(2):
        out_ref[i] = jnp.where(first, totals[i], totals[1 - i]).astype(BF16)


def paste_kernel(parts_ref, img_ref, txt_ref):
    rows, cols = parts_ref.shape[2:]
    for s in range(8):
        row, col = (s // 2) * rows, (s % 2) * cols
        for kind, out in enumerate((img_ref, txt_ref)):
            for h in range(2):
                place = (pl.ds(row, rows), pl.ds(2 * h * cols + col, cols))
                out[place] = parts_ref[2 * s + kind, h].astype(F32)


def copies_kernel(source, out_ref, sems):
    wait_all(start_all([(source, out_ref.at[i]) for i in range(out_ref.shape[0])], sems))


def shards(img_emb, txt_emb, img_feat_t, txt_feat_t, logit_scale, logit_bias):
    rows, width = img_emb.shape
    sub = txt_emb.shape[0]
    half = rows // 2
    feats = img_feat_t.shape[0]
    full = width + LANES
    dp_index = lax.axis_index("dp").astype(jnp.int32)
    mp_index = lax.axis_index("mp").astype(jnp.int32)
    core, chip = mp_index % 2, mp_index // 2
    z, y = dp_index // 2, dp_index % 2

    same_y = [[2 * s + t for s in range(8)] for t in range(2)]

    def over_z(value):
        return lax.all_to_all(value, "dp", 0, 0, tiled=True, axis_index_groups=same_y)

    copies = local(
        copies_kernel, ((8, sub, width), BF16), [txt_emb], WHOLE, [ANY], [HBM], [DMA((8,))]
    )
    texts = over_z(copies).reshape(half, width)
    mine = jnp.where(y == 0, img_feat_t, txt_feat_t)
    theirs = jnp.where(y == 0, txt_feat_t, img_feat_t)
    came, mine_x, came_x = swap_y(theirs), swap_x(mine), swap_both(theirs)
    sources = (mine, came, mine_x, came_x)
    feat_part = local(
        feature_kernel,
        ((4 * feats, rows), BF16),
        [jnp.stack([y, core]), *sources, *map(swap_core, sources)],
        8,
        [SMEM] + [VMEM] * 8,
    )
    texts, feat_part = lax.optimization_barrier((texts, feat_part))
    by_core = img_emb.reshape(8, 2, sub, width)
    own = lax.dynamic_slice_in_dim(by_core, core, 1, 1).reshape(half, width)
    partner = swap_y(own)
    owners = 2 * jnp.arange(8, dtype=jnp.int32) + y
    cores = jnp.stack([mp_index, mp_index ^ 1])
    text_ids = owners[None, :, None] * rows + cores[:, None, None] * sub
    text_ids = text_ids + jnp.arange(sub, dtype=jnp.int32)[None, None]
    count = jnp.arange(half, dtype=jnp.int32)
    in_shard = (count // sub) * 2 * sub + core * sub + count % sub
    image_ids = jnp.concatenate(
        [(2 * z + y) * rows + in_shard, (2 * z + 1 - y) * rows + in_shard]
    )
    places = jnp.stack([8 * y, 8 * (1 - y)])
    numbers = jnp.concatenate([logit_scale, logit_bias])
    image_part, keep, send = local(
        tile_kernel,
        [((16, sub, full), BF16), ((half, width), F32), ((half, width), BF16)],
        [
            numbers,
            places.astype(jnp.int32),
            text_ids.astype(jnp.int32).reshape(1, rows),
            image_ids.astype(jnp.int32).reshape(rows, 1),
            texts,
            swap_core(texts),
            own,
            partner,
        ],
        24,
        [SMEM, SMEM] + [VMEM] * 6,
        None,
        [pltpu.VMEM((rows, width), BF16)] * 2
        + [pltpu.VMEM((rows, rows), BF16)],
    )
    plane = [
        [(2 * s + t) * 16 + 2 * k + c for t in range(2) for k in range(8)]
        for s in range(8)
        for c in range(2)
    ]

    def over_plane(value):
        return lax.all_to_all(
            value, ("dp", "mp"), 0, 0, tiled=True, axis_index_groups=plane
        )

    came_grad = swap_core(send)
    image_part, came_grad = lax.optimization_barrier((image_part, came_grad))
    text_parts = local(
        join_kernel,
        [((sub, width), BF16)] * 8,
        [z.reshape(1), keep, came_grad],
        WHOLE,
        [SMEM, VMEM, VMEM],
        [HBM] * 8,
        [pltpu.VMEM((8, sub, width), BF16), DMA((8,))],
    )
    image_pieces = over_plane(image_part)
    text_came = [text_parts[0]] + [
        along_z(part, -steps) for part, steps in zip(text_parts[1:], ALONG[1:], strict=True)
    ]
    d_txt = local(
        text_kernel,
        ((sub, width), BF16),
        [*text_came, txt_emb],
        WHOLE,
        [ANY] * 8 + [VMEM],
        None,
        [pltpu.VMEM((8, sub, width), BF16), DMA((8,))],
    )
    raw_img = lax.dynamic_slice_in_dim(img_emb, (2 * chip + core) * sub, sub, 0)
    narrow = width // 2
    kinds = local(
        grad_kernel,
        ((2, 2, sub, narrow + LANES), BF16),
        [image_pieces, d_txt, raw_img],
        12,
    )
    spread = jnp.broadcast_to(kinds[:, None], (2, 4, 2, sub, narrow + LANES))
    grads = over_plane(spread.reshape(16, sub, narrow + LANES))

    kept, sent = local(
        weight_kernel,
        [((2 * feats, narrow), F32), ((2 * feats, narrow), BF16)],
        [feat_part, grads],
        12,
    )
    shape = (feats // 4, narrow // 2)
    cut = local(cut_kernel, ((8, 2, *shape), BF16), [kept, swap_core(sent)], 6)
    parts = over_z(cut)
    summed = local(
        sum_kernel,
        ((2, *shape), BF16),
        [(chip % 2).reshape(1), parts],
        6,
        [SMEM, VMEM],
    )
    columns = [
        [16 * d + 4 * q + 2 * k + c for d in range(16) for k in range(2)]
        for q in range(4)
        for c in range(2)
    ]
    weights = lax.all_to_all(
        jnp.broadcast_to(summed[None], (16, 2, *shape)).reshape(32, *shape),
        ("dp", "mp"), 0, 0, tiled=True, axis_index_groups=columns,
    )
    img_weight, txt_weight = local(
        paste_kernel, [((feats, width), F32)] * 2, [weights.reshape(16, 2, *shape)], 8
    )

    extra = grads[:, :, narrow : narrow + 2].astype(F32)
    both_loss = (extra[:, :, 0] + extra[:, :, 1]).reshape(2, 8, sub)
    own_loss = jnp.where(y == 0, both_loss[0], both_loss[1])
    other_loss = swap_core(own_loss)
    row_loss = jnp.where(
        core == 0, jnp.stack([own_loss, other_loss], 1), jnp.stack([other_loss, own_loss], 1)
    ).reshape(rows)
    return (row_loss, img_weight, txt_weight)


def solution(mesh):
    in_specs = (P("dp", None), P(("dp", "mp"), None), P("mp", "dp"), P("mp", "dp"), P(), P())
    out_specs = (P("dp"), P("mp", None), P("mp", None))
    return jax.shard_map(shards, mesh=mesh, in_specs=in_specs, out_specs=out_specs, check_vma=False)
```

```python
import jax
import jax.numpy as jnp
from jax import lax
from jax.experimental import pallas as pl
from jax.experimental.pallas import tpu as pltpu
from jax.sharding import PartitionSpec as P

F32 = jnp.float32
BF16 = jnp.bfloat16
ALONG = (0, 1, -1, 2, -2, 3, -3, 4)
VMEM = pl.BlockSpec(memory_space=pltpu.VMEM)
SMEM = pl.BlockSpec(memory_space=pltpu.SMEM)
HBM = pl.BlockSpec(memory_space=pltpu.HBM)
ANY = pl.BlockSpec(memory_space=pl.ANY)
DMA = pltpu.SemaphoreType.DMA
WHOLE = 58


def local(kernel, outs, operands, mib, specs=None, out_specs=None, scratch=()):
    single = not isinstance(outs, list)
    shapes = [jax.ShapeDtypeStruct(*out) for out in ([outs] if single else outs)]
    result = pl.pallas_call(
        kernel,
        out_shape=shapes,
        in_specs=specs or [VMEM] * len(operands),
        out_specs=out_specs or [VMEM] * len(shapes),
        scratch_shapes=list(scratch),
        compiler_params=pltpu.CompilerParams(vmem_limit_bytes=mib * 2**20),
    )(*operands)
    return result[0] if single else result


def start_all(pairs, sems):
    copies = [
        pltpu.make_async_copy(source, target, sems.at[i]) for i, (source, target) in enumerate(pairs)
    ]
    for copy in copies:
        copy.start()
    return copies


def wait_all(copies):
    for copy in copies:
        copy.wait()


def normalize(raw):
    values = raw.astype(F32)
    inverse = lax.rsqrt(jnp.sum(values * values, axis=1, keepdims=True) + 1e-06)
    return (values * inverse, inverse)


def through_norm(upstream, normed, inverse):
    return (upstream - normed * jnp.sum(normed * upstream, axis=1, keepdims=True)) * inverse


def along_z(value, steps):
    return lax.ppermute(value, "dp", [(d, (d + 2 * steps) % 16) for d in range(16)])


def swap_y(value):
    return lax.ppermute(value, "dp", [(d, d ^ 1) for d in range(16)])


def swap_core(value):
    return lax.ppermute(value, "mp", [(m, m ^ 1) for m in range(16)])


def swap_x(value):
    return lax.ppermute(value, "mp", [(m, m ^ 2) for m in range(16)])


def swap_both(value):
    pairs = [(16 * d + m, 16 * (d ^ 1) + (m ^ 2)) for d in range(16) for m in range(16)]
    return lax.ppermute(value, ("dp", "mp"), pairs)


def feature_kernel(flags, *refs):
    sources, out_ref = refs[:8], refs[8]
    count, rows = sources[0].shape
    half = rows // 2
    y, core = flags[0], flags[1]
    source = lax.broadcasted_iota(jnp.int32, (rows, half), 0)
    target = lax.broadcasted_iota(jnp.int32, (rows, half), 1)
    chosen = source == (target // 32) * 64 + core * 32 + target % 32
    pick = jnp.where(chosen, 1.0, 0.0).astype(BF16)
    for i in range(4):
        own = jnp.dot(sources[2 * i][...], pick, preferred_element_type=F32).astype(BF16)
        other = jnp.dot(sources[2 * i + 1][...], pick, preferred_element_type=F32).astype(BF16)
        place = pl.ds(i * count, count)
        out_ref[place, pl.ds(0, half)] = jnp.where(y == 0, own, other)
        out_ref[place, pl.ds(half, half)] = jnp.where(y == 0, other, own)


def tile_kernel(*refs):
    numbers, places, text_ids = refs[0], refs[1], refs[2]
    blocks, own, partner = refs[3:5], refs[5], refs[6]
    image_out, keep_ref, send_ref, loss_ref, texts, images, slopes = refs[7:]
    sub, width = image_out.shape[1], own.shape[1]
    scale, bias = numbers[0], numbers[1]
    rows = own.shape[0]
    pieces = rows // sub
    for i, block in enumerate(blocks):
        texts[pl.ds(i * rows, rows), :] = normalize(block[...])[0].astype(BF16)
    for part, source in enumerate((own, partner)):
        place = pl.ds(part * rows, rows)
        images[place, :] = normalize(source[...])[0].astype(BF16)
        logits = scale * lax.dot_general(
            images[place, :], texts[...], (((1,), (1,)), ((), ())), preferred_element_type=F32
        ) + bias
        row = lax.broadcasted_iota(jnp.int32, (rows, 1), 0)
        image_ids = places[2 + part] + (row // sub) * 2 * sub + row % sub
        match = image_ids == text_ids[...]
        u = jnp.where(match, -logits, logits)
        e = jnp.exp(-jnp.abs(u))
        w = 1.0 + e
        inverse = 1.0 / w
        grown = jnp.log(w) + (e - (w - 1.0)) * inverse
        losses = jnp.sum(jnp.maximum(u, 0.0) + grown, axis=1, keepdims=True)
        slope = jnp.where(match, -scale, scale) * (jnp.where(u >= 0.0, 1.0, e) * inverse)
        slopes[place, :] = slope.astype(BF16)
        grad = jnp.dot(slopes[place, :], texts[...], preferred_element_type=F32).astype(BF16)
        loss_ref[pl.ds(places[part] // 8, 1), :] = losses.reshape(1, rows)
        first = places[part]
        for i in range(pieces):
            image_out[first + i] = grad[i * sub : (i + 1) * sub]
    text_grad = lax.dot_general(
        slopes[...], images[...], (((0,), (0,)), ((), ())), preferred_element_type=F32
    )
    half = text_grad.shape[0] // 2
    keep_ref[...] = text_grad[:half]
    send_ref[...] = text_grad[half:].astype(BF16)


def join_kernel(flags, keep_ref, came_ref, *refs):
    outs, keep, came, stage, keep_sems, came_sems, out_sems = refs[:8], *refs[8:]
    sub = stage.shape[1]
    places = []
    for steps in ALONG:
        owner = lax.rem(flags[0] + (8 - steps), 8)
        places.append(pl.ds(pl.multiple_of(owner * sub, sub), sub))
    keeps = start_all([(keep_ref.at[p], keep.at[i]) for i, p in enumerate(places)], keep_sems)
    cames = start_all([(came_ref.at[p], came.at[i]) for i, p in enumerate(places)], came_sems)
    sent = []
    for i, out in enumerate(outs):
        keeps[i].wait()
        cames[i].wait()
        stage[i] = (keep[i] + came[i].astype(F32)).astype(BF16)
        copy = pltpu.make_async_copy(stage.at[i], out, out_sems.at[i])
        copy.start()
        sent.append(copy)
    wait_all(sent)


def text_kernel(*refs):
    blocks, raw_ref, out_ref, came, raw_txt, sems, raw_sem = refs[:8], *refs[8:]
    load = start_all([(raw_ref, raw_txt)], raw_sem)
    loads = start_all([(block, came.at[i]) for i, block in enumerate(blocks)], sems)
    wait_all(load)
    normed, inverse = normalize(raw_txt[...])
    loads[0].wait()
    text_grad = came[0].astype(F32)
    for i in range(1, came.shape[0]):
        loads[i].wait()
        text_grad += came[i].astype(F32)
    out_ref[...] = through_norm(text_grad, normed, inverse).astype(BF16)


def grad_kernel(flags, pieces, d_txt_ref, img_ref, out_ref, raw_img, d_txt, sems):
    sub = raw_img.shape[0]
    half = raw_img.shape[1] // 2
    rows = pl.ds(pl.multiple_of(flags[0] * sub, sub), sub)
    loads = start_all([(img_ref.at[rows], raw_img), (d_txt_ref, d_txt)], sems)
    image_grad = pieces[0].astype(F32)
    for i in range(1, pieces.shape[0]):
        image_grad += pieces[i].astype(F32)
    wait_all(loads)
    d_img = through_norm(image_grad, *normalize(raw_img[...])).astype(BF16)
    for h in range(2):
        out_ref[0, h] = d_img[:, h * half : (h + 1) * half]
        out_ref[1, h] = d_txt[:, pl.ds(h * half, half)]


def weight_kernel(feats_ref, grads_ref, keep_ref, send_ref):
    count, width = keep_ref.shape
    grads = jnp.concatenate(
        [grads_ref[j, :, pl.ds(0, width)] for j in range(grads_ref.shape[0])], axis=0
    )
    both = jnp.dot(feats_ref[...], grads, preferred_element_type=F32)
    keep_ref[...] = both[:count]
    send_ref[...] = both[count:].astype(BF16)


def cut_kernel(keep_ref, came_ref, out_ref):
    rows, cols = out_ref.shape[2:]
    total = keep_ref[...] + came_ref[...].astype(F32)
    for part in range(2):
        for s in range(8):
            row, col = part * 4 * rows + (s // 2) * rows, (s % 2) * cols
            out_ref[s, part] = total[row : row + rows, col : col + cols].astype(BF16)


def sum_kernel(flags, parts_ref, out_ref):
    totals = []
    for part in range(2):
        total = parts_ref[0, part].astype(F32)
        for i in range(1, parts_ref.shape[0]):
            total += parts_ref[i, part].astype(F32)
        totals.append(total)
    first = flags[0] == 0
    for i in range(2):
        out_ref[i] = jnp.where(first, totals[i], totals[1 - i]).astype(BF16)


def paste_kernel(parts_ref, img_ref, txt_ref):
    rows, cols = parts_ref.shape[2:]
    for s in range(8):
        row, col = (s // 2) * rows, (s % 2) * cols
        for kind, out in enumerate((img_ref, txt_ref)):
            for h in range(2):
                place = (pl.ds(row, rows), pl.ds(2 * h * cols + col, cols))
                out[place] = parts_ref[2 * s + kind, h].astype(F32)


def shards(img_emb, txt_emb, img_feat_t, txt_feat_t, logit_scale, logit_bias):
    rows, width = img_emb.shape
    sub = txt_emb.shape[0]
    half = rows // 2
    feats = img_feat_t.shape[0]
    dp_index = lax.axis_index("dp").astype(jnp.int32)
    mp_index = lax.axis_index("mp").astype(jnp.int32)
    core, chip = mp_index % 2, mp_index // 2
    z, y = dp_index // 2, dp_index % 2

    same_y = [[2 * s + t for s in range(8)] for t in range(2)]

    def over_z(value):
        return lax.all_to_all(value, "dp", 0, 0, tiled=True, axis_index_groups=same_y)

    texts = over_z(jnp.broadcast_to(txt_emb[None], (8, sub, width))).reshape(half, width)
    mine = jnp.where(y == 0, img_feat_t, txt_feat_t)
    theirs = jnp.where(y == 0, txt_feat_t, img_feat_t)
    came, mine_x, came_x = swap_y(theirs), swap_x(mine), swap_both(theirs)
    sources = (mine, came, mine_x, came_x)
    feat_part = local(
        feature_kernel,
        ((4 * feats, rows), BF16),
        [jnp.stack([y, core]), *sources, *map(swap_core, sources)],
        8,
        [SMEM] + [VMEM] * 8,
    )
    texts, feat_part = lax.optimization_barrier((texts, feat_part))
    by_core = img_emb.reshape(8, 2, sub, width)
    own = lax.dynamic_slice_in_dim(by_core, core, 1, 1).reshape(half, width)
    partner = swap_y(own)
    owners = 2 * jnp.arange(8, dtype=jnp.int32) + y
    cores = jnp.stack([mp_index, mp_index ^ 1])
    text_ids = owners[None, :, None] * rows + cores[:, None, None] * sub
    text_ids = text_ids + jnp.arange(sub, dtype=jnp.int32)[None, None]
    shard_start = 2 * z * rows + core * sub
    places = jnp.stack(
        [8 * y, 8 * (1 - y), shard_start + y * rows, shard_start + (1 - y) * rows]
    )
    numbers = jnp.concatenate([logit_scale, logit_bias])
    image_part, keep, send, losses = local(
        tile_kernel,
        [
            ((16, sub, width), BF16),
            ((half, width), F32),
            ((half, width), BF16),
            ((2, half), F32),
        ],
        [
            numbers,
            places.astype(jnp.int32),
            text_ids.astype(jnp.int32).reshape(1, rows),
            texts,
            swap_core(texts),
            own,
            partner,
        ],
        24,
        [SMEM, SMEM] + [VMEM] * 5,
        None,
        [pltpu.VMEM((rows, width), BF16)] * 2
        + [pltpu.VMEM((rows, rows), BF16)],
    )
    plane = [
        [(2 * s + t) * 16 + 2 * k + c for t in range(2) for k in range(8)]
        for s in range(8)
        for c in range(2)
    ]

    def over_plane(value):
        return lax.all_to_all(
            value, ("dp", "mp"), 0, 0, tiled=True, axis_index_groups=plane
        )

    came_grad = swap_core(send)
    losses = losses + lax.ppermute(losses, "mp", [(m, m ^ 2) for m in range(16)])
    image_part, came_grad, losses = lax.optimization_barrier((image_part, came_grad, losses))
    text_parts = local(
        join_kernel,
        [((sub, width), BF16)] * 8,
        [z.reshape(1), keep, came_grad],
        WHOLE,
        [SMEM, ANY, ANY],
        [HBM] * 8,
        [
            pltpu.VMEM((8, sub, width), F32),
            pltpu.VMEM((8, sub, width), BF16),
            pltpu.VMEM((8, sub, width), BF16),
        ]
        + [DMA((8,))] * 3,
    )
    image_pieces = over_plane(image_part)
    text_came = [text_parts[0]] + [
        along_z(part, -steps) for part, steps in zip(text_parts[1:], ALONG[1:], strict=True)
    ]
    d_txt = local(
        text_kernel,
        ((sub, width), BF16),
        [*text_came, txt_emb],
        WHOLE,
        [ANY] * 9,
        None,
        [
            pltpu.VMEM((8, sub, width), BF16),
            pltpu.VMEM((sub, width), BF16),
            DMA((8,)),
            DMA((1,)),
        ],
    )
    narrow = width // 2
    kinds = local(
        grad_kernel,
        ((2, 2, sub, narrow), BF16),
        [mp_index.reshape(1), image_pieces, d_txt, img_emb],
        12,
        [SMEM, VMEM, ANY, ANY],
        None,
        [pltpu.VMEM((sub, width), BF16), pltpu.VMEM((sub, width), BF16), DMA((2,))],
    )
    spread = jnp.broadcast_to(kinds[:, None], (2, 4, 2, sub, narrow))
    grads = over_plane(spread.reshape(16, sub, narrow))

    kept, sent = local(
        weight_kernel,
        [((2 * feats, narrow), F32), ((2 * feats, narrow), BF16)],
        [feat_part, grads],
        12,
    )
    shape = (feats // 4, narrow // 2)
    cut = local(cut_kernel, ((8, 2, *shape), BF16), [kept, swap_core(sent)], 6)
    parts = over_z(cut)
    for turn in (4, 8):
        losses = losses + lax.ppermute(losses, "mp", [(m, m ^ turn) for m in range(16)])
    parts, losses = lax.optimization_barrier((parts, losses))
    losses = losses + swap_y(losses)
    summed = local(
        sum_kernel,
        ((2, *shape), BF16),
        [(chip % 2).reshape(1), parts],
        6,
        [SMEM, VMEM],
    )
    columns = [
        [16 * d + 4 * q + 2 * k + c for d in range(16) for k in range(2)]
        for q in range(4)
        for c in range(2)
    ]
    weights = lax.all_to_all(
        jnp.broadcast_to(summed[None], (16, 2, *shape)).reshape(32, *shape),
        ("dp", "mp"), 0, 0, tiled=True, axis_index_groups=columns,
    )
    img_weight, txt_weight = local(
        paste_kernel, [((feats, width), F32)] * 2, [weights.reshape(16, 2, *shape)], 8
    )

    own_loss = jnp.where(y == 0, losses[0], losses[1]).reshape(8, sub)
    other_loss = swap_core(own_loss)
    row_loss = jnp.where(
        core == 0, jnp.stack([own_loss, other_loss], 1), jnp.stack([other_loss, own_loss], 1)
    ).reshape(rows)
    return (row_loss, img_weight, txt_weight)


def solution(mesh):
    in_specs = (P("dp", None), P(("dp", "mp"), None), P("mp", "dp"), P("mp", "dp"), P(), P())
    out_specs = (P("dp"), P("mp", None), P("mp", None))
    return jax.shard_map(shards, mesh=mesh, in_specs=in_specs, out_specs=out_specs, check_vma=False)
```

```python
import jax
import jax.numpy as jnp
from jax import lax
from jax.experimental import pallas as pl
from jax.experimental.pallas import tpu as pltpu
from jax.sharding import PartitionSpec as P

F32 = jnp.float32
BF16 = jnp.bfloat16
ALONG = (0, 1, -1, 2, -2, 3, -3, 4)
VMEM = pl.BlockSpec(memory_space=pltpu.VMEM)
SMEM = pl.BlockSpec(memory_space=pltpu.SMEM)
HBM = pl.BlockSpec(memory_space=pltpu.HBM)
ANY = pl.BlockSpec(memory_space=pl.ANY)
DMA = pltpu.SemaphoreType.DMA
WHOLE = 58


def local(kernel, outs, operands, mib, specs=None, out_specs=None, scratch=()):
    single = not isinstance(outs, list)
    shapes = [jax.ShapeDtypeStruct(*out) for out in ([outs] if single else outs)]
    result = pl.pallas_call(
        kernel,
        out_shape=shapes,
        in_specs=specs or [VMEM] * len(operands),
        out_specs=out_specs or [VMEM] * len(shapes),
        scratch_shapes=list(scratch),
        compiler_params=pltpu.CompilerParams(vmem_limit_bytes=mib * 2**20),
    )(*operands)
    return result[0] if single else result


def start_all(pairs, sems):
    copies = [
        pltpu.make_async_copy(source, target, sems.at[i]) for i, (source, target) in enumerate(pairs)
    ]
    for copy in copies:
        copy.start()
    return copies


def wait_all(copies):
    for copy in copies:
        copy.wait()


def normalize(raw):
    values = raw.astype(F32)
    inverse = lax.rsqrt(jnp.sum(values * values, axis=1, keepdims=True) + 1e-06)
    return (values * inverse, inverse)


def through_norm(upstream, normed, inverse):
    return (upstream - normed * jnp.sum(normed * upstream, axis=1, keepdims=True)) * inverse


def along_z(value, steps):
    return lax.ppermute(value, "dp", [(d, (d + 2 * steps) % 16) for d in range(16)])


def swap_y(value):
    return lax.ppermute(value, "dp", [(d, d ^ 1) for d in range(16)])


def swap_core(value):
    return lax.ppermute(value, "mp", [(m, m ^ 1) for m in range(16)])


def swap_x(value):
    return lax.ppermute(value, "mp", [(m, m ^ 2) for m in range(16)])


def swap_both(value):
    pairs = [(16 * d + m, 16 * (d ^ 1) + (m ^ 2)) for d in range(16) for m in range(16)]
    return lax.ppermute(value, ("dp", "mp"), pairs)


def feature_kernel(flags, *refs):
    sources, out_ref = refs[:8], refs[8]
    count, rows = sources[0].shape
    half = rows // 2
    y, core = flags[0], flags[1]
    source = lax.broadcasted_iota(jnp.int32, (rows, half), 0)
    target = lax.broadcasted_iota(jnp.int32, (rows, half), 1)
    chosen = source == (target // 32) * 64 + core * 32 + target % 32
    pick = jnp.where(chosen, 1.0, 0.0).astype(BF16)
    for i in range(4):
        own = jnp.dot(sources[2 * i][...], pick, preferred_element_type=F32).astype(BF16)
        other = jnp.dot(sources[2 * i + 1][...], pick, preferred_element_type=F32).astype(BF16)
        place = pl.ds(i * count, count)
        out_ref[place, pl.ds(0, half)] = jnp.where(y == 0, own, other)
        out_ref[place, pl.ds(half, half)] = jnp.where(y == 0, other, own)


def tile_kernel(*refs):
    numbers, places, text_ids = refs[0], refs[1], refs[2]
    blocks, own, partner = refs[3:5], refs[5], refs[6]
    image_out, keep_ref, send_ref, loss_ref, texts, images, slopes = refs[7:]
    sub, width = image_out.shape[1], own.shape[1]
    scale, bias = numbers[0], numbers[1]
    rows = own.shape[0]
    pieces = rows // sub
    for i, block in enumerate(blocks):
        texts[pl.ds(i * rows, rows), :] = normalize(block[...])[0].astype(BF16)
    for part, source in enumerate((own, partner)):
        place = pl.ds(part * rows, rows)
        images[place, :] = normalize(source[...])[0].astype(BF16)
        logits = scale * lax.dot_general(
            images[place, :], texts[...], (((1,), (1,)), ((), ())), preferred_element_type=F32
        ) + bias
        row = lax.broadcasted_iota(jnp.int32, (rows, 1), 0)
        image_ids = places[2 + part] + (row // sub) * 2 * sub + row % sub
        match = image_ids == text_ids[...]
        u = jnp.where(match, -logits, logits)
        e = jnp.exp(-jnp.abs(u))
        w = 1.0 + e
        inverse = 1.0 / w
        grown = jnp.log(w) + (e - (w - 1.0)) * inverse
        losses = jnp.sum(jnp.maximum(u, 0.0) + grown, axis=1, keepdims=True)
        slope = jnp.where(match, -scale, scale) * (jnp.where(u >= 0.0, 1.0, e) * inverse)
        slopes[place, :] = slope.astype(BF16)
        grad = jnp.dot(slopes[place, :], texts[...], preferred_element_type=F32).astype(BF16)
        loss_ref[pl.ds(places[part] // 8, 1), :] = losses.reshape(1, rows)
        first = places[part]
        for i in range(pieces):
            image_out[first + i] = grad[i * sub : (i + 1) * sub]
    text_grad = lax.dot_general(
        slopes[...], images[...], (((0,), (0,)), ((), ())), preferred_element_type=F32
    )
    half = text_grad.shape[0] // 2
    keep_ref[...] = text_grad[:half]
    send_ref[...] = text_grad[half:].astype(BF16)


def join_kernel(flags, keep_ref, came_ref, *refs):
    outs, keep, came, stage, keep_sems, came_sems, out_sems = refs[:8], *refs[8:]
    sub = stage.shape[1]
    places = []
    for steps in ALONG:
        owner = lax.rem(flags[0] + (8 - steps), 8)
        places.append(pl.ds(pl.multiple_of(owner * sub, sub), sub))
    keeps = start_all([(keep_ref.at[p], keep.at[i]) for i, p in enumerate(places)], keep_sems)
    cames = start_all([(came_ref.at[p], came.at[i]) for i, p in enumerate(places)], came_sems)
    sent = []
    for i, out in enumerate(outs):
        keeps[i].wait()
        cames[i].wait()
        stage[i] = (keep[i] + came[i].astype(F32)).astype(BF16)
        copy = pltpu.make_async_copy(stage.at[i], out, out_sems.at[i])
        copy.start()
        sent.append(copy)
    wait_all(sent)


def text_kernel(*refs):
    blocks, raw_ref, out_ref, came, raw_txt, sems, raw_sem = refs[:8], *refs[8:]
    load = start_all([(raw_ref, raw_txt)], raw_sem)
    loads = start_all([(block, came.at[i]) for i, block in enumerate(blocks)], sems)
    wait_all(load)
    normed, inverse = normalize(raw_txt[...])
    loads[0].wait()
    text_grad = came[0].astype(F32)
    for i in range(1, came.shape[0]):
        loads[i].wait()
        text_grad += came[i].astype(F32)
    out_ref[...] = through_norm(text_grad, normed, inverse).astype(BF16)


def grad_kernel(flags, pieces, d_txt_ref, img_ref, out_ref, raw_img, d_txt, sems):
    sub = raw_img.shape[0]
    half = raw_img.shape[1] // 2
    rows = pl.ds(pl.multiple_of(flags[0] * sub, sub), sub)
    loads = start_all([(img_ref.at[rows], raw_img), (d_txt_ref, d_txt)], sems)
    image_grad = pieces[0].astype(F32)
    for i in range(1, pieces.shape[0]):
        image_grad += pieces[i].astype(F32)
    wait_all(loads)
    d_img = through_norm(image_grad, *normalize(raw_img[...])).astype(BF16)
    for h in range(2):
        out_ref[0, h] = d_img[:, h * half : (h + 1) * half]
        out_ref[1, h] = d_txt[:, pl.ds(h * half, half)]


def weight_kernel(feats_ref, grads_ref, keep_ref, send_ref):
    count, width = keep_ref.shape
    grads = jnp.concatenate(
        [grads_ref[j, :, pl.ds(0, width)] for j in range(grads_ref.shape[0])], axis=0
    )
    both = jnp.dot(feats_ref[...], grads, preferred_element_type=F32)
    keep_ref[...] = both[:count]
    send_ref[...] = both[count:].astype(BF16)


def cut_kernel(keep_ref, came_ref, out_ref):
    rows, cols = out_ref.shape[2:]
    total = keep_ref[...] + came_ref[...].astype(F32)
    for part in range(2):
        for s in range(8):
            row, col = part * 4 * rows + (s // 2) * rows, (s % 2) * cols
            out_ref[s, part] = total[row : row + rows, col : col + cols].astype(BF16)


def sum_kernel(flags, parts_ref, out_ref):
    totals = []
    for part in range(2):
        total = parts_ref[0, part].astype(F32)
        for i in range(1, parts_ref.shape[0]):
            total += parts_ref[i, part].astype(F32)
        totals.append(total)
    first = flags[0] == 0
    for i in range(2):
        out_ref[i] = jnp.where(first, totals[i], totals[1 - i]).astype(BF16)


def paste_kernel(parts_ref, img_ref, txt_ref):
    rows, cols = parts_ref.shape[2:]
    for s in range(8):
        row, col = (s // 2) * rows, (s % 2) * cols
        for kind, out in enumerate((img_ref, txt_ref)):
            for h in range(2):
                place = (pl.ds(row, rows), pl.ds(2 * h * cols + col, cols))
                out[place] = parts_ref[2 * s + kind, h].astype(F32)


def shards(img_emb, txt_emb, img_feat_t, txt_feat_t, logit_scale, logit_bias):
    rows, width = img_emb.shape
    sub = txt_emb.shape[0]
    half = rows // 2
    feats = img_feat_t.shape[0]
    dp_index = lax.axis_index("dp").astype(jnp.int32)
    mp_index = lax.axis_index("mp").astype(jnp.int32)
    core, chip = mp_index % 2, mp_index // 2
    z, y = dp_index // 2, dp_index % 2

    same_y = [[2 * s + t for s in range(8)] for t in range(2)]

    def over_z(value):
        return lax.all_to_all(value, "dp", 0, 0, tiled=True, axis_index_groups=same_y)

    texts = over_z(jnp.broadcast_to(txt_emb[None], (8, sub, width))).reshape(half, width)
    mine = jnp.where(y == 0, img_feat_t, txt_feat_t)
    theirs = jnp.where(y == 0, txt_feat_t, img_feat_t)
    came, mine_x, came_x = swap_y(theirs), swap_x(mine), swap_both(theirs)
    sources = (mine, came, mine_x, came_x)
    feat_part = local(
        feature_kernel,
        ((4 * feats, rows), BF16),
        [jnp.stack([y, core]), *sources, *map(swap_core, sources)],
        8,
        [SMEM] + [VMEM] * 8,
    )
    texts, feat_part = lax.optimization_barrier((texts, feat_part))
    by_core = img_emb.reshape(8, 2, sub, width)
    own = lax.dynamic_slice_in_dim(by_core, core, 1, 1).reshape(half, width)
    partner = swap_y(own)
    owners = 2 * jnp.arange(8, dtype=jnp.int32) + y
    cores = jnp.stack([mp_index, mp_index ^ 1])
    text_ids = owners[None, :, None] * rows + cores[:, None, None] * sub
    text_ids = text_ids + jnp.arange(sub, dtype=jnp.int32)[None, None]
    shard_start = 2 * z * rows + core * sub
    places = jnp.stack(
        [8 * y, 8 * (1 - y), shard_start + y * rows, shard_start + (1 - y) * rows]
    )
    numbers = jnp.concatenate([logit_scale, logit_bias])
    image_part, keep, send, losses = local(
        tile_kernel,
        [
            ((16, sub, width), BF16),
            ((half, width), F32),
            ((half, width), BF16),
            ((2, half), F32),
        ],
        [
            numbers,
            places.astype(jnp.int32),
            text_ids.astype(jnp.int32).reshape(1, rows),
            texts,
            swap_core(texts),
            own,
            partner,
        ],
        50,
        [SMEM, SMEM] + [VMEM] * 5,
        None,
        [pltpu.VMEM((rows, width), BF16)] * 2
        + [pltpu.VMEM((rows, rows), BF16)],
    )
    plane = [
        [(2 * s + t) * 16 + 2 * k + c for t in range(2) for k in range(8)]
        for s in range(8)
        for c in range(2)
    ]

    def over_plane(value):
        return lax.all_to_all(
            value, ("dp", "mp"), 0, 0, tiled=True, axis_index_groups=plane
        )

    came_grad = swap_core(send)
    losses = losses + lax.ppermute(losses, "mp", [(m, m ^ 2) for m in range(16)])
    image_part, came_grad, losses = lax.optimization_barrier((image_part, came_grad, losses))
    text_parts = local(
        join_kernel,
        [((sub, width), BF16)] * 8,
        [z.reshape(1), keep, came_grad],
        WHOLE,
        [SMEM, ANY, ANY],
        [HBM] * 8,
        [
            pltpu.VMEM((8, sub, width), F32),
            pltpu.VMEM((8, sub, width), BF16),
            pltpu.VMEM((8, sub, width), BF16),
        ]
        + [DMA((8,))] * 3,
    )
    image_pieces = over_plane(image_part)
    text_came = [text_parts[0]] + [
        along_z(part, -steps) for part, steps in zip(text_parts[1:], ALONG[1:], strict=True)
    ]
    d_txt = local(
        text_kernel,
        ((sub, width), BF16),
        [*text_came, txt_emb],
        WHOLE,
        [ANY] * 9,
        None,
        [
            pltpu.VMEM((8, sub, width), BF16),
            pltpu.VMEM((sub, width), BF16),
            DMA((8,)),
            DMA((1,)),
        ],
    )
    narrow = width // 2
    kinds = local(
        grad_kernel,
        ((2, 2, sub, narrow), BF16),
        [mp_index.reshape(1), image_pieces, d_txt, img_emb],
        12,
        [SMEM, VMEM, ANY, ANY],
        None,
        [pltpu.VMEM((sub, width), BF16), pltpu.VMEM((sub, width), BF16), DMA((2,))],
    )
    spread = jnp.broadcast_to(kinds[:, None], (2, 4, 2, sub, narrow))
    grads = over_plane(spread.reshape(16, sub, narrow))

    kept, sent = local(
        weight_kernel,
        [((2 * feats, narrow), F32), ((2 * feats, narrow), BF16)],
        [feat_part, grads],
        12,
    )
    shape = (feats // 4, narrow // 2)
    cut = local(cut_kernel, ((8, 2, *shape), BF16), [kept, swap_core(sent)], 6)
    parts = over_z(cut)
    for turn in (4, 8):
        losses = losses + lax.ppermute(losses, "mp", [(m, m ^ turn) for m in range(16)])
    parts, losses = lax.optimization_barrier((parts, losses))
    losses = losses + swap_y(losses)
    summed = local(
        sum_kernel,
        ((2, *shape), BF16),
        [(chip % 2).reshape(1), parts],
        6,
        [SMEM, VMEM],
    )
    columns = [
        [16 * d + 4 * q + 2 * k + c for d in range(16) for k in range(2)]
        for q in range(4)
        for c in range(2)
    ]
    weights = lax.all_to_all(
        jnp.broadcast_to(summed[None], (16, 2, *shape)).reshape(32, *shape),
        ("dp", "mp"), 0, 0, tiled=True, axis_index_groups=columns,
    )
    img_weight, txt_weight = local(
        paste_kernel, [((feats, width), F32)] * 2, [weights.reshape(16, 2, *shape)], 8
    )

    own_loss = jnp.where(y == 0, losses[0], losses[1]).reshape(8, sub)
    other_loss = swap_core(own_loss)
    row_loss = jnp.where(
        core == 0, jnp.stack([own_loss, other_loss], 1), jnp.stack([other_loss, own_loss], 1)
    ).reshape(rows)
    return (row_loss, img_weight, txt_weight)


def solution(mesh):
    in_specs = (P("dp", None), P(("dp", "mp"), None), P("mp", "dp"), P("mp", "dp"), P(), P())
    out_specs = (P("dp"), P("mp", None), P("mp", None))
    return jax.shard_map(shards, mesh=mesh, in_specs=in_specs, out_specs=out_specs, check_vma=False)
```

```python
import jax
import jax.numpy as jnp
from jax import lax
from jax.experimental import pallas as pl
from jax.experimental.pallas import tpu as pltpu
from jax.sharding import PartitionSpec as P

F32 = jnp.float32
BF16 = jnp.bfloat16
ALONG = (0, 1, -1, 2, -2, 3, -3, 4)
VMEM = pl.BlockSpec(memory_space=pltpu.VMEM)
SMEM = pl.BlockSpec(memory_space=pltpu.SMEM)
HBM = pl.BlockSpec(memory_space=pltpu.HBM)
ANY = pl.BlockSpec(memory_space=pl.ANY)
DMA = pltpu.SemaphoreType.DMA
WHOLE = 58


def local(kernel, outs, operands, mib, specs=None, out_specs=None, scratch=()):
    single = not isinstance(outs, list)
    shapes = [jax.ShapeDtypeStruct(*out) for out in ([outs] if single else outs)]
    result = pl.pallas_call(
        kernel,
        out_shape=shapes,
        in_specs=specs or [VMEM] * len(operands),
        out_specs=out_specs or [VMEM] * len(shapes),
        scratch_shapes=list(scratch),
        compiler_params=pltpu.CompilerParams(vmem_limit_bytes=mib * 2**20),
    )(*operands)
    return result[0] if single else result


def start_all(pairs, sems):
    copies = [
        pltpu.make_async_copy(source, target, sems.at[i]) for i, (source, target) in enumerate(pairs)
    ]
    for copy in copies:
        copy.start()
    return copies


def wait_all(copies):
    for copy in copies:
        copy.wait()


def normalize(raw):
    values = raw.astype(F32)
    inverse = lax.rsqrt(jnp.sum(values * values, axis=1, keepdims=True) + 1e-06)
    return (values * inverse, inverse)


def through_norm(upstream, normed, inverse):
    return (upstream - normed * jnp.sum(normed * upstream, axis=1, keepdims=True)) * inverse


def along_z(value, steps):
    return lax.ppermute(value, "dp", [(d, (d + 2 * steps) % 16) for d in range(16)])


def swap_y(value):
    return lax.ppermute(value, "dp", [(d, d ^ 1) for d in range(16)])


def swap_core(value):
    return lax.ppermute(value, "mp", [(m, m ^ 1) for m in range(16)])


def swap_x(value):
    return lax.ppermute(value, "mp", [(m, m ^ 2) for m in range(16)])


def swap_both(value):
    pairs = [(16 * d + m, 16 * (d ^ 1) + (m ^ 2)) for d in range(16) for m in range(16)]
    return lax.ppermute(value, ("dp", "mp"), pairs)


def feature_kernel(flags, *refs):
    sources, out_ref = refs[:8], refs[8]
    count, rows = sources[0].shape
    half = rows // 2
    y, core = flags[0], flags[1]
    source = lax.broadcasted_iota(jnp.int32, (rows, half), 0)
    target = lax.broadcasted_iota(jnp.int32, (rows, half), 1)
    chosen = source == (target // 32) * 64 + core * 32 + target % 32
    pick = jnp.where(chosen, 1.0, 0.0).astype(BF16)
    for i in range(4):
        own = jnp.dot(sources[2 * i][...], pick, preferred_element_type=F32).astype(BF16)
        other = jnp.dot(sources[2 * i + 1][...], pick, preferred_element_type=F32).astype(BF16)
        place = pl.ds(i * count, count)
        out_ref[place, pl.ds(0, half)] = jnp.where(y == 0, own, other)
        out_ref[place, pl.ds(half, half)] = jnp.where(y == 0, other, own)


def tile_kernel(*refs):
    numbers, places, text_ids = refs[0], refs[1], refs[2]
    blocks, own, partner = refs[3:5], refs[5], refs[6]
    image_out, keep_ref, send_ref, loss_ref, texts, images, slopes = refs[7:]
    sub, width = image_out.shape[1], own.shape[1]
    scale, bias = numbers[0], numbers[1]
    rows = own.shape[0]
    pieces = rows // sub
    for i, block in enumerate(blocks):
        texts[pl.ds(i * rows, rows), :] = normalize(block[...])[0].astype(BF16)
    for part, source in enumerate((own, partner)):
        place = pl.ds(part * rows, rows)
        images[place, :] = normalize(source[...])[0].astype(BF16)
        logits = scale * lax.dot_general(
            images[place, :], texts[...], (((1,), (1,)), ((), ())), preferred_element_type=F32
        ) + bias
        row = lax.broadcasted_iota(jnp.int32, (rows, 1), 0)
        image_ids = places[2 + part] + (row // sub) * 2 * sub + row % sub
        match = image_ids == text_ids[...]
        u = jnp.where(match, -logits, logits)
        e = jnp.exp(-jnp.abs(u))
        w = 1.0 + e
        inverse = 1.0 / w
        grown = jnp.log(w) + (e - (w - 1.0)) * inverse
        losses = jnp.sum(jnp.maximum(u, 0.0) + grown, axis=1, keepdims=True)
        slope = jnp.where(match, -scale, scale) * (jnp.where(u >= 0.0, 1.0, e) * inverse)
        slopes[place, :] = slope.astype(BF16)
        grad = jnp.dot(slopes[place, :], texts[...], preferred_element_type=F32).astype(BF16)
        loss_ref[pl.ds(places[part] // 8, 1), :] = losses.reshape(1, rows)
        first = places[part]
        for i in range(pieces):
            image_out[first + i] = grad[i * sub : (i + 1) * sub]
    text_grad = lax.dot_general(
        slopes[...], images[...], (((0,), (0,)), ((), ())), preferred_element_type=F32
    )
    half = text_grad.shape[0] // 2
    keep_ref[...] = text_grad[:half]
    send_ref[...] = text_grad[half:].astype(BF16)


def join_kernel(flags, keep_ref, came_ref, *refs):
    outs, keep, came, stage, keep_sems, came_sems, out_sems = refs[:8], *refs[8:]
    sub = stage.shape[1]
    places = []
    for steps in ALONG:
        owner = lax.rem(flags[0] + (8 - steps), 8)
        places.append(pl.ds(pl.multiple_of(owner * sub, sub), sub))
    keeps = start_all([(keep_ref.at[p], keep.at[i]) for i, p in enumerate(places)], keep_sems)
    cames = start_all([(came_ref.at[p], came.at[i]) for i, p in enumerate(places)], came_sems)
    sent = []
    for i, out in enumerate(outs):
        keeps[i].wait()
        cames[i].wait()
        stage[i] = (keep[i] + came[i].astype(F32)).astype(BF16)
        copy = pltpu.make_async_copy(stage.at[i], out, out_sems.at[i])
        copy.start()
        sent.append(copy)
    wait_all(sent)


def text_kernel(*refs):
    blocks, raw_ref, out_ref, came, raw_txt, sems, raw_sem = refs[:8], *refs[8:]
    load = start_all([(raw_ref, raw_txt)], raw_sem)
    loads = start_all([(block, came.at[i]) for i, block in enumerate(blocks)], sems)
    wait_all(load)
    normed, inverse = normalize(raw_txt[...])
    loads[0].wait()
    text_grad = came[0].astype(F32)
    for i in range(1, came.shape[0]):
        loads[i].wait()
        text_grad += came[i].astype(F32)
    out_ref[...] = through_norm(text_grad, normed, inverse).astype(BF16)


def grad_kernel(flags, pieces, d_txt_ref, img_ref, out_ref, raw_img, d_txt, sems):
    sub = raw_img.shape[0]
    half = raw_img.shape[1] // 2
    rows = pl.ds(pl.multiple_of(flags[0] * sub, sub), sub)
    loads = start_all([(img_ref.at[rows], raw_img), (d_txt_ref, d_txt)], sems)
    image_grad = pieces[0].astype(F32)
    for i in range(1, pieces.shape[0]):
        image_grad += pieces[i].astype(F32)
    wait_all(loads)
    d_img = through_norm(image_grad, *normalize(raw_img[...])).astype(BF16)
    for h in range(2):
        out_ref[0, h] = d_img[:, h * half : (h + 1) * half]
        out_ref[1, h] = d_txt[:, pl.ds(h * half, half)]


def weight_kernel(feats_ref, grads_ref, keep_ref, send_ref):
    count, width = keep_ref.shape
    grads = jnp.concatenate(
        [grads_ref[j, :, pl.ds(0, width)] for j in range(grads_ref.shape[0])], axis=0
    )
    both = jnp.dot(feats_ref[...], grads, preferred_element_type=F32)
    keep_ref[...] = both[:count]
    send_ref[...] = both[count:].astype(BF16)


def cut_kernel(keep_ref, came_ref, out_ref):
    rows, cols = out_ref.shape[2:]
    total = keep_ref[...] + came_ref[...].astype(F32)
    for part in range(2):
        for s in range(8):
            row, col = part * 4 * rows + (s // 2) * rows, (s % 2) * cols
            out_ref[s, part] = total[row : row + rows, col : col + cols].astype(BF16)


def sum_kernel(flags, parts_ref, out_ref):
    totals = []
    for part in range(2):
        total = parts_ref[0, part].astype(F32)
        for i in range(1, parts_ref.shape[0]):
            total += parts_ref[i, part].astype(F32)
        totals.append(total)
    first = flags[0] == 0
    for i in range(2):
        out_ref[i] = jnp.where(first, totals[i], totals[1 - i]).astype(BF16)


def paste_kernel(parts_ref, img_ref, txt_ref):
    rows, cols = parts_ref.shape[2:]
    for s in range(8):
        row, col = (s // 2) * rows, (s % 2) * cols
        for kind, out in enumerate((img_ref, txt_ref)):
            for h in range(2):
                place = (pl.ds(row, rows), pl.ds(2 * h * cols + col, cols))
                out[place] = parts_ref[2 * s + kind, h].astype(F32)


def shards(img_emb, txt_emb, img_feat_t, txt_feat_t, logit_scale, logit_bias):
    rows, width = img_emb.shape
    sub = txt_emb.shape[0]
    half = rows // 2
    feats = img_feat_t.shape[0]
    dp_index = lax.axis_index("dp").astype(jnp.int32)
    mp_index = lax.axis_index("mp").astype(jnp.int32)
    core, chip = mp_index % 2, mp_index // 2
    z, y = dp_index // 2, dp_index % 2

    same_y = [[2 * s + t for s in range(8)] for t in range(2)]

    def over_z(value):
        return lax.all_to_all(value, "dp", 0, 0, tiled=True, axis_index_groups=same_y)

    texts = over_z(jnp.broadcast_to(txt_emb[None], (8, sub, width))).reshape(half, width)
    mine = jnp.where(y == 0, img_feat_t, txt_feat_t)
    theirs = jnp.where(y == 0, txt_feat_t, img_feat_t)
    came, mine_x, came_x = swap_y(theirs), swap_x(mine), swap_both(theirs)
    sources = (mine, came, mine_x, came_x)
    feat_part = local(
        feature_kernel,
        ((4 * feats, rows), BF16),
        [jnp.stack([y, core]), *sources, *map(swap_core, sources)],
        8,
        [SMEM] + [VMEM] * 8,
    )
    texts, feat_part = lax.optimization_barrier((texts, feat_part))
    by_core = img_emb.reshape(8, 2, sub, width)
    own = lax.dynamic_slice_in_dim(by_core, core, 1, 1).reshape(half, width)
    partner = swap_y(own)
    owners = 2 * jnp.arange(8, dtype=jnp.int32) + y
    cores = jnp.stack([mp_index, mp_index ^ 1])
    text_ids = owners[None, :, None] * rows + cores[:, None, None] * sub
    text_ids = text_ids + jnp.arange(sub, dtype=jnp.int32)[None, None]
    shard_start = 2 * z * rows + core * sub
    places = jnp.stack(
        [8 * y, 8 * (1 - y), shard_start + y * rows, shard_start + (1 - y) * rows]
    )
    numbers = jnp.concatenate([logit_scale, logit_bias])
    image_part, keep, send, losses = local(
        tile_kernel,
        [
            ((16, sub, width), BF16),
            ((half, width), F32),
            ((half, width), BF16),
            ((2, half), F32),
        ],
        [
            numbers,
            places.astype(jnp.int32),
            text_ids.astype(jnp.int32).reshape(1, rows),
            texts,
            swap_core(texts),
            own,
            partner,
        ],
        50,
        [SMEM, SMEM] + [VMEM] * 5,
        None,
        [pltpu.VMEM((rows, width), BF16)] * 2
        + [pltpu.VMEM((rows, rows), BF16)],
    )
    plane = [
        [(2 * s + t) * 16 + 2 * k + c for t in range(2) for k in range(8)]
        for s in range(8)
        for c in range(2)
    ]

    def over_plane(value):
        return lax.all_to_all(
            value, ("dp", "mp"), 0, 0, tiled=True, axis_index_groups=plane
        )

    came_grad = swap_core(send)
    image_part, came_grad = lax.optimization_barrier((image_part, came_grad))
    text_parts = local(
        join_kernel,
        [((sub, width), BF16)] * 8,
        [z.reshape(1), keep, came_grad],
        WHOLE,
        [SMEM, ANY, ANY],
        [HBM] * 8,
        [
            pltpu.VMEM((8, sub, width), F32),
            pltpu.VMEM((8, sub, width), BF16),
            pltpu.VMEM((8, sub, width), BF16),
        ]
        + [DMA((8,))] * 3,
    )
    image_pieces = over_plane(image_part)
    text_came = [text_parts[0]] + [
        along_z(part, -steps) for part, steps in zip(text_parts[1:], ALONG[1:], strict=True)
    ]
    d_txt = local(
        text_kernel,
        ((sub, width), BF16),
        [*text_came, txt_emb],
        WHOLE,
        [ANY] * 9,
        None,
        [
            pltpu.VMEM((8, sub, width), BF16),
            pltpu.VMEM((sub, width), BF16),
            DMA((8,)),
            DMA((1,)),
        ],
    )
    narrow = width // 2
    kinds = local(
        grad_kernel,
        ((2, 2, sub, narrow), BF16),
        [mp_index.reshape(1), image_pieces, d_txt, img_emb],
        12,
        [SMEM, VMEM, ANY, ANY],
        None,
        [pltpu.VMEM((sub, width), BF16), pltpu.VMEM((sub, width), BF16), DMA((2,))],
    )
    spread = jnp.broadcast_to(kinds[:, None], (2, 4, 2, sub, narrow))
    grads = over_plane(spread.reshape(16, sub, narrow))

    kept, sent = local(
        weight_kernel,
        [((2 * feats, narrow), F32), ((2 * feats, narrow), BF16)],
        [feat_part, grads],
        12,
    )
    shape = (feats // 4, narrow // 2)
    cut = local(cut_kernel, ((8, 2, *shape), BF16), [kept, swap_core(sent)], 6)
    parts = over_z(cut)
    for turn in (2, 4):
        losses = losses + lax.ppermute(losses, "mp", [(m, m ^ turn) for m in range(16)])
    parts, losses = lax.optimization_barrier((parts, losses))
    losses = losses + lax.ppermute(losses, "mp", [(m, m ^ 8) for m in range(16)])
    losses = losses + swap_y(losses)
    summed = local(
        sum_kernel,
        ((2, *shape), BF16),
        [(chip % 2).reshape(1), parts],
        6,
        [SMEM, VMEM],
    )
    columns = [
        [16 * d + 4 * q + 2 * k + c for d in range(16) for k in range(2)]
        for q in range(4)
        for c in range(2)
    ]
    weights = lax.all_to_all(
        jnp.broadcast_to(summed[None], (16, 2, *shape)).reshape(32, *shape),
        ("dp", "mp"), 0, 0, tiled=True, axis_index_groups=columns,
    )
    img_weight, txt_weight = local(
        paste_kernel, [((feats, width), F32)] * 2, [weights.reshape(16, 2, *shape)], 8
    )

    own_loss = jnp.where(y == 0, losses[0], losses[1]).reshape(8, sub)
    other_loss = swap_core(own_loss)
    row_loss = jnp.where(
        core == 0, jnp.stack([own_loss, other_loss], 1), jnp.stack([other_loss, own_loss], 1)
    ).reshape(rows)
    return (row_loss, img_weight, txt_weight)


def solution(mesh):
    in_specs = (P("dp", None), P(("dp", "mp"), None), P("mp", "dp"), P("mp", "dp"), P(), P())
    out_specs = (P("dp"), P("mp", None), P("mp", None))
    return jax.shard_map(shards, mesh=mesh, in_specs=in_specs, out_specs=out_specs, check_vma=False)
```
